128 devices in a mesh: section: 2 (over z_lo), dp: 4 (over y), ctx: 16 (over z_hi, x, core).
Axes of the slice: x: 4, y: 4, z: 4 (z_hi: 2, z_lo: 2; z = z_hi * 2 + z_lo), core: 2. Of those that a mesh axis runs over, the one named last changes fastest.
Arguments:
- ends: bfloat16 [2, 2, 8, 1024, 768], P('section', None, 'dp', 'ctx'), may hold values from -6 to 6
- cond: bfloat16 [2, 8, 768], P(None, 'dp'), may hold values from -6 to 6
- w_ada: bfloat16 [2, 768, 4608], P('section', 'dp'), may hold values from -0.109375 to 0.109375
- b_ada: bfloat16 [2, 4608], P('section', 'dp'), may hold values from -2 to 2
- w_qkv: bfloat16 [2, 768, 2304], P('section', 'dp'), may hold values from -0.21875 to 0.21875
- w_out: bfloat16 [2, 768, 768], P('section', 'dp'), may hold values from -0.4375 to 0.4375
- w_fc1: bfloat16 [2, 768, 3072], P('section', 'dp'), may hold values from -0.21875 to 0.21875
- w_fc2: bfloat16 [2, 3072, 768], P('section', 'dp'), may hold values from -0.109375 to 0.109375
Outputs:
- boundary: float32 [2, 2, 8, 1024, 768], P('section', None, 'dp', 'ctx')
- grad_cond: float32 [2, 8, 768], P(None, 'dp')
- grad_ada: float32 [2, 768, 4608], P('section', 'dp')
- grad_bias: float32 [2, 4608], P('section', 'dp')
- grad_qkv: float32 [2, 768, 2304], P('section', 'dp')
- grad_out: float32 [2, 768, 768], P('section', 'dp')
- grad_fc1: float32 [2, 768, 3072], P('section', 'dp')
- grad_fc2: float32 [2, 3072, 768], P('section', 'dp')
The draws below stay inside these ranges and needn't reach their ends.
All inputs are finite; a program needn't handle non-finite values.
Results may differ from the reference program's by a relative error of at most 0.017.
Values may be sent and summed in bfloat16 or wider, within the bound.
No kernel may reach another device: no remote copies, remote signals or barrier semaphores. Data moves between devices by JAX's collectives and lax.ppermute only.
A program may use at most 256 MiB of HBM per device.

```python
import jax
import jax.numpy as jnp
from jax import lax

D = 768
HEADS = 12
HEAD = 64
FF = 3072
C = 768
SEQ = 1024
MICRO = 2
LAT = 8
SECTIONS = 2
N_SECTION = 2


def steps_of(own_key, shape, cuts, least, high):
    factor_of = 1.0
    for dim, blocks in cuts:
        draws = jax.random.uniform(jax.random.fold_in(jax.random.fold_in(own_key, 6), dim), (blocks,), jnp.float32, least / len(cuts), high / len(cuts))
        factor_of = factor_of * jnp.repeat(jnp.exp(draws), shape[dim] // blocks).reshape((-1,) + (1,) * (len(shape) - 1 - dim))
    return factor_of


def noise(stream_key, dims, scale, limit, cuts=(), dtype=jnp.bfloat16):
    entries = scale * jax.random.normal(stream_key, dims, jnp.float32)
    if cuts:
        entries = entries * steps_of(stream_key, dims, cuts, -0.22, 0.18)
    return jnp.clip(entries, -limit, limit).astype(dtype)


def setup_inputs(seed: int = 0) -> dict:
    keys = jax.random.split(jax.random.key(seed), 9)
    return {
        "ends": noise(keys[0], (2, MICRO, LAT, SEQ, D), 1.0, 6.0, ((0, 2), (2, 4), (3, 16))),
        "cond": noise(keys[1], (MICRO, LAT, C), 1.0, 6.0, ((1, 4),)),
        "w_ada": noise(keys[2], (SECTIONS, C, 6 * D), (4 * C) ** -0.5, 0.109375, ((0, 2), (1, 4))),
        "b_ada": noise(keys[3], (SECTIONS, 6 * D), 0.3, 2.0, ((0, 2), (1, 4))),
        "w_qkv": noise(keys[4], (SECTIONS, D, 3 * D), D ** -0.5, 0.21875, ((0, 2), (1, 4))),
        "w_out": noise(keys[5], (SECTIONS, D, D), (D // 4) ** -0.5, 0.4375, ((0, 2), (1, 4))),
        "w_fc1": noise(keys[6], (SECTIONS, D, FF), D ** -0.5, 0.21875, ((0, 2), (1, 4))),
        "w_fc2": noise(keys[7], (SECTIONS, FF, D), FF ** -0.5, 0.109375, ((0, 2), (1, 4))),
    }


@jax.custom_vjp
def low(v):
    return lax.optimization_barrier(v.astype(jnp.bfloat16)).astype(jnp.float32)

@jax.custom_vjp
def low_back(v):
    return v

def low_keep(v):
    return (low(v), None)

def low_pass(kept, grad):
    return (grad,)

def back_keep(v):
    return (v, None)

def back_low(kept, grad):
    return (low(grad),)
low.defvjp(low_keep, low_pass)
low_back.defvjp(back_keep, back_low)

def matprod(left_side, right_side):
    return jnp.dot(left_side, right_side, precision=lax.Precision.HIGHEST)

def normalize(activations):
    center = activations - lax.optimization_barrier(jnp.mean(activations, axis=-1, keepdims=True))
    return center * lax.rsqrt(lax.optimization_barrier(jnp.mean(center * center, axis=-1, keepdims=True)) + 1e-06)

def residual_block(hidden_in, modulation, w_qkv, w_out, w_fc1, w_fc2):
    shift_first, scale_first, gate_first, shift_second, scale_second, gate_second = jnp.split(modulation, 6)
    entry_low = low(normalize(hidden_in) * (1.0 + scale_first) + shift_first)
    joined_qkv = matprod(entry_low, w_qkv)
    queries = low_back(low(joined_qkv[:, :D])).reshape(SEQ, HEADS, HEAD)
    keys_all = low_back(low(joined_qkv[:, D:2 * D])).reshape(SEQ, HEADS, HEAD)
    values_all = low_back(low(joined_qkv[:, 2 * D:])).reshape(SEQ, HEADS, HEAD)
    scores = jnp.einsum('she,the->hst', queries, keys_all, precision=lax.Precision.HIGHEST) * HEAD ** (-0.5)
    scores = low_back(scores)
    attn_probs = low(jax.nn.softmax(scores, axis=-1))
    mixed_out = jnp.einsum('hst,the->she', attn_probs, values_all, precision=lax.Precision.HIGHEST)
    mixed_out = low_back(low(mixed_out.reshape(SEQ, D)))
    branch = low_back(matprod(mixed_out, w_out))
    second = hidden_in + gate_first * branch
    mlp_input = low(normalize(second) * (1.0 + scale_second) + shift_second)
    pre_act = low_back(matprod(mlp_input, w_fc1))
    hidden = low(jax.nn.gelu(pre_act, approximate=True))
    return second + gate_second * low_back(matprod(hidden, w_fc2))

def latent_pass(hidden_in, condition, params_all):
    cond_low = low(jax.nn.silu(condition))
    current = hidden_in
    for layer_index in range(N_SECTION):
        w_ada, b_ada, w_qkv, w_out, w_fc1, w_fc2 = [param[layer_index] for param in params_all]
        modulation = matprod(cond_low, w_ada) + b_ada
        current = residual_block(current, modulation, w_qkv, w_out, w_fc1, w_fc2)
        if layer_index + 1 < N_SECTION:
            current = low_back(low(current))
    return current

def reference(ends, cond, w_ada, b_ada, w_qkv, w_out, w_fc1, w_fc2):
    inputs = ends[0].astype(jnp.float32).reshape(MICRO * LAT, SEQ, D)
    cotangent = ends[1].astype(jnp.float32).reshape(MICRO * LAT, SEQ, D)
    conditions = cond.astype(jnp.float32).reshape(MICRO * LAT, C)
    params = tuple((param.astype(jnp.float32) for param in (w_ada, b_ada, w_qkv, w_out, w_fc1, w_fc2)))

    def forward(inputs_all, conds_all, params_all):

        def one_latent(latent_pair):
            return latent_pass(latent_pair[0], latent_pair[1], params_all)
        return lax.map(jax.checkpoint(one_latent), (inputs_all, conds_all))
    last_out, pullback = jax.vjp(forward, inputs, conditions, params)
    grad_input, grad_conds, grad_params = pullback(cotangent)
    boundary = jnp.stack([grad_input.reshape(MICRO, LAT, SEQ, D), last_out.reshape(MICRO, LAT, SEQ, D)])
    return (boundary, grad_conds.reshape(MICRO, LAT, C), grad_params[0], grad_params[1], grad_params[2], grad_params[3], grad_params[4], grad_params[5])
```

```python
from functools import partial

import jax
import jax.numpy as jnp
from jax import lax
from jax.experimental import pallas as pl
from jax.experimental.pallas import tpu as pltpu
from jax.sharding import Mesh
from jax.sharding import PartitionSpec as P

HEAD = 64
BF = jnp.bfloat16
F32 = jnp.float32
GROUP = ("zh", "xh")
RING_X = ("xh", "xl")
CTX = ("zh", "xh", "xl", "core")


def shift(array, axis, by, size=4):
    return lax.ppermute(array, axis, [(i, (i + by) % size) for i in range(size)])


def swap(array, axis):
    return lax.ppermute(array, axis, [(0, 1), (1, 0)])


def pick(blocks, index):
    return lax.dynamic_index_in_dim(blocks, index, 0, keepdims=False)


def place(pieces, first):
    stacked = jnp.zeros((4, *pieces[0].shape), pieces[0].dtype)
    for s, piece in enumerate(pieces):
        stacked = lax.dynamic_update_index_in_dim(stacked, piece, (first + s) % 4, 0)
    return stacked


def by_core(core, mine, other, axis=0):
    return jnp.where(
        core == 0,
        jnp.concatenate([mine, other], axis=axis),
        jnp.concatenate([other, mine], axis=axis),
    )


def gather_ring(piece, axis, index):
    half = piece.shape[0] // 2
    below = shift(piece, axis, 1)
    above = shift(piece, axis, -1)
    far_low = shift(below[:half], axis, 1)
    far_high = shift(above[half:], axis, -1)
    return place([piece, above, jnp.concatenate([far_low, far_high]), below], index)


def gather_direct(piece, axis, index):
    return place([piece] + [shift(piece, axis, -s) for s in (1, 2, 3)], index)


def scatter_ring(blocks, axis, index):
    half = blocks.shape[1] // 2
    far = pick(blocks, (index + 2) % 4)
    from_below = shift(far[:half], axis, 1)
    from_above = shift(far[half:], axis, -1)
    up = pick(blocks, (index + 1) % 4)
    up = jnp.concatenate([(up[:half].astype(F32) + from_below.astype(F32)).astype(BF), up[half:]])
    down = pick(blocks, (index + 3) % 4)
    down = jnp.concatenate([down[:half], (down[half:].astype(F32) + from_above.astype(F32)).astype(BF)])
    got_up = shift(up, axis, 1)
    got_down = shift(down, axis, -1)
    return pick(blocks, index).astype(F32) + got_up.astype(F32) + got_down.astype(F32)


def scatter_direct(blocks, axis, index):
    total = pick(blocks, index).astype(F32)
    for s in (1, 2, 3):
        total = total + shift(pick(blocks, (index + s) % 4), axis, s).astype(F32)
    return total


def dot(left, right):
    return jnp.dot(left, right, preferred_element_type=F32)


def dot_nt(left, right):
    return lax.dot_general(left, right, (((1,), (1,)), ((), ())), preferred_element_type=F32)


def dot_tn(left, right):
    return lax.dot_general(left, right, (((0,), (0,)), ((), ())), preferred_element_type=F32)


def attention_kernel(q_ref, ko_ref, kp_ref, vo_ref, vp_ref, out_ref, lse_ref):
    rows = q_ref.shape[0]
    step = 256
    for h in range(2):
        cols = slice(HEAD * h, HEAD * (h + 1))
        keys_own, keys_peer = ko_ref[:, cols], kp_ref[:, cols]
        values_own, values_peer = vo_ref[:, cols], vp_ref[:, cols]
        for start in range(0, rows, step):
            queries = q_ref[start : start + step, cols] * HEAD ** (-0.5)
            scores_own = dot_nt(keys_own, queries)
            scores_peer = dot_nt(keys_peer, queries)
            top = jnp.maximum(
                jnp.max(scores_own, axis=0, keepdims=True),
                jnp.max(scores_peer, axis=0, keepdims=True),
            )
            probs_own = jnp.exp(scores_own - top)
            probs_peer = jnp.exp(scores_peer - top)
            total = jnp.sum(probs_own, axis=0, keepdims=True) + jnp.sum(
                probs_peer, axis=0, keepdims=True
            )
            mixed = dot_tn(values_own, probs_own.astype(BF)) + dot_tn(
                values_peer, probs_peer.astype(BF)
            )
            mixed = mixed / total
            out_ref[start : start + step, cols] = mixed.T.astype(BF)
            lse_ref[0, h : h + 1, start : start + step] = top + jnp.log(total)


def attention(queries, kv_own, kv_peer):
    rows, width = queries.shape
    pairs = width // 128
    block = lambda offset: pl.BlockSpec((rows, 128), lambda h: (0, h + offset))
    return pl.pallas_call(
        attention_kernel,
        grid=(pairs,),
        in_specs=[block(0), block(0), block(0), block(pairs), block(pairs)],
        out_specs=[block(0), pl.BlockSpec((1, 2, rows), lambda h: (h, 0, 0))],
        out_shape=[
            jax.ShapeDtypeStruct((rows, width), BF),
            jax.ShapeDtypeStruct((pairs, 2, rows), F32),
        ],
        compiler_params=pltpu.CompilerParams(vmem_limit_bytes=40 * 2**20),
        cost_estimate=pl.CostEstimate(
            flops=8 * rows * rows * width,
            bytes_accessed=12 * rows * width,
            transcendentals=2 * rows * rows * width // HEAD,
        ),
        name="attention",
    )(queries, kv_own, kv_peer, kv_own, kv_peer)


def attention_back_kernel(
    q_ref, ko_ref, kp_ref, vo_ref, vp_ref, out_ref, gout_ref, lse_ref, gq_ref, go_ref, gp_ref
):
    rows = q_ref.shape[0]
    step = 256
    scale = HEAD ** (-0.5)
    for h in range(2):
        cols = slice(HEAD * h, HEAD * (h + 1))
        sides = ((ko_ref, vo_ref, go_ref), (kp_ref, vp_ref, gp_ref))
        grad_kv = [[None, None], [None, None]]
        for start in range(0, rows, step):
            span = slice(start, start + step)
            queries = q_ref[span, cols] * scale
            grad_out = gout_ref[span, cols]
            lse = lse_ref[0, h : h + 1, span]
            both = grad_out.astype(F32) * out_ref[span, cols].astype(F32)
            row_total = jnp.sum(both.T, axis=0, keepdims=True)
            grad_queries = None
            for side, (k_ref, v_ref, g_ref) in enumerate(sides):
                keys, values = k_ref[:, cols], v_ref[:, cols]
                probs = jnp.exp(dot_nt(keys, queries) - lse)
                grad_probs = dot_nt(values, grad_out)
                grad_scores = (probs * (grad_probs - row_total)).astype(BF)
                part = dot_tn(keys, grad_scores)
                grad_queries = part if grad_queries is None else grad_queries + part
                terms = (dot(grad_scores, queries), dot(probs.astype(BF), grad_out))
                for i in range(2):
                    old = grad_kv[side][i]
                    grad_kv[side][i] = terms[i] if old is None else old + terms[i]
            gq_ref[span, cols] = (grad_queries * scale).T.astype(BF)
        for side, (k_ref, v_ref, g_ref) in enumerate(sides):
            for i in range(2):
                g_ref[i, :, cols] = grad_kv[side][i].astype(g_ref.dtype)


def attention_back(queries, kv_own, kv_peer, mixed, grad_mixed, lse):
    rows, width = queries.shape
    pairs = width // 128
    block = lambda offset: pl.BlockSpec((rows, 128), lambda h: (0, h + offset))
    double = pl.BlockSpec((2, rows, 128), lambda h: (0, 0, h))
    return pl.pallas_call(
        attention_back_kernel,
        grid=(pairs,),
        in_specs=[
            block(0),
            block(0),
            block(0),
            block(pairs),
            block(pairs),
            block(0),
            block(0),
            pl.BlockSpec((1, 2, rows), lambda h: (h, 0, 0)),
        ],
        out_specs=[block(0), double, double],
        out_shape=[
            jax.ShapeDtypeStruct((rows, width), BF),
            jax.ShapeDtypeStruct((2, rows, width), F32),
            jax.ShapeDtypeStruct((2, rows, width), BF),
        ],
        compiler_params=pltpu.CompilerParams(vmem_limit_bytes=40 * 2**20),
        cost_estimate=pl.CostEstimate(
            flops=20 * rows * rows * width,
            bytes_accessed=24 * rows * width,
            transcendentals=2 * rows * rows * width // HEAD,
        ),
        name="attention_back",
    )(queries, kv_own, kv_peer, kv_own, kv_peer, mixed, grad_mixed, lse)


def norm_stats(activations):
    center = activations - jnp.mean(activations, axis=-1, keepdims=True)
    inverse = lax.rsqrt(jnp.mean(center * center, axis=-1, keepdims=True) + 1e-06)
    return (center * inverse, inverse)


def norm_back(grad_norm, normal, inverse):
    return inverse * (
        grad_norm
        - jnp.mean(grad_norm, axis=-1, keepdims=True)
        - normal * jnp.mean(grad_norm * normal, axis=-1, keepdims=True)
    )


def core_sum(partial_sum):
    low = partial_sum.astype(BF)
    return low.astype(F32) + swap(low, "core").astype(F32)


def gelu_back(pre_act, grad_hidden):
    unused, pullback = jax.vjp(partial(jax.nn.gelu, approximate=True), pre_act)
    return pullback(grad_hidden)[0]


def layer_forward(activations, modulation, weights):
    w_q, w_kv, w_out, w_fc1, w_fc2 = weights
    shift_first, scale_first, gate_first, shift_second, scale_second, gate_second = modulation
    normal_first, inverse_first = norm_stats(activations)
    entry = (normal_first * (1.0 + scale_first) + shift_first).astype(BF)
    kv_own = dot(entry, w_kv).astype(BF)
    kv_peer = swap(kv_own, "xl")
    queries = dot(entry, w_q).astype(BF)
    mixed, lse = attention(queries, kv_own, kv_peer)
    branch = core_sum(dot(mixed, w_out))
    second = activations + gate_first * branch
    normal_second, inverse_second = norm_stats(second)
    mlp_input = (normal_second * (1.0 + scale_second) + shift_second).astype(BF)
    pre_act = dot(mlp_input, w_fc1)
    hidden = jax.nn.gelu(pre_act, approximate=True).astype(BF)
    branch_mlp = core_sum(dot(hidden, w_fc2))
    result = second + gate_second * branch_mlp
    state = (
        normal_first,
        inverse_first,
        entry,
        queries,
        kv_own,
        kv_peer,
        lse,
        mixed,
        branch,
        normal_second,
        inverse_second,
        mlp_input,
        pre_act,
        hidden,
        branch_mlp,
    )
    return (result, state)


def layer_backward(grad_result, state, modulation, weights):
    w_q, w_kv, w_out, w_fc1, w_fc2 = weights
    shift_first, scale_first, gate_first, shift_second, scale_second, gate_second = modulation
    (
        normal_first,
        inverse_first,
        entry,
        queries,
        kv_own,
        kv_peer,
        lse,
        mixed,
        branch,
        normal_second,
        inverse_second,
        mlp_input,
        pre_act,
        hidden,
        branch_mlp,
    ) = state
    rows = lambda value: jnp.sum(value, axis=0)
    grad_gate_second = rows(grad_result * branch_mlp)
    grad_branch_mlp = (grad_result * gate_second).astype(BF)
    grad_hidden = dot_nt(grad_branch_mlp, w_fc2)
    grad_pre = gelu_back(pre_act, grad_hidden).astype(BF)
    grad_mlp_input = core_sum(dot_nt(grad_pre, w_fc1))
    grad_fc2 = dot_tn(hidden, grad_branch_mlp).astype(BF)
    grad_fc1 = dot_tn(mlp_input, grad_pre).astype(BF)
    grad_scale_second = rows(grad_mlp_input * normal_second)
    grad_shift_second = rows(grad_mlp_input)
    grad_second = grad_result + norm_back(
        grad_mlp_input * (1.0 + scale_second), normal_second, inverse_second
    )
    grad_gate_first = rows(grad_second * branch)
    grad_branch = (grad_second * gate_first).astype(BF)
    grad_mixed = dot_nt(grad_branch, w_out).astype(BF)
    grad_out = dot_tn(mixed, grad_branch).astype(BF)
    grad_queries, grad_own, grad_peer = attention_back(
        queries, kv_own, kv_peer, mixed, grad_mixed, lse
    )
    grad_kv = (grad_own + swap(grad_peer, "xl").astype(F32)).astype(BF)
    grad_kv = jnp.concatenate([grad_kv[0], grad_kv[1]], axis=1)
    grad_entry = core_sum(dot_nt(grad_queries, w_q) + dot_nt(grad_kv, w_kv))
    grad_q_proj = dot_tn(entry, grad_queries).astype(BF)
    grad_kv_proj = dot_tn(entry, grad_kv).astype(BF)
    grad_scale_first = rows(grad_entry * normal_first)
    grad_shift_first = rows(grad_entry)
    grad_input = grad_second + norm_back(
        grad_entry * (1.0 + scale_first), normal_first, inverse_first
    )
    grad_modulation = jnp.stack(
        [
            grad_shift_first,
            grad_scale_first,
            grad_gate_first,
            grad_shift_second,
            grad_scale_second,
            grad_gate_second,
        ]
    )
    return (grad_input, grad_modulation, (grad_q_proj, grad_kv_proj, grad_out, grad_fc1, grad_fc2))


def sum_over_plane(block):
    x = lax.axis_index(RING_X)
    rows, columns = block.shape
    piece = scatter_direct(block.astype(BF).reshape(4, rows // 4, columns), RING_X, x)
    low = piece.astype(BF)
    low = (low.astype(F32) + swap(low, "zh").astype(F32)).astype(BF)
    return gather_direct(low, RING_X, x).reshape(rows, columns)


def on_device(ends, cond, w_ada, b_ada, w_qkv, w_out, w_fc1, w_fc2):
    section = lax.axis_index("section")
    d = lax.axis_index("dp")
    a = lax.axis_index(GROUP)
    core = lax.axis_index("core")
    width = w_out.shape[2]
    half = width // 2
    rows_d = w_out.shape[1]

    cond_float = cond.astype(F32).reshape(4, width)
    cond_low = jax.nn.silu(cond_float).astype(BF)
    cond_rows = cond_low.reshape(4, 4, rows_d).transpose(1, 0, 2)
    cond_parts = [pick(cond_rows, d)] + [
        shift(pick(cond_rows, (d + s) % 4), "dp", s) for s in (1, 2, 3)
    ]
    latent_rows = jnp.stack([pick(part, a) for part in cond_parts])
    part_mod = dot(latent_rows, w_ada[0])
    bias = lax.dynamic_update_slice(
        jnp.zeros((6 * width,), F32), b_ada[0].astype(F32), (d * b_ada.shape[1],)
    )
    part_mod = part_mod + bias[None]
    modulation = part_mod[0:1]
    for s in (1, 2, 3):
        modulation = modulation + shift(part_mod[s : s + 1], "dp", -s)
    modulation = [modulation[:, width * i : width * (i + 1)] for i in range(6)]

    blocks = ends[0].reshape(4, *ends.shape[3:])
    mine = [pick(blocks, a)] + [shift(pick(blocks, (a + s) % 4), GROUP, s) for s in (1, 2, 3)]
    mine = jnp.concatenate(mine)
    tokens_half = mine.shape[0]
    start = by_core(core, mine, swap(mine, "core"))

    qkv_half = pick(w_qkv[0].reshape(rows_d, 3, 2, half).transpose(2, 0, 1, 3), core)
    qkv_half = qkv_half.reshape(rows_d, 3 * half)
    out_half = pick(w_out[0].reshape(rows_d, 2, half).transpose(1, 0, 2), core)
    fc1_half = pick(w_fc1[0].reshape(rows_d, 4, 2, half).transpose(2, 0, 1, 3), core)
    fc1_half = fc1_half.reshape(rows_d, 4 * half)
    fc2_half = pick(w_fc2[0].reshape(2, half, width), core)
    full_qkv = gather_ring(qkv_half, "dp", d).reshape(width, 3 * half)
    full_out = gather_direct(out_half, "dp", d).reshape(width, half)
    sent = swap(pick(full_out.reshape(2, half, half), 1 - core), "core")
    full_out = by_core(core, pick(full_out.reshape(2, half, half), core), sent, axis=1)
    full_fc1 = gather_ring(fc1_half, "dp", d).reshape(width, 4 * half)
    full_fc2 = gather_ring(fc2_half, "dp", d).reshape(4 * half, width)
    weights = (full_qkv[:, :half], full_qkv[:, half:], full_out, full_fc1, full_fc2)

    def across(value, pairs):
        part = lax.dynamic_slice_in_dim(value.astype(BF), core * tokens_half, tokens_half, 0)
        part = lax.ppermute(part, "section", pairs)
        return by_core(core, part, swap(part, "core"))

    result, unused = layer_forward(start.astype(F32), modulation, weights)
    arrived = across(result, [(0, 1)])
    second_input = jnp.where(section == 0, start, arrived).astype(F32)
    result, state = layer_forward(second_input, modulation, weights)

    grad_input, unused, unused_too = layer_backward(start.astype(F32), state, modulation, weights)
    arrived = across(grad_input, [(1, 0)])
    seed = jnp.where(section == 0, arrived, start).astype(F32)
    grad_input, grad_modulation, grads = layer_backward(seed, state, modulation, weights)
    grad_q, grad_kv, grad_out, grad_fc1, grad_fc2 = grads

    group_fc = jnp.concatenate(
        [
            grad_fc2.reshape(4, half, width),
            grad_fc1[:, :width].reshape(4, rows_d, width),
            grad_fc1[:, width:].reshape(4, rows_d, width),
        ],
        axis=1,
    )
    out_cols = grad_out.reshape(half, 2, half).transpose(1, 0, 2)
    out_own = by_core(core, pick(out_cols, core), swap(pick(out_cols, 1 - core), "core"))
    group_attn = jnp.concatenate(
        [
            grad_kv.reshape(4, rows_d, width),
            jnp.concatenate([grad_q, out_own], axis=1).reshape(4, rows_d, width),
        ],
        axis=1,
    )
    sum_fc = sum_over_plane(scatter_ring(group_fc, "dp", d))
    sum_attn = sum_over_plane(scatter_ring(group_attn, "dp", d))

    def halves(total):
        other = swap(total, "core")
        return jnp.where(core == 0, total, other), jnp.where(core == 0, other, total)

    fc_halves = halves(sum_fc)
    attn_halves = halves(sum_attn)
    out_fc2 = jnp.concatenate([part[:half] for part in fc_halves]).astype(F32)
    fc1_parts = [
        jnp.concatenate([part[half : half + rows_d], part[half + rows_d :]], axis=1).reshape(
            rows_d, 4, 1, half
        )
        for part in fc_halves
    ]
    out_fc1 = jnp.concatenate(fc1_parts, axis=2).reshape(rows_d, 8 * half).astype(F32)
    kv_parts = [part[:rows_d] for part in attn_halves]
    q_parts = [part[rows_d:, :half] for part in attn_halves]
    out_qkv = jnp.concatenate(
        q_parts + [part[:, :half] for part in kv_parts] + [part[:, half:] for part in kv_parts],
        axis=1,
    ).astype(F32)
    out_out = jnp.concatenate([part[rows_d:, half:] for part in attn_halves], axis=1).astype(F32)

    grad_mod = grad_modulation.reshape(1, 6 * width)
    grad_mod = grad_mod + swap(grad_mod, "xl")
    plane_mod = gather_direct(grad_mod, GROUP, a).reshape(4, 6 * width)
    all_mod = jnp.concatenate(
        [plane_mod] + [shift(plane_mod, "dp", s) for s in (1, 2, 3)]
    )
    all_cond = jnp.concatenate(cond_parts).astype(F32)
    out_ada = lax.dot_general(
        all_cond, all_mod, (((0,), (0,)), ((), ())), precision=lax.Precision.HIGHEST
    )
    out_bias = jnp.sum(
        lax.dynamic_slice_in_dim(all_mod, d * b_ada.shape[1], b_ada.shape[1], 1), axis=0
    )
    grad_silu = lax.dot_general(
        all_mod,
        w_ada[0].astype(F32),
        (((1,), (1,)), ((), ())),
        precision=lax.Precision.HIGHEST,
    ).reshape(4, 4, rows_d)
    silu_parts = [grad_silu[0]] + [shift(grad_silu[s], "dp", -s) for s in (1, 2, 3)]
    silu_full = place(silu_parts, d).transpose(1, 0, 2).reshape(4, width)
    silu_full = silu_full + swap(silu_full, "section")
    unused, silu_pull = jax.vjp(jax.nn.silu, cond_float)
    out_cond = silu_pull(silu_full)[0].reshape(cond.shape)

    edge = jnp.where(section == 0, grad_input, result)
    edge = lax.dynamic_slice_in_dim(edge, core * tokens_half, tokens_half, 0)
    edge = edge.reshape(4, tokens_half // 4, width)
    back = [edge[0]] + [shift(edge[s].astype(BF), GROUP, -s).astype(F32) for s in (1, 2, 3)]
    boundary = place(back, a).reshape(ends.shape)

    return (
        boundary,
        out_cond,
        out_ada[None],
        out_bias[None],
        out_qkv[None],
        out_out[None],
        out_fc1[None],
        out_fc2[None],
    )


def solution(mesh):
    finer = Mesh(
        mesh.devices.reshape(2, 4, 2, 2, 2, 2), ("section", "dp", "zh", "xh", "xl", "core")
    )
    ends_spec = P("section", None, "dp", CTX, None)
    cond_spec = P(None, "dp", None)
    matrix = P("section", "dp", None)
    vector = P("section", "dp")
    return jax.shard_map(
        on_device,
        mesh=finer,
        in_specs=(ends_spec, cond_spec, matrix, vector, matrix, matrix, matrix, matrix),
        out_specs=(ends_spec, cond_spec, matrix, vector, matrix, matrix, matrix, matrix),
        check_vma=False,
    )
```

```python
import jax
import jax.numpy as jnp
from jax import lax
from jax.experimental import pallas as pl
from jax.experimental.pallas import tpu as pltpu
from jax.sharding import Mesh
from jax.sharding import PartitionSpec as P

HEAD = 64
BF = jnp.bfloat16
F32 = jnp.float32
RING_X = ("xh", "xl")
CTX = ("zh", "xh", "xl", "core")


def shift(array, axis, by, size=4):
    return lax.ppermute(array, axis, [(i, (i + by) % size) for i in range(size)])


def swap(array, axis):
    return lax.ppermute(array, axis, [(0, 1), (1, 0)])


def swap_odd(array, axis):
    return lax.ppermute(array, axis, [(0, 3), (1, 2), (2, 1), (3, 0)])


def swap_even(array, axis):
    return lax.ppermute(array, axis, [(0, 1), (1, 0), (2, 3), (3, 2)])


def pick(blocks, index):
    return lax.dynamic_index_in_dim(blocks, index, 0, keepdims=False)


def rows_at(array, start, size):
    return lax.dynamic_slice_in_dim(array, start, size, 0)


def ordered(first, mine, other, axis=0):
    return jnp.where(
        first,
        jnp.concatenate([mine, other], axis=axis),
        jnp.concatenate([other, mine], axis=axis),
    )


def gather_small(piece, axis, index):
    two = ordered(index % 2 == 0, piece, swap_even(piece, axis))
    return ordered(index < 2, two, swap_odd(two, axis))


def gather_ring(piece, axis):
    half = piece.shape[0] // 2
    below = shift(piece, axis, 1)
    above = shift(piece, axis, -1)
    far_low = shift(below[:half], axis, 1)
    far_high = shift(above[half:], axis, -1)
    return [(piece,), (above,), (far_low, far_high), (below,)]


def scatter_ring(block, axis, index):
    add = lambda one, two: (one.astype(F32) + two.astype(F32)).astype(BF)
    far = block((index + 2) % 4)
    half = far.shape[0] // 2
    from_below = shift(far[:half], axis, 1)
    from_above = shift(far[half:], axis, -1)
    up = block((index + 1) % 4)
    up = jnp.concatenate([add(up[:half], from_below), up[half:]])
    down = block((index + 3) % 4)
    down = jnp.concatenate([down[:half], add(down[half:], from_above)])
    got_up = shift(up, axis, 1)
    got_down = shift(down, axis, -1)
    return block(index).astype(F32) + got_up.astype(F32) + got_down.astype(F32)


def dot(left, right):
    return jnp.dot(left, right, preferred_element_type=F32)


def dot_nt(left, right):
    return lax.dot_general(left, right, (((1,), (1,)), ((), ())), preferred_element_type=F32)


def dot_tn(left, right):
    return lax.dot_general(left, right, (((0,), (0,)), ((), ())), preferred_element_type=F32)


def attention_kernel(q_ref, ko_ref, kp_ref, vo_ref, vp_ref, out_ref, lse_ref):
    rows = q_ref.shape[0]
    step = 256
    for h in range(2):
        cols = slice(HEAD * h, HEAD * (h + 1))
        keys_own, keys_peer = ko_ref[:, cols], kp_ref[:, cols]
        values_own, values_peer = vo_ref[:, cols], vp_ref[:, cols]
        for start in range(0, rows, step):
            queries = q_ref[start : start + step, cols] * HEAD ** (-0.5)
            scores_own = dot_nt(keys_own, queries)
            scores_peer = dot_nt(keys_peer, queries)
            top = jnp.maximum(
                jnp.max(scores_own, axis=0, keepdims=True),
                jnp.max(scores_peer, axis=0, keepdims=True),
            )
            probs_own = jnp.exp(scores_own - top)
            probs_peer = jnp.exp(scores_peer - top)
            total = jnp.sum(probs_own, axis=0, keepdims=True) + jnp.sum(
                probs_peer, axis=0, keepdims=True
            )
            mixed = dot_tn(values_own, probs_own.astype(BF)) + dot_tn(
                values_peer, probs_peer.astype(BF)
            )
            mixed = mixed / total
            out_ref[start : start + step, cols] = mixed.T.astype(BF)
            lse_ref[0, h : h + 1, start : start + step] = top + jnp.log(total)


def attention(queries, kv_own, kv_peer):
    rows, width = queries.shape
    pairs = width // 128
    block = lambda offset: pl.BlockSpec((rows, 128), lambda h: (0, h + offset))
    return pl.pallas_call(
        attention_kernel,
        grid=(pairs,),
        in_specs=[block(0), block(0), block(0), block(pairs), block(pairs)],
        out_specs=[block(0), pl.BlockSpec((1, 2, rows), lambda h: (h, 0, 0))],
        out_shape=[
            jax.ShapeDtypeStruct((rows, width), BF),
            jax.ShapeDtypeStruct((pairs, 2, rows), F32),
        ],
        compiler_params=pltpu.CompilerParams(vmem_limit_bytes=40 * 2**20),
        cost_estimate=pl.CostEstimate(
            flops=8 * rows * rows * width,
            bytes_accessed=12 * rows * width,
            transcendentals=2 * rows * rows * width // HEAD,
        ),
        name="attention",
    )(queries, kv_own, kv_peer, kv_own, kv_peer)


def attention_back_kernel(
    q_ref, ko_ref, kp_ref, vo_ref, vp_ref, out_ref, gout_ref, lse_ref, gq_ref, go_ref, gp_ref
):
    rows = q_ref.shape[0]
    step = 256
    scale = HEAD ** (-0.5)
    for h in range(2):
        cols = slice(HEAD * h, HEAD * (h + 1))
        sides = ((ko_ref, vo_ref, go_ref), (kp_ref, vp_ref, gp_ref))
        grad_kv = [[None, None], [None, None]]
        for start in range(0, rows, step):
            span = slice(start, start + step)
            queries = q_ref[span, cols] * scale
            grad_out = gout_ref[span, cols]
            lse = lse_ref[0, h : h + 1, span]
            both = grad_out.astype(F32) * out_ref[span, cols].astype(F32)
            row_total = jnp.sum(both.T, axis=0, keepdims=True)
            grad_queries = None
            for side, (k_ref, v_ref, g_ref) in enumerate(sides):
                keys, values = k_ref[:, cols], v_ref[:, cols]
                probs = jnp.exp(dot_nt(keys, queries) - lse)
                grad_probs = dot_nt(values, grad_out)
                grad_scores = (probs * (grad_probs - row_total)).astype(BF)
                part = dot_tn(keys, grad_scores)
                grad_queries = part if grad_queries is None else grad_queries + part
                terms = (dot(grad_scores, queries), dot(probs.astype(BF), grad_out))
                for i in range(2):
                    old = grad_kv[side][i]
                    grad_kv[side][i] = terms[i] if old is None else old + terms[i]
            gq_ref[span, cols] = (grad_queries * scale).T.astype(BF)
        for side, (k_ref, v_ref, g_ref) in enumerate(sides):
            for i in range(2):
                g_ref[i, :, cols] = grad_kv[side][i].astype(g_ref.dtype)


def attention_back(queries, kv_own, kv_peer, mixed, grad_mixed, lse):
    rows, width = queries.shape
    pairs = width // 128
    block = lambda offset: pl.BlockSpec((rows, 128), lambda h: (0, h + offset))
    double = pl.BlockSpec((2, rows, 128), lambda h: (0, 0, h))
    return pl.pallas_call(
        attention_back_kernel,
        grid=(pairs,),
        in_specs=[
            block(0),
            block(0),
            block(0),
            block(pairs),
            block(pairs),
            block(0),
            block(0),
            pl.BlockSpec((1, 2, rows), lambda h: (h, 0, 0)),
        ],
        out_specs=[block(0), double, double],
        out_shape=[
            jax.ShapeDtypeStruct((rows, width), BF),
            jax.ShapeDtypeStruct((2, rows, width), F32),
            jax.ShapeDtypeStruct((2, rows, width), BF),
        ],
        compiler_params=pltpu.CompilerParams(vmem_limit_bytes=40 * 2**20),
        cost_estimate=pl.CostEstimate(
            flops=20 * rows * rows * width,
            bytes_accessed=24 * rows * width,
            transcendentals=2 * rows * rows * width // HEAD,
        ),
        name="attention_back",
    )(queries, kv_own, kv_peer, kv_own, kv_peer, mixed, grad_mixed, lse)


def norm_stats(activations):
    center = activations - jnp.mean(activations, axis=-1, keepdims=True)
    inverse = lax.rsqrt(jnp.mean(center * center, axis=-1, keepdims=True) + 1e-06)
    return (center * inverse, inverse)


def norm_back(grad_norm, normal, inverse):
    return inverse * (
        grad_norm
        - jnp.mean(grad_norm, axis=-1, keepdims=True)
        - normal * jnp.mean(grad_norm * normal, axis=-1, keepdims=True)
    )


def core_sum(partial_sum):
    low = partial_sum.astype(BF)
    return low.astype(F32) + swap(low, "core").astype(F32)


def gelu_and_slope(pre_act):
    linear = 2.0 * (2.0 / jnp.pi) ** 0.5
    cubic = 0.044715 * linear
    square = pre_act * pre_act
    gate = 1.0 / (1.0 + jnp.exp(-pre_act * (linear + cubic * square)))
    value = pre_act * gate
    slope = gate + value * (1.0 - gate) * (linear + 3.0 * cubic * square)
    return value.astype(BF), slope.astype(BF)


def layer_forward(activations, modulation, weights):
    w_q, w_kv, w_out, w_fc1, w_fc2 = weights
    shift_first, scale_first, gate_first, shift_second, scale_second, gate_second = modulation
    normal_first, inverse_first = norm_stats(activations)
    entry = (normal_first * (1.0 + scale_first) + shift_first).astype(BF)
    kv_own = dot(entry, w_kv).astype(BF)
    kv_peer = swap(kv_own, "xl")
    queries = dot(entry, w_q).astype(BF)
    mixed, lse = attention(queries, kv_own, kv_peer)
    branch = core_sum(dot(mixed, w_out))
    second = activations + gate_first * branch
    normal_second, inverse_second = norm_stats(second)
    mlp_input = (normal_second * (1.0 + scale_second) + shift_second).astype(BF)
    pre_act = dot(mlp_input, w_fc1)
    hidden, slope = gelu_and_slope(pre_act)
    branch_mlp = core_sum(dot(hidden, w_fc2))
    result = second + gate_second * branch_mlp
    state = (
        normal_first,
        inverse_first,
        entry,
        queries,
        kv_own,
        kv_peer,
        lse,
        mixed,
        branch,
        normal_second,
        inverse_second,
        mlp_input,
        slope,
        hidden,
        branch_mlp,
    )
    return (result, state)


def layer_backward(grad_result, state, modulation, weights):
    w_q, w_kv, w_out, w_fc1, w_fc2 = weights
    shift_first, scale_first, gate_first, shift_second, scale_second, gate_second = modulation
    (
        normal_first,
        inverse_first,
        entry,
        queries,
        kv_own,
        kv_peer,
        lse,
        mixed,
        branch,
        normal_second,
        inverse_second,
        mlp_input,
        slope,
        hidden,
        branch_mlp,
    ) = state
    rows = lambda value: jnp.sum(value, axis=0)
    grad_gate_second = rows(grad_result * branch_mlp)
    grad_branch_mlp = (grad_result * gate_second).astype(BF)
    grad_hidden = dot_nt(grad_branch_mlp, w_fc2)
    grad_pre = (grad_hidden * slope.astype(F32)).astype(BF)
    grad_mlp_input = core_sum(dot_nt(grad_pre, w_fc1))
    grad_fc2 = dot_tn(hidden, grad_branch_mlp).astype(BF)
    grad_fc1 = dot_tn(mlp_input, grad_pre).astype(BF)
    grad_scale_second = rows(grad_mlp_input * normal_second)
    grad_shift_second = rows(grad_mlp_input)
    grad_second = grad_result + norm_back(
        grad_mlp_input * (1.0 + scale_second), normal_second, inverse_second
    )
    grad_gate_first = rows(grad_second * branch)
    grad_branch = (grad_second * gate_first).astype(BF)
    grad_mixed = dot_nt(grad_branch, w_out).astype(BF)
    grad_out = dot_tn(mixed, grad_branch).astype(BF)
    grad_queries, grad_own, grad_peer = attention_back(
        queries, kv_own, kv_peer, mixed, grad_mixed, lse
    )
    grad_kv = (grad_own + swap(grad_peer, "xl").astype(F32)).astype(BF)
    grad_kv = jnp.concatenate([grad_kv[0], grad_kv[1]], axis=1)
    grad_entry = core_sum(dot_nt(grad_queries, w_q) + dot_nt(grad_kv, w_kv))
    grad_q_proj = dot_tn(entry, grad_queries).astype(BF)
    grad_kv_proj = dot_tn(entry, grad_kv).astype(BF)
    grad_scale_first = rows(grad_entry * normal_first)
    grad_shift_first = rows(grad_entry)
    grad_input = grad_second + norm_back(
        grad_entry * (1.0 + scale_first), normal_first, inverse_first
    )
    grad_modulation = jnp.stack(
        [
            grad_shift_first,
            grad_scale_first,
            grad_gate_first,
            grad_shift_second,
            grad_scale_second,
            grad_gate_second,
        ]
    )
    return (grad_input, grad_modulation, (grad_q_proj, grad_kv_proj, grad_out, grad_fc1, grad_fc2))


def sum_over_plane(block):
    x = lax.axis_index(RING_X)
    half, quarter = (x + 1) // 2 % 2, x // 2
    rows, columns = block.shape
    parts = block.astype(BF).reshape(2, rows // 2, columns)
    part = pick(parts, half).astype(F32) + swap(pick(parts, 1 - half), "xl").astype(F32)
    parts = part.astype(BF).reshape(2, rows // 4, columns)
    part = pick(parts, quarter).astype(F32) + swap_odd(pick(parts, 1 - quarter), RING_X).astype(F32)
    part = part.astype(BF)
    part = (part.astype(F32) + swap(part, "zh").astype(F32)).astype(BF)
    part = ordered(quarter == 0, part, swap_odd(part, RING_X))
    return ordered(half == 0, part, swap(part, "xl"))


def fill_fc_kernel(core_ref, mine_ref, other_ref, fc1_ref, fc2_ref):
    half = mine_ref.shape[1] // 2
    rows = fc1_ref.shape[0]
    first = core_ref[0] == 0
    mine, other = mine_ref[...].astype(F32), other_ref[...].astype(F32)
    for c, part in enumerate((jnp.where(first, mine, other), jnp.where(first, other, mine))):
        fc2_ref[half * c : half * (c + 1), :] = part[:half]
        for j in range(4):
            top = half + rows * (j // 2)
            left = half * (j % 2)
            to = half * (2 * j + c)
            fc1_ref[:, to : to + half] = part[top : top + rows, left : left + half]


def fill_attn_kernel(core_ref, mine_ref, other_ref, qkv_ref, out_ref):
    rows, width = out_ref.shape
    half = width // 2
    first = core_ref[0] == 0
    mine, other = mine_ref[...].astype(F32), other_ref[...].astype(F32)
    for c, part in enumerate((jnp.where(first, mine, other), jnp.where(first, other, mine))):
        at = half * c
        qkv_ref[:, at : at + half] = part[rows:, :half]
        qkv_ref[:, width + at : width + at + half] = part[:rows, :half]
        qkv_ref[:, 2 * width + at : 2 * width + at + half] = part[:rows, half:]
        out_ref[:, at : at + half] = part[rows:, half:]


def fill(kernel, core, total, shapes, name):
    whole = pl.BlockSpec(memory_space=pltpu.VMEM)
    return pl.pallas_call(
        kernel,
        in_specs=[pl.BlockSpec(memory_space=pltpu.SMEM), whole, whole],
        out_specs=[whole] * len(shapes),
        out_shape=[jax.ShapeDtypeStruct(shape, F32) for shape in shapes],
        compiler_params=pltpu.CompilerParams(vmem_limit_bytes=40 * 2**20),
        cost_estimate=pl.CostEstimate(flops=0, bytes_accessed=12 * total.size, transcendentals=0),
        name=name,
    )(core.astype(jnp.int32).reshape(1), total, swap(total, "core"))


def on_device(ends, cond, w_ada, b_ada, w_qkv, w_out, w_fc1, w_fc2):
    section = lax.axis_index("section")
    d = lax.axis_index("dp")
    zh, xh = lax.axis_index("zh"), lax.axis_index("xh")
    a = zh * 2 + xh
    core = lax.axis_index("core")
    width = w_out.shape[2]
    half = width // 2
    rows_d = w_out.shape[1]
    columns = lambda array, start: lax.dynamic_slice_in_dim(array, start, half, 1)

    cond_float = cond.astype(F32).reshape(4, width)
    cond_low = jax.nn.silu(cond_float).astype(BF)
    all_cond = gather_small(cond_low, "dp", d)
    all_cond = pick(all_cond.reshape(16, 4, rows_d).transpose(1, 0, 2), d)

    blocks = ends[0].reshape(2, 2, *ends.shape[3:])
    mine = lax.dynamic_index_in_dim(blocks, xh, 1, keepdims=False)
    theirs = lax.dynamic_index_in_dim(blocks, 1 - xh, 1, keepdims=False)
    blocks = jnp.stack([mine, swap(theirs, "xh")], axis=1)
    mine = jnp.stack([pick(blocks, zh), swap(pick(blocks, 1 - zh), "zh")])
    mine = mine.reshape(-1, width)
    tokens_half = mine.shape[0]
    start = ordered(core == 0, mine, swap(mine, "core"))

    piece_attn = jnp.concatenate(
        [columns(w_qkv[0], width * i + half * core) for i in range(3)]
        + [columns(w_out[0], half * core)],
        axis=1,
    )
    attn_blocks = gather_ring(piece_attn, "dp")

    latent_rows = pick(all_cond.reshape(4, 4, rows_d).transpose(1, 0, 2), a)
    part_mod = dot(latent_rows, w_ada[0])
    bias = lax.dynamic_update_slice(
        jnp.zeros((6 * width,), F32), b_ada[0].astype(F32), (d * b_ada.shape[1],)
    )
    part_mod = (part_mod + bias[None]).reshape(2, 2, 6 * width)
    part_mod = pick(part_mod, d // 2) + swap_odd(pick(part_mod, 1 - d // 2), "dp")
    part_mod = part_mod.reshape(2, 1, 6 * width)
    modulation = pick(part_mod, d % 2) + swap_even(pick(part_mod, 1 - d % 2), "dp")
    modulation = [modulation[:, width * i : width * (i + 1)] for i in range(6)]

    piece_fc = jnp.concatenate(
        [rows_at(w_fc2[0], half * core, half)]
        + [
            jnp.concatenate(
                [columns(w_fc1[0], width * j + half * core) for j in (2 * i, 2 * i + 1)], axis=1
            )
            for i in range(2)
        ]
    )
    piece_fc, unused = lax.optimization_barrier((piece_fc, attn_blocks[2]))
    fc_blocks = gather_ring(piece_fc, "dp")

    full_attn = jnp.zeros((width, 4 * half), BF)
    for s, parts in enumerate(attn_blocks):
        at = (d + s) % 4 * rows_d
        for part in parts:
            full_attn = lax.dynamic_update_slice(full_attn, part, (at, 0))
            at = at + part.shape[0]
    out_rows = full_attn[:, 3 * half :].reshape(2, half, half)
    full_out = ordered(
        core == 0, pick(out_rows, core), swap(pick(out_rows, 1 - core), "core"), axis=1
    )
    full_fc1 = jnp.zeros((width, 4 * half), BF)
    full_fc2 = jnp.zeros((4 * half, width), BF)
    for s, parts in enumerate(fc_blocks):
        place = (d + s) % 4
        fc2_part = parts[0][:half]
        fc1_part = parts[0][half:] if len(parts) == 1 else parts[1]
        full_fc2 = lax.dynamic_update_slice(full_fc2, fc2_part, (place * half, 0))
        full_fc1 = lax.dynamic_update_slice(full_fc1, fc1_part[:rows_d], (place * rows_d, 0))
        full_fc1 = lax.dynamic_update_slice(full_fc1, fc1_part[rows_d:], (place * rows_d, width))
    weights = (full_attn[:, :half], full_attn[:, half : 3 * half], full_out, full_fc1, full_fc2)

    def across(value, pairs):
        part = rows_at(value.astype(BF), core * tokens_half, tokens_half)
        part = lax.ppermute(part, "section", pairs)
        return ordered(core == 0, part, swap(part, "core"))

    result, unused = layer_forward(start.astype(F32), modulation, weights)
    arrived = across(result, [(0, 1)])
    second_input = jnp.where(section == 0, start, arrived).astype(F32)
    result, state = layer_forward(second_input, modulation, weights)

    grad_input, unused, unused_too = layer_backward(start.astype(F32), state, modulation, weights)
    arrived = across(grad_input, [(1, 0)])
    seed = jnp.where(section == 0, arrived, start).astype(F32)
    grad_input, grad_modulation, grads = layer_backward(seed, state, modulation, weights)
    grad_q, grad_kv, grad_out, grad_fc1, grad_fc2 = grads

    def block_fc(i):
        one = rows_at(grad_fc1, i * rows_d, rows_d)
        return jnp.concatenate([rows_at(grad_fc2, i * half, half), one[:, :width], one[:, width:]])

    sum_fc = sum_over_plane(scatter_ring(block_fc, "dp", d))
    out_fc1, out_fc2 = fill(
        fill_fc_kernel, core, sum_fc, ((rows_d, 8 * half), (2 * half, width)), "fill_fc"
    )
    out_own = ordered(
        core == 0,
        columns(grad_out, half * core),
        swap(columns(grad_out, half - half * core), "core"),
    )

    def block_attn(i):
        kv, q, out = (rows_at(g, i * rows_d, rows_d) for g in (grad_kv, grad_q, out_own))
        return jnp.concatenate([kv, jnp.concatenate([q, out], axis=1)])

    sum_attn = sum_over_plane(scatter_ring(block_attn, "dp", d))
    out_qkv, out_out = fill(
        fill_attn_kernel, core, sum_attn, ((rows_d, 6 * half), (rows_d, width)), "fill_attn"
    )

    grad_mod = grad_modulation.reshape(1, 6 * width)
    grad_mod = grad_mod + swap(grad_mod, "xl")
    plane_mod = ordered(xh == 0, grad_mod, swap(grad_mod, "xh"))
    plane_mod = ordered(zh == 0, plane_mod, swap(plane_mod, "zh"))
    all_mod = gather_small(plane_mod, "dp", d)
    out_ada = lax.dot_general(
        all_cond.astype(F32), all_mod, (((0,), (0,)), ((), ())), precision=lax.Precision.HIGHEST
    )
    out_bias = jnp.sum(
        lax.dynamic_slice_in_dim(all_mod, d * b_ada.shape[1], b_ada.shape[1], 1), axis=0
    )
    grad_silu = lax.dot_general(
        all_mod,
        w_ada[0].astype(F32),
        (((1,), (1,)), ((), ())),
        precision=lax.Precision.HIGHEST,
    ).reshape(2, 2, 4, rows_d)
    same = jnp.stack([pick(grad_silu, d // 2), swap_odd(pick(grad_silu, 1 - d // 2), "dp")], axis=1)
    got = swap_even(pick(same, 1 - d % 2), "dp")
    same = pick(same, d % 2)
    silu_full = jnp.zeros((4, 4, rows_d), F32)
    beside = d + 1 - 2 * (d % 2)
    for part, place in ((same[0], d), (same[1], 3 - d), (got[0], beside), (got[1], 3 - beside)):
        silu_full = lax.dynamic_update_index_in_dim(silu_full, part, place, 0)
    silu_full = silu_full.transpose(1, 0, 2).reshape(4, width)
    silu_full = silu_full + swap(silu_full, "section")
    unused, silu_pull = jax.vjp(jax.nn.silu, cond_float)
    out_cond = silu_pull(silu_full)[0].reshape(cond.shape)

    edge = jnp.where(section == 0, grad_input, result)
    edge = rows_at(edge, core * tokens_half, tokens_half).reshape(2, 2, -1, width)
    edge = ordered(zh == 0, edge[:1], swap(edge[1:].astype(BF), "zh").astype(F32))
    boundary = ordered(
        xh == 0, edge[:, :1], swap(edge[:, 1:].astype(BF), "xh").astype(F32), axis=1
    ).reshape(ends.shape)

    return (
        boundary,
        out_cond,
        out_ada[None],
        out_bias[None],
        out_qkv[None],
        out_out[None],
        out_fc1[None],
        out_fc2[None],
    )


def solution(mesh):
    finer = Mesh(
        mesh.devices.reshape(2, 4, 2, 2, 2, 2), ("section", "dp", "zh", "xh", "xl", "core")
    )
    ends_spec = P("section", None, "dp", CTX, None)
    cond_spec = P(None, "dp", None)
    matrix = P("section", "dp", None)
    vector = P("section", "dp")
    return jax.shard_map(
        on_device,
        mesh=finer,
        in_specs=(ends_spec, cond_spec, matrix, vector, matrix, matrix, matrix, matrix),
        out_specs=(ends_spec, cond_spec, matrix, vector, matrix, matrix, matrix, matrix),
        check_vma=False,
    )
```

```python
import jax
import jax.numpy as jnp
from jax import lax
from jax.experimental import pallas as pl
from jax.experimental.pallas import tpu as pltpu
from jax.sharding import Mesh
from jax.sharding import PartitionSpec as P

HEAD = 64
BF = jnp.bfloat16
F32 = jnp.float32
RING_X = ("xh", "xl")
CTX = ("zh", "xh", "xl", "core")


def shift(array, axis, by, size=4):
    return lax.ppermute(array, axis, [(i, (i + by) % size) for i in range(size)])


def swap(array, axis):
    return lax.ppermute(array, axis, [(0, 1), (1, 0)])


def swap_odd(array, axis):
    return lax.ppermute(array, axis, [(0, 3), (1, 2), (2, 1), (3, 0)])


def swap_even(array, axis):
    return lax.ppermute(array, axis, [(0, 1), (1, 0), (2, 3), (3, 2)])


def pick(blocks, index):
    return lax.dynamic_index_in_dim(blocks, index, 0, keepdims=False)


def rows_at(array, start, size):
    return lax.dynamic_slice_in_dim(array, start, size, 0)


def ordered(first, mine, other, axis=0):
    return jnp.where(
        first,
        jnp.concatenate([mine, other], axis=axis),
        jnp.concatenate([other, mine], axis=axis),
    )


def gather_small(piece, axis, index):
    two = ordered(index % 2 == 0, piece, swap_even(piece, axis))
    return ordered(index < 2, two, swap_odd(two, axis))


def gather_near(piece, axis):
    return shift(piece, axis, 1), shift(piece, axis, -1)


def gather_far(piece, below, above, axis):
    half = piece.shape[0] // 2
    far_low = shift(below[:half], axis, 1)
    far_high = shift(above[half:], axis, -1)
    return [(piece,), (above,), (far_low, far_high), (below,)]


def scatter_ring(block, axis, index, after=None):
    add = lambda one, two: (one.astype(F32) + two.astype(F32)).astype(BF)
    far = block((index + 2) % 4)
    half = far.shape[0] // 2
    from_below = shift(far[:half], axis, 1)
    from_above = shift(far[half:], axis, -1)
    if after is not None:
        from_below, from_above, after = lax.optimization_barrier((from_below, from_above, after))
    up = block((index + 1) % 4)
    up = jnp.concatenate([add(up[:half], from_below), up[half:]])
    down = block((index + 3) % 4)
    down = jnp.concatenate([down[:half], add(down[half:], from_above)])
    got_up = shift(up, axis, 1)
    got_down = shift(down, axis, -1)
    return block(index).astype(F32) + got_up.astype(F32) + got_down.astype(F32)


def dot(left, right):
    return jnp.dot(left, right, preferred_element_type=F32)


def dot_nt(left, right):
    return lax.dot_general(left, right, (((1,), (1,)), ((), ())), preferred_element_type=F32)


def dot_tn(left, right):
    return lax.dot_general(left, right, (((0,), (0,)), ((), ())), preferred_element_type=F32)


def attention_kernel(q_ref, ko_ref, kp_ref, vo_ref, vp_ref, out_ref, lse_ref):
    rows = q_ref.shape[0]
    step = 256
    for h in range(2):
        cols = slice(HEAD * h, HEAD * (h + 1))
        keys_own, keys_peer = ko_ref[:, cols], kp_ref[:, cols]
        values_own, values_peer = vo_ref[:, cols], vp_ref[:, cols]
        for start in range(0, rows, step):
            queries = q_ref[start : start + step, cols] * HEAD ** (-0.5)
            scores_own = dot_nt(keys_own, queries)
            scores_peer = dot_nt(keys_peer, queries)
            top = jnp.maximum(
                jnp.max(scores_own, axis=0, keepdims=True),
                jnp.max(scores_peer, axis=0, keepdims=True),
            )
            probs_own = jnp.exp(scores_own - top)
            probs_peer = jnp.exp(scores_peer - top)
            total = jnp.sum(probs_own, axis=0, keepdims=True) + jnp.sum(
                probs_peer, axis=0, keepdims=True
            )
            mixed = dot_tn(values_own, probs_own.astype(BF)) + dot_tn(
                values_peer, probs_peer.astype(BF)
            )
            mixed = mixed / total
            out_ref[start : start + step, cols] = mixed.T.astype(BF)
            lse_ref[0, h : h + 1, start : start + step] = top + jnp.log(total)


def attention(queries, kv_own, kv_peer):
    rows, width = queries.shape
    pairs = width // 128
    block = lambda offset: pl.BlockSpec((rows, 128), lambda h: (0, h + offset))
    return pl.pallas_call(
        attention_kernel,
        grid=(pairs,),
        in_specs=[block(0), block(0), block(0), block(pairs), block(pairs)],
        out_specs=[block(0), pl.BlockSpec((1, 2, rows), lambda h: (h, 0, 0))],
        out_shape=[
            jax.ShapeDtypeStruct((rows, width), BF),
            jax.ShapeDtypeStruct((pairs, 2, rows), F32),
        ],
        compiler_params=pltpu.CompilerParams(vmem_limit_bytes=40 * 2**20),
        cost_estimate=pl.CostEstimate(
            flops=8 * rows * rows * width,
            bytes_accessed=12 * rows * width,
            transcendentals=2 * rows * rows * width // HEAD,
        ),
        name="attention",
    )(queries, kv_own, kv_peer, kv_own, kv_peer)


def attention_back_kernel(
    q_ref, ko_ref, kp_ref, vo_ref, vp_ref, out_ref, gout_ref, lse_ref, gq_ref, gk_ref, gv_ref
):
    rows = q_ref.shape[0]
    step = 256
    scale = HEAD ** (-0.5)
    for h in range(2):
        cols = slice(HEAD * h, HEAD * (h + 1))
        sides = ((ko_ref, vo_ref), (kp_ref, vp_ref))
        grad_kv = [[None, None], [None, None]]
        for start in range(0, rows, step):
            span = slice(start, start + step)
            queries = q_ref[span, cols] * scale
            grad_out = gout_ref[span, cols]
            lse = lse_ref[0, h : h + 1, span]
            both = grad_out.astype(F32) * out_ref[span, cols].astype(F32)
            row_total = jnp.sum(both.T, axis=0, keepdims=True)
            grad_queries = None
            for side, (k_ref, v_ref) in enumerate(sides):
                keys, values = k_ref[:, cols], v_ref[:, cols]
                probs = jnp.exp(dot_nt(keys, queries) - lse)
                grad_probs = dot_nt(values, grad_out)
                grad_scores = (probs * (grad_probs - row_total)).astype(BF)
                part = dot_tn(keys, grad_scores)
                grad_queries = part if grad_queries is None else grad_queries + part
                terms = (dot(grad_scores, queries), dot(probs.astype(BF), grad_out))
                for i in range(2):
                    old = grad_kv[side][i]
                    grad_kv[side][i] = terms[i] if old is None else old + terms[i]
            gq_ref[span, cols] = (grad_queries * scale).T.astype(BF)
        for side in range(2):
            span = slice(rows * side, rows * (side + 1))
            gk_ref[span, cols] = grad_kv[side][0].astype(BF)
            gv_ref[span, cols] = grad_kv[side][1].astype(BF)


def attention_back(queries, kv_own, kv_peer, mixed, grad_mixed, lse):
    rows, width = queries.shape
    pairs = width // 128
    block = lambda offset: pl.BlockSpec((rows, 128), lambda h: (0, h + offset))
    double = pl.BlockSpec((2 * rows, 128), lambda h: (0, h))
    return pl.pallas_call(
        attention_back_kernel,
        grid=(pairs,),
        in_specs=[
            block(0),
            block(0),
            block(0),
            block(pairs),
            block(pairs),
            block(0),
            block(0),
            pl.BlockSpec((1, 2, rows), lambda h: (h, 0, 0)),
        ],
        out_specs=[block(0), double, double],
        out_shape=[
            jax.ShapeDtypeStruct((rows, width), BF),
            jax.ShapeDtypeStruct((2 * rows, width), BF),
            jax.ShapeDtypeStruct((2 * rows, width), BF),
        ],
        compiler_params=pltpu.CompilerParams(vmem_limit_bytes=40 * 2**20),
        cost_estimate=pl.CostEstimate(
            flops=20 * rows * rows * width,
            bytes_accessed=24 * rows * width,
            transcendentals=2 * rows * rows * width // HEAD,
        ),
        name="attention_back",
    )(queries, kv_own, kv_peer, kv_own, kv_peer, mixed, grad_mixed, lse)


def norm_stats(activations):
    center = activations - jnp.mean(activations, axis=-1, keepdims=True)
    inverse = lax.rsqrt(jnp.mean(center * center, axis=-1, keepdims=True) + 1e-06)
    return (center * inverse, inverse)


def norm_back(grad_norm, normal, inverse):
    return inverse * (
        grad_norm
        - jnp.mean(grad_norm, axis=-1, keepdims=True)
        - normal * jnp.mean(grad_norm * normal, axis=-1, keepdims=True)
    )


def core_sum(partial_sum):
    low = partial_sum.astype(BF)
    return low.astype(F32) + swap(low, "core").astype(F32)


def gelu_and_slope(pre_act):
    linear = 2.0 * (2.0 / jnp.pi) ** 0.5
    cubic = 0.044715 * linear
    square = pre_act * pre_act
    gate = 1.0 / (1.0 + jnp.exp(-pre_act * (linear + cubic * square)))
    value = pre_act * gate
    slope = gate + value * (1.0 - gate) * (linear + 3.0 * cubic * square)
    return value.astype(BF), slope.astype(BF)


def attend(activations, activations_peer, modulation, weights, together=lambda value: value):
    w_q, w_kv, w_out = weights
    shift_first, scale_first, gate_first = modulation[:3]
    normal_first, inverse_first = norm_stats(activations)
    entry = (normal_first * (1.0 + scale_first) + shift_first).astype(BF)
    entry_peer = norm_stats(activations_peer)[0] * (1.0 + scale_first) + shift_first
    entry_peer = entry_peer.astype(BF)
    kv_own = dot(entry, w_kv).astype(BF)
    queries = together(dot(entry, w_q).astype(BF))
    kv_peer = dot(entry_peer, w_kv).astype(BF)
    mixed, lse = attention(queries, kv_own, kv_peer)
    branch = core_sum(dot(mixed, w_out))
    second = activations + gate_first * branch
    return (
        second,
        normal_first,
        inverse_first,
        entry,
        entry_peer,
        queries,
        kv_own,
        kv_peer,
        lse,
        mixed,
        branch,
    )


def feed_forward(attn_state, modulation, weights):
    w_fc1, w_fc2 = weights
    shift_second, scale_second, gate_second = modulation[3:]
    second, *kept = attn_state
    normal_second, inverse_second = norm_stats(second)
    mlp_input = (normal_second * (1.0 + scale_second) + shift_second).astype(BF)
    hidden, slope = gelu_and_slope(dot(mlp_input, w_fc1))
    branch_mlp = core_sum(dot(hidden, w_fc2))
    result = second + gate_second * branch_mlp
    state = (*kept, normal_second, inverse_second, mlp_input, slope, hidden, branch_mlp)
    return (result, state)


def layer_backward(grad_result, state, modulation, weights, core):
    w_q, w_kv, w_out, w_fc1, w_fc2 = weights
    shift_first, scale_first, gate_first, shift_second, scale_second, gate_second = modulation
    (
        normal_first,
        inverse_first,
        entry,
        entry_peer,
        queries,
        kv_own,
        kv_peer,
        lse,
        mixed,
        branch,
        normal_second,
        inverse_second,
        mlp_input,
        slope,
        hidden,
        branch_mlp,
    ) = state
    rows = lambda value: jnp.sum(value, axis=0)
    grad_gate_second = rows(grad_result * branch_mlp)
    grad_branch_mlp = (grad_result * gate_second).astype(BF)
    grad_hidden = dot_nt(grad_branch_mlp, w_fc2)
    grad_pre = (grad_hidden * slope.astype(F32)).astype(BF)
    grad_mlp_input = core_sum(dot_nt(grad_pre, w_fc1))
    grad_fc2 = dot_tn(hidden, grad_branch_mlp).astype(BF)
    grad_fc1 = dot_tn(mlp_input, grad_pre).astype(BF)
    grad_scale_second = rows(grad_mlp_input * normal_second)
    grad_shift_second = rows(grad_mlp_input)
    grad_second = grad_result + norm_back(
        grad_mlp_input * (1.0 + scale_second), normal_second, inverse_second
    )
    grad_gate_first = rows(grad_second * branch)
    grad_branch = (grad_second * gate_first).astype(BF)
    grad_mixed = dot_nt(grad_branch, w_out).astype(BF)
    grad_out = dot_tn(mixed, grad_branch).astype(BF)
    grad_queries, grad_keys, grad_values = attention_back(
        queries, kv_own, kv_peer, mixed, grad_mixed, lse
    )
    tokens, half = mixed.shape
    w_k, w_v = w_kv[:, :half], w_kv[:, half:]
    far = (
        dot_nt(grad_keys[tokens:], w_k) + dot_nt(grad_values[tokens:], w_v)
    ).astype(BF)
    kept = rows_at(far, core * (tokens // 2), tokens // 2)
    given = rows_at(far, (1 - core) * (tokens // 2), tokens // 2)
    far = (kept.astype(F32) + swap(given, "core").astype(F32)).astype(BF)
    far = swap(far, "xl")
    far = ordered(core == 0, far, swap(far, "core"))
    near = (
        dot_nt(grad_queries, w_q)
        + dot_nt(grad_keys[:tokens], w_k)
        + dot_nt(grad_values[:tokens], w_v)
    )
    grad_entry = core_sum(near) + far.astype(F32)
    entry_all = jnp.concatenate([entry, entry_peer])
    grad_q_proj = dot_tn(entry, grad_queries).astype(BF)
    grad_k_proj = dot_tn(entry_all, grad_keys).astype(BF)
    grad_v_proj = dot_tn(entry_all, grad_values).astype(BF)
    grad_scale_first = rows(grad_entry * normal_first)
    grad_shift_first = rows(grad_entry)
    grad_input = grad_second + norm_back(
        grad_entry * (1.0 + scale_first), normal_first, inverse_first
    )
    grad_modulation = jnp.stack(
        [
            grad_shift_first,
            grad_scale_first,
            grad_gate_first,
            grad_shift_second,
            grad_scale_second,
            grad_gate_second,
        ]
    )
    grads = (grad_q_proj, grad_k_proj, grad_v_proj, grad_out, grad_fc1, grad_fc2)
    return (grad_input, grad_modulation, grads)


def sum_over_plane(block):
    x = lax.axis_index(RING_X)
    half, quarter = (x + 1) // 2 % 2, x // 2
    rows, columns = block.shape
    parts = block.astype(BF).reshape(2, rows // 2, columns)
    part = pick(parts, half).astype(F32) + swap(pick(parts, 1 - half), "xl").astype(F32)
    parts = part.astype(BF).reshape(2, rows // 4, columns)
    part = pick(parts, quarter).astype(F32) + swap_odd(pick(parts, 1 - quarter), RING_X).astype(F32)
    part = part.astype(BF)
    part = (part.astype(F32) + swap(part, "zh").astype(F32)).astype(BF)
    part = ordered(quarter == 0, part, swap_odd(part, RING_X))
    return ordered(half == 0, part, swap(part, "xl"))


def fill_fc_kernel(core_ref, mine_ref, other_ref, fc1_ref, fc2_ref):
    half = mine_ref.shape[1] // 2
    rows = fc1_ref.shape[0]
    first = core_ref[0] == 0
    mine, other = mine_ref[...].astype(F32), other_ref[...].astype(F32)
    for c, part in enumerate((jnp.where(first, mine, other), jnp.where(first, other, mine))):
        fc2_ref[half * c : half * (c + 1), :] = part[:half]
        for j in range(4):
            top = half + rows * (j // 2)
            left = half * (j % 2)
            to = half * (2 * j + c)
            fc1_ref[:, to : to + half] = part[top : top + rows, left : left + half]


def fill_attn_kernel(core_ref, mine_ref, other_ref, qkv_ref, out_ref):
    rows, width = out_ref.shape
    half = width // 2
    first = core_ref[0] == 0
    mine, other = mine_ref[...].astype(F32), other_ref[...].astype(F32)
    for c, part in enumerate((jnp.where(first, mine, other), jnp.where(first, other, mine))):
        at = half * c
        qkv_ref[:, at : at + half] = part[rows:, :half]
        qkv_ref[:, width + at : width + at + half] = part[:rows, :half]
        qkv_ref[:, 2 * width + at : 2 * width + at + half] = part[:rows, half:]
        out_ref[:, at : at + half] = part[rows:, half:]


def fill(kernel, core, total, shapes, name):
    whole = pl.BlockSpec(memory_space=pltpu.VMEM)
    return pl.pallas_call(
        kernel,
        in_specs=[pl.BlockSpec(memory_space=pltpu.SMEM), whole, whole],
        out_specs=[whole] * len(shapes),
        out_shape=[jax.ShapeDtypeStruct(shape, F32) for shape in shapes],
        compiler_params=pltpu.CompilerParams(vmem_limit_bytes=40 * 2**20),
        cost_estimate=pl.CostEstimate(flops=0, bytes_accessed=12 * total.size, transcendentals=0),
        name=name,
    )(core.astype(jnp.int32).reshape(1), total, swap(total, "core"))


def on_device(ends, cond, w_ada, b_ada, w_qkv, w_out, w_fc1, w_fc2):
    section = lax.axis_index("section")
    d = lax.axis_index("dp")
    zh, xh = lax.axis_index("zh"), lax.axis_index("xh")
    a = zh * 2 + xh
    core = lax.axis_index("core")
    width = w_out.shape[2]
    half = width // 2
    rows_d = w_out.shape[1]
    columns = lambda array, start: lax.dynamic_slice_in_dim(array, start, half, 1)

    cond_float = cond.astype(F32).reshape(4, width)
    cond_low = jax.nn.silu(cond_float).astype(BF)
    two = ordered(d % 2 == 0, cond_low, swap_even(cond_low, "dp"))
    piece_attn = jnp.concatenate(
        [columns(w_qkv[0], width * i + half * core) for i in range(3)]
        + [columns(w_out[0], half * core)],
        axis=1,
    )
    two, piece_attn = lax.optimization_barrier((two, piece_attn))
    all_cond = ordered(d < 2, two, swap_odd(two, "dp"))
    all_cond = pick(all_cond.reshape(16, 4, rows_d).transpose(1, 0, 2), d)

    blocks = ends[0].reshape(2, 2, *ends.shape[3:])
    mine = lax.dynamic_index_in_dim(blocks, xh, 1, keepdims=False)
    theirs = lax.dynamic_index_in_dim(blocks, 1 - xh, 1, keepdims=False)
    blocks = jnp.stack([mine, swap(theirs, "xh")], axis=1)
    mine = jnp.stack([pick(blocks, zh), swap(pick(blocks, 1 - zh), "zh")])
    mine = mine.reshape(-1, width)
    tokens_half = mine.shape[0]
    start = ordered(core == 0, mine, swap(mine, "core"))
    peer = swap(mine, "xl")
    start_peer = ordered(core == 0, peer, swap(peer, "core"))

    below, above = gather_near(piece_attn, "dp")

    latent_rows = pick(all_cond.reshape(4, 4, rows_d).transpose(1, 0, 2), a)
    part_mod = dot(latent_rows, w_ada[0])
    bias = lax.dynamic_update_slice(
        jnp.zeros((6 * width,), F32), b_ada[0].astype(F32), (d * b_ada.shape[1],)
    )
    part_mod = (part_mod + bias[None]).reshape(2, 2, 6 * width)
    given = pick(part_mod, 1 - d // 2)
    given, below, above = lax.optimization_barrier((given, below, above))
    part_mod = pick(part_mod, d // 2) + swap_odd(given, "dp")
    attn_blocks = gather_far(piece_attn, below, above, "dp")
    part_mod = part_mod.reshape(2, 1, 6 * width)
    modulation = pick(part_mod, d % 2) + swap_even(pick(part_mod, 1 - d % 2), "dp")
    modulation = [modulation[:, width * i : width * (i + 1)] for i in range(6)]

    piece_fc = jnp.concatenate(
        [rows_at(w_fc2[0], half * core, half)]
        + [
            jnp.concatenate(
                [columns(w_fc1[0], width * j + half * core) for j in (2 * i, 2 * i + 1)], axis=1
            )
            for i in range(2)
        ]
    )
    piece_fc, unused = lax.optimization_barrier((piece_fc, attn_blocks[2]))
    below, above = gather_near(piece_fc, "dp")

    full_attn = jnp.zeros((width, 4 * half), BF)
    for s, parts in enumerate(attn_blocks):
        at = (d + s) % 4 * rows_d
        for part in parts:
            full_attn = lax.dynamic_update_slice(full_attn, part, (at, 0))
            at = at + part.shape[0]
    out_rows = full_attn[:, 3 * half :].reshape(2, half, half)
    full_out = ordered(
        core == 0, pick(out_rows, core), swap(pick(out_rows, 1 - core), "core"), axis=1
    )
    fc_near = [below, above]

    def with_fc(value):
        value, *fc_near[:] = lax.optimization_barrier((value, *fc_near))
        return value

    def across(value, pairs, with_peer):
        part = rows_at(value.astype(BF), core * tokens_half, tokens_half)
        part = lax.ppermute(part, "section", pairs)
        own = ordered(core == 0, part, swap(part, "core"))
        if not with_peer:
            return own, None
        peer = swap(part, "xl")
        return own, ordered(core == 0, peer, swap(peer, "core"))

    attn_weights = (full_attn[:, :half], full_attn[:, half : 3 * half], full_out)
    attn_state = attend(start.astype(F32), start_peer.astype(F32), modulation, attn_weights, with_fc)
    full_fc1 = jnp.zeros((width, 4 * half), BF)
    full_fc2 = jnp.zeros((4 * half, width), BF)
    for s, parts in enumerate(gather_far(piece_fc, *fc_near, "dp")):
        place = (d + s) % 4
        fc2_part = parts[0][:half]
        fc1_part = parts[0][half:] if len(parts) == 1 else parts[1]
        full_fc2 = lax.dynamic_update_slice(full_fc2, fc2_part, (place * half, 0))
        full_fc1 = lax.dynamic_update_slice(full_fc1, fc1_part[:rows_d], (place * rows_d, 0))
        full_fc1 = lax.dynamic_update_slice(full_fc1, fc1_part[rows_d:], (place * rows_d, width))
    fc_weights = (full_fc1, full_fc2)
    weights = attn_weights + fc_weights
    result, unused = feed_forward(attn_state, modulation, fc_weights)
    arrived, arrived_peer = across(result, [(0, 1)], True)
    second_input = jnp.where(section == 0, start, arrived).astype(F32)
    second_peer = jnp.where(section == 0, start_peer, arrived_peer).astype(F32)
    attn_state = attend(second_input, second_peer, modulation, attn_weights)
    result, state = feed_forward(attn_state, modulation, fc_weights)

    grad_input, *unused = layer_backward(start.astype(F32), state, modulation, weights, core)
    arrived, unused = across(grad_input, [(1, 0)], False)
    seed = jnp.where(section == 0, arrived, start).astype(F32)
    grad_input, grad_modulation, grads = layer_backward(seed, state, modulation, weights, core)
    grad_q, grad_k, grad_v, grad_out, grad_fc1, grad_fc2 = grads

    def block_fc(i):
        one = rows_at(grad_fc1, i * rows_d, rows_d)
        return jnp.concatenate([rows_at(grad_fc2, i * half, half), one[:, :width], one[:, width:]])

    sum_fc = sum_over_plane(scatter_ring(block_fc, "dp", d, grad_q))
    out_fc1, out_fc2 = fill(
        fill_fc_kernel, core, sum_fc, ((rows_d, 8 * half), (2 * half, width)), "fill_fc"
    )
    out_own = ordered(
        core == 0,
        columns(grad_out, half * core),
        swap(columns(grad_out, half - half * core), "core"),
    )

    def block_attn(i):
        k, v, q, out = (rows_at(g, i * rows_d, rows_d) for g in (grad_k, grad_v, grad_q, out_own))
        return jnp.concatenate(
            [jnp.concatenate([k, v], axis=1), jnp.concatenate([q, out], axis=1)]
        )

    sum_attn = sum_over_plane(scatter_ring(block_attn, "dp", d))
    out_qkv, out_out = fill(
        fill_attn_kernel, core, sum_attn, ((rows_d, 6 * half), (rows_d, width)), "fill_attn"
    )

    grad_mod = grad_modulation.reshape(1, 6 * width)
    grad_mod = grad_mod + swap(grad_mod, "xl")
    plane_mod = ordered(xh == 0, grad_mod, swap(grad_mod, "xh"))
    plane_mod = ordered(zh == 0, plane_mod, swap(plane_mod, "zh"))
    all_mod = gather_small(plane_mod, "dp", d)
    out_ada = lax.dot_general(
        all_cond.astype(F32), all_mod, (((0,), (0,)), ((), ())), precision=lax.Precision.HIGHEST
    )
    out_bias = jnp.sum(
        lax.dynamic_slice_in_dim(all_mod, d * b_ada.shape[1], b_ada.shape[1], 1), axis=0
    )
    grad_silu = lax.dot_general(
        all_mod,
        w_ada[0].astype(F32),
        (((1,), (1,)), ((), ())),
        precision=lax.Precision.HIGHEST,
    ).reshape(2, 2, 4, rows_d)
    same = jnp.stack([pick(grad_silu, d // 2), swap_odd(pick(grad_silu, 1 - d // 2), "dp")], axis=1)
    got = swap_even(pick(same, 1 - d % 2), "dp")
    same = pick(same, d % 2)
    silu_full = jnp.zeros((4, 4, rows_d), F32)
    beside = d + 1 - 2 * (d % 2)
    for part, place in ((same[0], d), (same[1], 3 - d), (got[0], beside), (got[1], 3 - beside)):
        silu_full = lax.dynamic_update_index_in_dim(silu_full, part, place, 0)
    silu_full = silu_full.transpose(1, 0, 2).reshape(4, width)
    silu_full = silu_full + swap(silu_full, "section")
    unused, silu_pull = jax.vjp(jax.nn.silu, cond_float)
    out_cond = silu_pull(silu_full)[0].reshape(cond.shape)

    edge = jnp.where(section == 0, grad_input, result)
    edge = rows_at(edge, core * tokens_half, tokens_half).reshape(2, 2, -1, width)
    edge = ordered(zh == 0, edge[:1], swap(edge[1:].astype(BF), "zh").astype(F32))
    boundary = ordered(
        xh == 0, edge[:, :1], swap(edge[:, 1:].astype(BF), "xh").astype(F32), axis=1
    ).reshape(ends.shape)

    return (
        boundary,
        out_cond,
        out_ada[None],
        out_bias[None],
        out_qkv[None],
        out_out[None],
        out_fc1[None],
        out_fc2[None],
    )


def solution(mesh):
    finer = Mesh(
        mesh.devices.reshape(2, 4, 2, 2, 2, 2), ("section", "dp", "zh", "xh", "xl", "core")
    )
    ends_spec = P("section", None, "dp", CTX, None)
    cond_spec = P(None, "dp", None)
    matrix = P("section", "dp", None)
    vector = P("section", "dp")
    return jax.shard_map(
        on_device,
        mesh=finer,
        in_specs=(ends_spec, cond_spec, matrix, vector, matrix, matrix, matrix, matrix),
        out_specs=(ends_spec, cond_spec, matrix, vector, matrix, matrix, matrix, matrix),
        check_vma=False,
    )
```

```python
import jax
import jax.numpy as jnp
from jax import lax
from jax.experimental import pallas as pl
from jax.experimental.pallas import tpu as pltpu
from jax.sharding import Mesh
from jax.sharding import PartitionSpec as P

HEAD = 64
BF = jnp.bfloat16
F32 = jnp.float32
RING_X = ("xh", "xl")
CTX = ("zh", "xh", "xl", "core")


def shift(array, axis, by, size=4):
    return lax.ppermute(array, axis, [(i, (i + by) % size) for i in range(size)])


def swap(array, axis):
    return lax.ppermute(array, axis, [(0, 1), (1, 0)])


def pick(blocks, index):
    return lax.dynamic_index_in_dim(blocks, index, 0, keepdims=False)


def rows_at(array, start, size):
    return lax.dynamic_slice_in_dim(array, start, size, 0)


def ordered(first, mine, other, axis=0):
    return jnp.where(
        first,
        jnp.concatenate([mine, other], axis=axis),
        jnp.concatenate([other, mine], axis=axis),
    )


def gather_near(piece, axis):
    return shift(piece, axis, 1), shift(piece, axis, -1)


def gather_far(piece, below, above, axis):
    half = piece.shape[0] // 2
    far_low = shift(below[:half], axis, 1)
    far_high = shift(above[half:], axis, -1)
    return [(piece,), (above,), (far_low, far_high), (below,)]


def scatter_ring(block, axis, index):
    add = lambda one, two: (one.astype(F32) + two.astype(F32)).astype(BF)
    far = block((index + 2) % 4)
    half = far.shape[0] // 2
    from_below = shift(far[:half], axis, 1)
    from_above = shift(far[half:], axis, -1)
    up = block((index + 1) % 4)
    up = jnp.concatenate([add(up[:half], from_below), up[half:]])
    down = block((index + 3) % 4)
    down = jnp.concatenate([down[:half], add(down[half:], from_above)])
    got_up = shift(up, axis, 1)
    got_down = shift(down, axis, -1)
    return block(index).astype(F32) + got_up.astype(F32) + got_down.astype(F32)


def dot(left, right):
    return jnp.dot(left, right, preferred_element_type=F32)


def dot_nt(left, right):
    return lax.dot_general(left, right, (((1,), (1,)), ((), ())), preferred_element_type=F32)


def dot_tn(left, right):
    return lax.dot_general(left, right, (((0,), (0,)), ((), ())), preferred_element_type=F32)


def attention_kernel(q_ref, ko_ref, kp_ref, vo_ref, vp_ref, out_ref, lse_ref):
    rows = q_ref.shape[0]
    step = 256
    for h in range(2):
        cols = slice(HEAD * h, HEAD * (h + 1))
        keys_own, keys_peer = ko_ref[:, cols], kp_ref[:, cols]
        values_own, values_peer = vo_ref[:, cols], vp_ref[:, cols]
        for start in range(0, rows, step):
            queries = q_ref[start : start + step, cols] * HEAD ** (-0.5)
            scores_own = dot_nt(keys_own, queries)
            scores_peer = dot_nt(keys_peer, queries)
            top = jnp.maximum(
                jnp.max(scores_own, axis=0, keepdims=True),
                jnp.max(scores_peer, axis=0, keepdims=True),
            )
            probs_own = jnp.exp(scores_own - top)
            probs_peer = jnp.exp(scores_peer - top)
            total = jnp.sum(probs_own, axis=0, keepdims=True) + jnp.sum(
                probs_peer, axis=0, keepdims=True
            )
            mixed = dot_tn(values_own, probs_own.astype(BF)) + dot_tn(
                values_peer, probs_peer.astype(BF)
            )
            mixed = mixed / total
            out_ref[start : start + step, cols] = mixed.T.astype(BF)
            lse_ref[0, h : h + 1, start : start + step] = top + jnp.log(total)


def attention(queries, kv_own, kv_peer):
    rows, width = queries.shape
    pairs = width // 128
    block = lambda offset: pl.BlockSpec((rows, 128), lambda h: (0, h + offset))
    return pl.pallas_call(
        attention_kernel,
        grid=(pairs,),
        in_specs=[block(0), block(0), block(0), block(pairs), block(pairs)],
        out_specs=[block(0), pl.BlockSpec((1, 2, rows), lambda h: (h, 0, 0))],
        out_shape=[
            jax.ShapeDtypeStruct((rows, width), BF),
            jax.ShapeDtypeStruct((pairs, 2, rows), F32),
        ],
        compiler_params=pltpu.CompilerParams(vmem_limit_bytes=40 * 2**20),
        cost_estimate=pl.CostEstimate(
            flops=100 * rows * rows * width,
            bytes_accessed=12 * rows * width,
            transcendentals=2 * rows * rows * width // HEAD,
        ),
        name="attention",
    )(queries, kv_own, kv_peer, kv_own, kv_peer)


def attention_back_kernel(
    q_ref, ko_ref, kp_ref, vo_ref, vp_ref, out_ref, gout_ref, lse_ref, gq_ref, gk_ref, gv_ref
):
    rows = q_ref.shape[0]
    step = 256
    scale = HEAD ** (-0.5)
    for h in range(2):
        cols = slice(HEAD * h, HEAD * (h + 1))
        sides = ((ko_ref, vo_ref), (kp_ref, vp_ref))
        grad_kv = [[None, None], [None, None]]
        for start in range(0, rows, step):
            span = slice(start, start + step)
            queries = q_ref[span, cols] * scale
            grad_out = gout_ref[span, cols]
            lse = lse_ref[0, h : h + 1, span]
            both = grad_out.astype(F32) * out_ref[span, cols].astype(F32)
            row_total = jnp.sum(both.T, axis=0, keepdims=True)
            grad_queries = None
            for side, (k_ref, v_ref) in enumerate(sides):
                keys, values = k_ref[:, cols], v_ref[:, cols]
                probs = jnp.exp(dot_nt(keys, queries) - lse)
                grad_probs = dot_nt(values, grad_out)
                grad_scores = (probs * (grad_probs - row_total)).astype(BF)
                part = dot_tn(keys, grad_scores)
                grad_queries = part if grad_queries is None else grad_queries + part
                terms = (dot(grad_scores, queries), dot(probs.astype(BF), grad_out))
                for i in range(2):
                    old = grad_kv[side][i]
                    grad_kv[side][i] = terms[i] if old is None else old + terms[i]
            gq_ref[span, cols] = (grad_queries * scale).T.astype(BF)
        for side in range(2):
            span = slice(rows * side, rows * (side + 1))
            gk_ref[span, cols] = grad_kv[side][0].astype(BF)
            gv_ref[span, cols] = grad_kv[side][1].astype(BF)


def attention_back(queries, kv_own, kv_peer, mixed, grad_mixed, lse):
    rows, width = queries.shape
    pairs = width // 128
    block = lambda offset: pl.BlockSpec((rows, 128), lambda h: (0, h + offset))
    double = pl.BlockSpec((2 * rows, 128), lambda h: (0, h))
    return pl.pallas_call(
        attention_back_kernel,
        grid=(pairs,),
        in_specs=[
            block(0),
            block(0),
            block(0),
            block(pairs),
            block(pairs),
            block(0),
            block(0),
            pl.BlockSpec((1, 2, rows), lambda h: (h, 0, 0)),
        ],
        out_specs=[block(0), double, double],
        out_shape=[
            jax.ShapeDtypeStruct((rows, width), BF),
            jax.ShapeDtypeStruct((2 * rows, width), BF),
            jax.ShapeDtypeStruct((2 * rows, width), BF),
        ],
        compiler_params=pltpu.CompilerParams(vmem_limit_bytes=40 * 2**20),
        cost_estimate=pl.CostEstimate(
            flops=130 * rows * rows * width,
            bytes_accessed=24 * rows * width,
            transcendentals=2 * rows * rows * width // HEAD,
        ),
        name="attention_back",
    )(queries, kv_own, kv_peer, kv_own, kv_peer, mixed, grad_mixed, lse)


def norm_stats(activations):
    center = activations - jnp.mean(activations, axis=-1, keepdims=True)
    inverse = lax.rsqrt(jnp.mean(center * center, axis=-1, keepdims=True) + 1e-06)
    return (center * inverse, inverse)


def norm_back(grad_norm, normal, inverse):
    return inverse * (
        grad_norm
        - jnp.mean(grad_norm, axis=-1, keepdims=True)
        - normal * jnp.mean(grad_norm * normal, axis=-1, keepdims=True)
    )


def core_sum(partial_sum):
    low = partial_sum.astype(BF)
    return low.astype(F32) + swap(low, "core").astype(F32)


def gelu_and_slope(pre_act):
    linear = 2.0 * (2.0 / jnp.pi) ** 0.5
    cubic = 0.044715 * linear
    square = pre_act * pre_act
    gate = 1.0 / (1.0 + jnp.exp(-pre_act * (linear + cubic * square)))
    value = pre_act * gate
    slope = gate + value * (1.0 - gate) * (linear + 3.0 * cubic * square)
    return value.astype(BF), slope.astype(BF)


def attend(activations, activations_peer, modulation, weights, before=(), after=()):
    w_q, w_kv, w_out = weights
    shift_first, scale_first, gate_first = modulation[:3]
    normal_first, inverse_first = norm_stats(activations)
    entry = (normal_first * (1.0 + scale_first) + shift_first).astype(BF)
    kv_own = dot(entry, w_kv).astype(BF)
    queries = dot(entry, w_q).astype(BF)
    activations_peer, kv_own, queries = lax.optimization_barrier(
        (activations_peer, kv_own, queries)
    )
    entry_peer = norm_stats(activations_peer.astype(F32))[0] * (1.0 + scale_first) + shift_first
    entry_peer = entry_peer.astype(BF)
    kv_peer = dot(entry_peer, w_kv).astype(BF)
    queries, *before = lax.optimization_barrier((queries, *before))
    mixed, lse = attention(queries, kv_own, kv_peer)
    mixed, *after = lax.optimization_barrier((mixed, *after))
    branch = core_sum(dot(mixed, w_out))
    second = activations + gate_first * branch
    return (
        second,
        normal_first,
        inverse_first,
        entry,
        entry_peer,
        queries,
        kv_own,
        kv_peer,
        lse,
        mixed,
        branch,
    ), (*before, *after)


def feed_forward(attn_state, modulation, weights):
    w_fc1, w_fc2 = weights
    shift_second, scale_second, gate_second = modulation[3:]
    second, *kept = attn_state
    normal_second, inverse_second = norm_stats(second)
    mlp_input = (normal_second * (1.0 + scale_second) + shift_second).astype(BF)
    hidden, slope = gelu_and_slope(dot(mlp_input, w_fc1))
    branch_mlp = core_sum(dot(hidden, w_fc2))
    result = second + gate_second * branch_mlp
    state = (*kept, normal_second, inverse_second, mlp_input, slope, hidden, branch_mlp)
    return (result, state)


def layer_backward(grad_result, state, modulation, weights, core, reduced=False):
    w_q, w_kv, w_out, w_fc1, w_fc2 = weights
    shift_first, scale_first, gate_first, shift_second, scale_second, gate_second = modulation
    (
        normal_first,
        inverse_first,
        entry,
        entry_peer,
        queries,
        kv_own,
        kv_peer,
        lse,
        mixed,
        branch,
        normal_second,
        inverse_second,
        mlp_input,
        slope,
        hidden,
        branch_mlp,
    ) = state
    rows = lambda value: jnp.sum(value, axis=0)
    grad_gate_second = rows(grad_result * branch_mlp)
    grad_branch_mlp = (grad_result * gate_second).astype(BF)
    grad_hidden = dot_nt(grad_branch_mlp, w_fc2)
    grad_pre = (grad_hidden * slope.astype(F32)).astype(BF)
    grad_mlp_input = core_sum(dot_nt(grad_pre, w_fc1))
    grad_fc2 = dot_tn(hidden, grad_branch_mlp).astype(BF)
    grad_fc1 = dot_tn(mlp_input, grad_pre).astype(BF)
    if reduced:
        grad_fc2 = lax.psum_scatter(grad_fc2, "dp", scatter_dimension=0, tiled=True)
        grad_fc1 = lax.psum_scatter(grad_fc1, "dp", scatter_dimension=0, tiled=True)
    grad_scale_second = rows(grad_mlp_input * normal_second)
    grad_shift_second = rows(grad_mlp_input)
    grad_second = grad_result + norm_back(
        grad_mlp_input * (1.0 + scale_second), normal_second, inverse_second
    )
    grad_gate_first = rows(grad_second * branch)
    grad_branch = (grad_second * gate_first).astype(BF)
    grad_mixed = dot_nt(grad_branch, w_out).astype(BF)
    grad_out = dot_tn(mixed, grad_branch).astype(BF)
    grad_queries, grad_keys, grad_values = attention_back(
        queries, kv_own, kv_peer, mixed, grad_mixed, lse
    )
    tokens, half = mixed.shape
    w_k, w_v = w_kv[:, :half], w_kv[:, half:]
    far = (
        dot_nt(grad_keys[tokens:], w_k) + dot_nt(grad_values[tokens:], w_v)
    ).astype(BF)
    kept = rows_at(far, core * (tokens // 2), tokens // 2)
    given = rows_at(far, (1 - core) * (tokens // 2), tokens // 2)
    far = (kept.astype(F32) + swap(given, "core").astype(F32)).astype(BF)
    far = swap(far, "xl")
    if reduced:
        far, grad_fc2 = lax.optimization_barrier((far, grad_fc2))
    far = ordered(core == 0, far, swap(far, "core"))
    near = (
        dot_nt(grad_queries, w_q)
        + dot_nt(grad_keys[:tokens], w_k)
        + dot_nt(grad_values[:tokens], w_v)
    )
    grad_entry = core_sum(near) + far.astype(F32)
    entry_all = jnp.concatenate([entry, entry_peer])
    grad_q_proj = dot_tn(entry, grad_queries).astype(BF)
    grad_k_proj = dot_tn(entry_all, grad_keys).astype(BF)
    grad_v_proj = dot_tn(entry_all, grad_values).astype(BF)
    grad_scale_first = rows(grad_entry * normal_first)
    grad_shift_first = rows(grad_entry)
    grad_input = grad_second + norm_back(
        grad_entry * (1.0 + scale_first), normal_first, inverse_first
    )
    grad_modulation = jnp.stack(
        [
            grad_shift_first,
            grad_scale_first,
            grad_gate_first,
            grad_shift_second,
            grad_scale_second,
            grad_gate_second,
        ]
    )
    grads = (grad_q_proj, grad_k_proj, grad_v_proj, grad_out, grad_fc1, grad_fc2)
    return (grad_input, grad_modulation, grads)


def sum_over_plane(block):
    x = lax.axis_index(RING_X)
    rows, columns = block.shape
    parts = block.astype(BF).reshape(4, rows // 4, columns)
    part = scatter_ring(lambda i: pick(parts, i), RING_X, x).astype(BF)
    part = (part.astype(F32) + swap(part, "zh").astype(F32)).astype(BF)
    below, above = gather_near(part, RING_X)
    total = jnp.zeros((rows, columns), BF)
    for s, pieces in enumerate(gather_far(part, below, above, RING_X)):
        at = (x + s) % 4 * (rows // 4)
        for piece in pieces:
            total = lax.dynamic_update_slice(total, piece, (at, 0))
            at = at + piece.shape[0]
    return total


def fill_fc_kernel(core_ref, mine_ref, other_ref, fc1_ref, fc2_ref):
    half = mine_ref.shape[1] // 2
    rows = fc1_ref.shape[0]
    first = core_ref[0] == 0
    mine, other = mine_ref[...].astype(F32), other_ref[...].astype(F32)
    for c, part in enumerate((jnp.where(first, mine, other), jnp.where(first, other, mine))):
        fc2_ref[half * c : half * (c + 1), :] = part[:half]
        for j in range(4):
            top = half + rows * (j // 2)
            left = half * (j % 2)
            to = half * (2 * j + c)
            fc1_ref[:, to : to + half] = part[top : top + rows, left : left + half]


def fill_attn_kernel(core_ref, mine_ref, other_ref, qkv_ref, out_ref):
    rows, width = out_ref.shape
    half = width // 2
    first = core_ref[0] == 0
    mine, other = mine_ref[...].astype(F32), other_ref[...].astype(F32)
    for c, part in enumerate((jnp.where(first, mine, other), jnp.where(first, other, mine))):
        at = half * c
        qkv_ref[:, at : at + half] = part[rows:, :half]
        qkv_ref[:, width + at : width + at + half] = part[:rows, :half]
        qkv_ref[:, 2 * width + at : 2 * width + at + half] = part[:rows, half:]
        out_ref[:, at : at + half] = part[rows:, half:]


def fill(kernel, core, total, shapes, name):
    whole = pl.BlockSpec(memory_space=pltpu.VMEM)
    return pl.pallas_call(
        kernel,
        in_specs=[pl.BlockSpec(memory_space=pltpu.SMEM), whole, whole],
        out_specs=[whole] * len(shapes),
        out_shape=[jax.ShapeDtypeStruct(shape, F32) for shape in shapes],
        compiler_params=pltpu.CompilerParams(vmem_limit_bytes=40 * 2**20),
        cost_estimate=pl.CostEstimate(flops=0, bytes_accessed=12 * total.size, transcendentals=0),
        name=name,
    )(core.astype(jnp.int32).reshape(1), total, swap(total, "core"))


def on_device(ends, cond, w_ada, b_ada, w_qkv, w_out, w_fc1, w_fc2):
    section = lax.axis_index("section")
    d = lax.axis_index("dp")
    zh, xh = lax.axis_index("zh"), lax.axis_index("xh")
    a = zh * 2 + xh
    core = lax.axis_index("core")
    width = w_out.shape[2]
    half = width // 2
    rows_d = w_out.shape[1]
    columns = lambda array, start: lax.dynamic_slice_in_dim(array, start, half, 1)

    cond_float = cond.astype(F32).reshape(4, width)
    cond_low = jax.nn.silu(cond_float).astype(BF)
    cond_rows = cond_low.reshape(4, 4, rows_d).transpose(1, 0, 2)
    cond_parts = [pick(cond_rows, d)] + [
        shift(pick(cond_rows, (d + s) % 4), "dp", s) for s in (1, 2, 3)
    ]
    piece_attn = jnp.concatenate(
        [columns(w_qkv[0], width * i + half * core) for i in range(3)]
        + [columns(w_out[0], half * core)],
        axis=1,
    )
    piece_attn, *cond_parts = lax.optimization_barrier((piece_attn, *cond_parts))

    blocks = ends[0].reshape(2, 2, *ends.shape[3:])
    mine = lax.dynamic_index_in_dim(blocks, xh, 1, keepdims=False)
    theirs = lax.dynamic_index_in_dim(blocks, 1 - xh, 1, keepdims=False)
    blocks = jnp.stack([mine, swap(theirs, "xh")], axis=1)
    mine = jnp.stack([pick(blocks, zh), swap(pick(blocks, 1 - zh), "zh")])
    mine = mine.reshape(-1, width)
    tokens_half = mine.shape[0]
    start = ordered(core == 0, mine, swap(mine, "core"))
    peer = swap(mine, "xl")
    start_peer = ordered(core == 0, peer, swap(peer, "core"))

    below, above = gather_near(piece_attn, "dp")

    latent_rows = jnp.stack([pick(part, a) for part in cond_parts])
    bias = lax.dynamic_update_slice(
        jnp.zeros((6 * width,), F32), b_ada[0].astype(F32), (d * b_ada.shape[1],)
    )
    part_mod = dot(latent_rows, w_ada[0]) + bias[None]
    part_mod, below, above = lax.optimization_barrier((part_mod, below, above))
    modulation = part_mod[0:1]
    for s in (1, 2, 3):
        modulation = modulation + shift(part_mod[s : s + 1], "dp", -s)
    modulation = [modulation[:, width * i : width * (i + 1)] for i in range(6)]
    attn_blocks = gather_far(piece_attn, below, above, "dp")

    piece_fc1 = jnp.concatenate(
        [columns(w_fc1[0], width * j + half * core) for j in range(4)], axis=1
    )
    full_fc1 = lax.all_gather(piece_fc1, "dp", axis=0, tiled=True)
    piece_fc2 = rows_at(w_fc2[0], half * core, half)
    piece_fc2, unused = lax.optimization_barrier((piece_fc2, attn_blocks[2]))
    below, above = gather_near(piece_fc2, "dp")

    full_attn = jnp.zeros((width, 4 * half), BF)
    for s, parts in enumerate(attn_blocks):
        at = (d + s) % 4 * rows_d
        for part in parts:
            full_attn = lax.dynamic_update_slice(full_attn, part, (at, 0))
            at = at + part.shape[0]
    out_rows = full_attn[:, 3 * half :].reshape(2, half, half)
    full_out = ordered(
        core == 0, pick(out_rows, core), swap(pick(out_rows, 1 - core), "core"), axis=1
    )
    def across(value, pairs, with_peer):
        part = rows_at(value.astype(BF), core * tokens_half, tokens_half)
        part = lax.ppermute(part, "section", pairs)
        own = ordered(core == 0, part, swap(part, "core"))
        if not with_peer:
            return own, None
        peer = swap(part, "xl")
        return own, ordered(core == 0, peer, swap(peer, "core"))

    attn_weights = (full_attn[:, :half], full_attn[:, half : 3 * half], full_out)
    attn_state, (full_fc1, below, above) = attend(
        start.astype(F32), start_peer, modulation, attn_weights, (full_fc1,), (below, above)
    )
    full_fc2 = jnp.zeros((4 * half, width), BF)
    for s, parts in enumerate(gather_far(piece_fc2, below, above, "dp")):
        at = (d + s) % 4 * half
        for part in parts:
            full_fc2 = lax.dynamic_update_slice(full_fc2, part, (at, 0))
            at = at + part.shape[0]
    fc_weights = (full_fc1, full_fc2)
    weights = attn_weights + fc_weights
    result, unused = feed_forward(attn_state, modulation, fc_weights)
    arrived, arrived_peer = across(result, [(0, 1)], True)
    second_input = jnp.where(section == 0, start, arrived).astype(F32)
    second_peer = jnp.where(section == 0, start_peer, arrived_peer)
    attn_state, unused = attend(second_input, second_peer, modulation, attn_weights)
    result, state = feed_forward(attn_state, modulation, fc_weights)

    grad_input, *unused = layer_backward(start.astype(F32), state, modulation, weights, core)
    arrived, unused = across(grad_input, [(1, 0)], False)
    seed = jnp.where(section == 0, arrived, start).astype(F32)
    grad_input, grad_modulation, grads = layer_backward(seed, state, modulation, weights, core, True)
    grad_q, grad_k, grad_v, grad_out, grad_fc1, grad_fc2 = grads

    sum_fc = sum_over_plane(
        jnp.concatenate([grad_fc2, grad_fc1[:, :width], grad_fc1[:, width:]])
    )
    out_fc1, out_fc2 = fill(
        fill_fc_kernel, core, sum_fc, ((rows_d, 8 * half), (2 * half, width)), "fill_fc"
    )
    out_own = ordered(
        core == 0,
        columns(grad_out, half * core),
        swap(columns(grad_out, half - half * core), "core"),
    )

    def block_attn(i):
        k, v, q, out = (rows_at(g, i * rows_d, rows_d) for g in (grad_k, grad_v, grad_q, out_own))
        return jnp.concatenate(
            [jnp.concatenate([k, v], axis=1), jnp.concatenate([q, out], axis=1)]
        )

    sum_attn = sum_over_plane(scatter_ring(block_attn, "dp", d))
    out_qkv, out_out = fill(
        fill_attn_kernel, core, sum_attn, ((rows_d, 6 * half), (rows_d, width)), "fill_attn"
    )

    grad_mod = grad_modulation.reshape(1, 6 * width)
    grad_mod = grad_mod + swap(grad_mod, "xl")
    beside = swap(grad_mod, "xh")
    behind = swap(grad_mod, "zh")
    across_both = lax.ppermute(grad_mod, ("zh", "xh"), [(i, 3 - i) for i in range(4)])
    plane_mod = ordered(
        zh == 0, ordered(xh == 0, grad_mod, beside), ordered(xh == 0, behind, across_both)
    )
    all_mod = jnp.concatenate([plane_mod] + [shift(plane_mod, "dp", s) for s in (1, 2, 3)])
    all_cond = jnp.concatenate(cond_parts)
    out_ada = lax.dot_general(
        all_cond.astype(F32), all_mod, (((0,), (0,)), ((), ())), precision=lax.Precision.HIGHEST
    )
    out_bias = jnp.sum(
        lax.dynamic_slice_in_dim(all_mod, d * b_ada.shape[1], b_ada.shape[1], 1), axis=0
    )
    grad_silu = lax.dot_general(
        all_mod,
        w_ada[0].astype(F32),
        (((1,), (1,)), ((), ())),
        precision=lax.Precision.HIGHEST,
    ).reshape(4, 4, rows_d)
    silu_full = jnp.zeros((4, 4, rows_d), F32)
    for s in range(4):
        part = shift(grad_silu[s], "dp", -s) if s else grad_silu[s]
        silu_full = lax.dynamic_update_index_in_dim(silu_full, part, (d + s) % 4, 0)
    silu_full = silu_full.transpose(1, 0, 2).reshape(4, width)
    silu_full = silu_full + swap(silu_full, "section")
    unused, silu_pull = jax.vjp(jax.nn.silu, cond_float)
    out_cond = silu_pull(silu_full)[0].reshape(cond.shape)

    edge = jnp.where(section == 0, grad_input, result)
    edge = rows_at(edge, core * tokens_half, tokens_half).reshape(2, 2, -1, width)
    edge = ordered(zh == 0, edge[:1], swap(edge[1:].astype(BF), "zh").astype(F32))
    boundary = ordered(
        xh == 0, edge[:, :1], swap(edge[:, 1:].astype(BF), "xh").astype(F32), axis=1
    ).reshape(ends.shape)

    return (
        boundary,
        out_cond,
        out_ada[None],
        out_bias[None],
        out_qkv[None],
        out_out[None],
        out_fc1[None],
        out_fc2[None],
    )


def solution(mesh):
    finer = Mesh(
        mesh.devices.reshape(2, 4, 2, 2, 2, 2), ("section", "dp", "zh", "xh", "xl", "core")
    )
    ends_spec = P("section", None, "dp", CTX, None)
    cond_spec = P(None, "dp", None)
    matrix = P("section", "dp", None)
    vector = P("section", "dp")
    return jax.shard_map(
        on_device,
        mesh=finer,
        in_specs=(ends_spec, cond_spec, matrix, vector, matrix, matrix, matrix, matrix),
        out_specs=(ends_spec, cond_spec, matrix, vector, matrix, matrix, matrix, matrix),
        check_vma=False,
    )
```

```python
import jax
import jax.numpy as jnp
from jax import lax
from jax.experimental import pallas as pl
from jax.experimental.pallas import tpu as pltpu
from jax.sharding import Mesh
from jax.sharding import PartitionSpec as P

HEAD = 64
BF = jnp.bfloat16
F32 = jnp.float32
RING_X = ("xh", "xl")
CTX = ("zh", "xh", "xl", "core")


def shift(array, axis, by, size=4):
    return lax.ppermute(array, axis, [(i, (i + by) % size) for i in range(size)])


def swap(array, axis):
    return lax.ppermute(array, axis, [(0, 1), (1, 0)])


def pick(blocks, index):
    return lax.dynamic_index_in_dim(blocks, index, 0, keepdims=False)


def rows_at(array, start, size):
    return lax.dynamic_slice_in_dim(array, start, size, 0)


def ordered(first, mine, other, axis=0):
    return jnp.where(
        first,
        jnp.concatenate([mine, other], axis=axis),
        jnp.concatenate([other, mine], axis=axis),
    )


def gather_near(piece, axis):
    return shift(piece, axis, 1), shift(piece, axis, -1)


def gather_far(piece, below, above, axis):
    half = piece.shape[0] // 2
    far_low = shift(below[:half], axis, 1)
    far_high = shift(above[half:], axis, -1)
    return [(piece,), (above,), (far_low, far_high), (below,)]


def scatter_first(block, axis, index):
    far = block((index + 2) % 4)
    half = far.shape[0] // 2
    return shift(far[:half], axis, 1), shift(far[half:], axis, -1)


def scatter_second(block, axis, index, from_below, from_above):
    add = lambda one, two: (one.astype(F32) + two.astype(F32)).astype(BF)
    half = from_below.shape[0]
    up = block((index + 1) % 4)
    up = jnp.concatenate([add(up[:half], from_below), up[half:]])
    down = block((index + 3) % 4)
    down = jnp.concatenate([down[:half], add(down[half:], from_above)])
    return shift(up, axis, 1), shift(down, axis, -1)


def scatter_sum(block, index, got_up, got_down):
    return block(index).astype(F32) + got_up.astype(F32) + got_down.astype(F32)


def fill_rows(size, blocks, index):
    total = jnp.zeros((size, blocks[0][0].shape[1]), BF)
    for s, pieces in enumerate(blocks):
        at = (index + s) % 4 * (size // 4)
        for piece in pieces:
            total = lax.dynamic_update_slice(total, piece, (at, 0))
            at = at + piece.shape[0]
    return total


def join(*values):
    return lax.optimization_barrier(values)


def dot(left, right):
    return jnp.dot(left, right, preferred_element_type=F32)


def dot_nt(left, right):
    return lax.dot_general(left, right, (((1,), (1,)), ((), ())), preferred_element_type=F32)


def dot_tn(left, right):
    return lax.dot_general(left, right, (((0,), (0,)), ((), ())), preferred_element_type=F32)


def attention_kernel(q_ref, ko_ref, kp_ref, vo_ref, vp_ref, out_ref, lse_ref):
    rows = q_ref.shape[0]
    step = 256
    for h in range(2):
        cols = slice(HEAD * h, HEAD * (h + 1))
        keys_own, keys_peer = ko_ref[:, cols], kp_ref[:, cols]
        values_own, values_peer = vo_ref[:, cols], vp_ref[:, cols]
        for start in range(0, rows, step):
            queries = q_ref[start : start + step, cols] * HEAD ** (-0.5)
            scores_own = dot_nt(keys_own, queries)
            scores_peer = dot_nt(keys_peer, queries)
            top = jnp.maximum(
                jnp.max(scores_own, axis=0, keepdims=True),
                jnp.max(scores_peer, axis=0, keepdims=True),
            )
            probs_own = jnp.exp(scores_own - top)
            probs_peer = jnp.exp(scores_peer - top)
            total = jnp.sum(probs_own, axis=0, keepdims=True) + jnp.sum(
                probs_peer, axis=0, keepdims=True
            )
            mixed = dot_tn(values_own, probs_own.astype(BF)) + dot_tn(
                values_peer, probs_peer.astype(BF)
            )
            mixed = mixed / total
            out_ref[start : start + step, cols] = mixed.T.astype(BF)
            lse_ref[0, h : h + 1, start : start + step] = top + jnp.log(total)


def attention(queries, kv_own, kv_peer):
    rows, width = queries.shape
    pairs = width // 128
    block = lambda offset: pl.BlockSpec((rows, 128), lambda h: (0, h + offset))
    return pl.pallas_call(
        attention_kernel,
        grid=(pairs,),
        in_specs=[block(0), block(0), block(0), block(pairs), block(pairs)],
        out_specs=[block(0), pl.BlockSpec((1, 2, rows), lambda h: (h, 0, 0))],
        out_shape=[
            jax.ShapeDtypeStruct((rows, width), BF),
            jax.ShapeDtypeStruct((pairs, 2, rows), F32),
        ],
        compiler_params=pltpu.CompilerParams(vmem_limit_bytes=40 * 2**20),
        cost_estimate=pl.CostEstimate(
            flops=100 * rows * rows * width,
            bytes_accessed=12 * rows * width,
            transcendentals=2 * rows * rows * width // HEAD,
        ),
        name="attention",
    )(queries, kv_own, kv_peer, kv_own, kv_peer)


def attention_back_kernel(
    q_ref, ko_ref, kp_ref, vo_ref, vp_ref, out_ref, gout_ref, lse_ref, gq_ref, gk_ref, gv_ref
):
    rows = q_ref.shape[0]
    step = 256
    scale = HEAD ** (-0.5)
    for h in range(2):
        cols = slice(HEAD * h, HEAD * (h + 1))
        sides = ((ko_ref, vo_ref), (kp_ref, vp_ref))
        grad_kv = [[None, None], [None, None]]
        for start in range(0, rows, step):
            span = slice(start, start + step)
            queries = q_ref[span, cols] * scale
            grad_out = gout_ref[span, cols]
            lse = lse_ref[0, h : h + 1, span]
            both = grad_out.astype(F32) * out_ref[span, cols].astype(F32)
            row_total = jnp.sum(both.T, axis=0, keepdims=True)
            grad_queries = None
            for side, (k_ref, v_ref) in enumerate(sides):
                keys, values = k_ref[:, cols], v_ref[:, cols]
                probs = jnp.exp(dot_nt(keys, queries) - lse)
                grad_probs = dot_nt(values, grad_out)
                grad_scores = (probs * (grad_probs - row_total)).astype(BF)
                part = dot_tn(keys, grad_scores)
                grad_queries = part if grad_queries is None else grad_queries + part
                terms = (dot(grad_scores, queries), dot(probs.astype(BF), grad_out))
                for i in range(2):
                    old = grad_kv[side][i]
                    grad_kv[side][i] = terms[i] if old is None else old + terms[i]
            gq_ref[span, cols] = (grad_queries * scale).T.astype(BF)
        for side in range(2):
            span = slice(rows * side, rows * (side + 1))
            gk_ref[span, cols] = grad_kv[side][0].astype(BF)
            gv_ref[span, cols] = grad_kv[side][1].astype(BF)


def attention_back(queries, kv_own, kv_peer, mixed, grad_mixed, lse):
    rows, width = queries.shape
    pairs = width // 128
    block = lambda offset: pl.BlockSpec((rows, 128), lambda h: (0, h + offset))
    double = pl.BlockSpec((2 * rows, 128), lambda h: (0, h))
    return pl.pallas_call(
        attention_back_kernel,
        grid=(pairs,),
        in_specs=[
            block(0),
            block(0),
            block(0),
            block(pairs),
            block(pairs),
            block(0),
            block(0),
            pl.BlockSpec((1, 2, rows), lambda h: (h, 0, 0)),
        ],
        out_specs=[block(0), double, double],
        out_shape=[
            jax.ShapeDtypeStruct((rows, width), BF),
            jax.ShapeDtypeStruct((2 * rows, width), BF),
            jax.ShapeDtypeStruct((2 * rows, width), BF),
        ],
        compiler_params=pltpu.CompilerParams(vmem_limit_bytes=40 * 2**20),
        cost_estimate=pl.CostEstimate(
            flops=130 * rows * rows * width,
            bytes_accessed=24 * rows * width,
            transcendentals=2 * rows * rows * width // HEAD,
        ),
        name="attention_back",
    )(queries, kv_own, kv_peer, kv_own, kv_peer, mixed, grad_mixed, lse)


def norm_stats(activations):
    center = activations - jnp.mean(activations, axis=-1, keepdims=True)
    inverse = lax.rsqrt(jnp.mean(center * center, axis=-1, keepdims=True) + 1e-06)
    return (center * inverse, inverse)


def norm_back(grad_norm, normal, inverse):
    return inverse * (
        grad_norm
        - jnp.mean(grad_norm, axis=-1, keepdims=True)
        - normal * jnp.mean(grad_norm * normal, axis=-1, keepdims=True)
    )


def core_sum(partial_sum):
    low = partial_sum.astype(BF)
    return low.astype(F32) + swap(low, "core").astype(F32)


def gelu_and_slope(pre_act):
    linear = 2.0 * (2.0 / jnp.pi) ** 0.5
    cubic = 0.044715 * linear
    square = pre_act * pre_act
    gate = 1.0 / (1.0 + jnp.exp(-pre_act * (linear + cubic * square)))
    value = pre_act * gate
    slope = gate + value * (1.0 - gate) * (linear + 3.0 * cubic * square)
    return value.astype(BF), slope.astype(BF)


def attend(activations, activations_peer, modulation, weights, before=None, after=None):
    w_q, w_kv, w_out = weights
    shift_first, scale_first, gate_first = modulation[:3]
    normal_first, inverse_first = norm_stats(activations)
    entry = (normal_first * (1.0 + scale_first) + shift_first).astype(BF)
    kv_own = dot(entry, w_kv).astype(BF)
    queries = dot(entry, w_q).astype(BF)
    activations_peer, kv_own, queries = lax.optimization_barrier(
        (activations_peer, kv_own, queries)
    )
    entry_peer = norm_stats(activations_peer.astype(F32))[0] * (1.0 + scale_first) + shift_first
    entry_peer = entry_peer.astype(BF)
    kv_peer = dot(entry_peer, w_kv).astype(BF)
    if before:
        queries = before(queries)
    mixed, lse = attention(queries, kv_own, kv_peer)
    if after:
        mixed = after(mixed)
    branch = core_sum(dot(mixed, w_out))
    second = activations + gate_first * branch
    return (
        second,
        normal_first,
        inverse_first,
        entry,
        entry_peer,
        queries,
        kv_own,
        kv_peer,
        lse,
        mixed,
        branch,
    )


def feed_forward(attn_state, modulation, weights):
    w_fc1, w_fc2 = weights
    shift_second, scale_second, gate_second = modulation[3:]
    second, *kept = attn_state
    normal_second, inverse_second = norm_stats(second)
    mlp_input = (normal_second * (1.0 + scale_second) + shift_second).astype(BF)
    hidden, slope = gelu_and_slope(dot(mlp_input, w_fc1))
    branch_mlp = core_sum(dot(hidden, w_fc2))
    result = second + gate_second * branch_mlp
    state = (*kept, normal_second, inverse_second, mlp_input, slope, hidden, branch_mlp)
    return (result, state)


def back_front(grad_result, state, modulation, weights, reduced=False):
    w_q, w_kv, w_out, w_fc1, w_fc2 = weights
    shift_first, scale_first, gate_first, shift_second, scale_second, gate_second = modulation
    (
        normal_first,
        inverse_first,
        entry,
        entry_peer,
        queries,
        kv_own,
        kv_peer,
        lse,
        mixed,
        branch,
        normal_second,
        inverse_second,
        mlp_input,
        slope,
        hidden,
        branch_mlp,
    ) = state
    rows = lambda value: jnp.sum(value, axis=0)
    grad_gate_second = rows(grad_result * branch_mlp)
    grad_branch_mlp = (grad_result * gate_second).astype(BF)
    grad_hidden = dot_nt(grad_branch_mlp, w_fc2)
    grad_pre = (grad_hidden * slope.astype(F32)).astype(BF)
    grad_mlp_input = core_sum(dot_nt(grad_pre, w_fc1))
    grad_fc2 = dot_tn(hidden, grad_branch_mlp).astype(BF)
    grad_fc1 = dot_tn(mlp_input, grad_pre).astype(BF)
    if reduced:
        grad_fc2 = lax.psum_scatter(grad_fc2, "dp", scatter_dimension=0, tiled=True)
        grad_fc1 = lax.psum_scatter(grad_fc1, "dp", scatter_dimension=0, tiled=True)
    grad_scale_second = rows(grad_mlp_input * normal_second)
    grad_shift_second = rows(grad_mlp_input)
    grad_second = grad_result + norm_back(
        grad_mlp_input * (1.0 + scale_second), normal_second, inverse_second
    )
    grad_gate_first = rows(grad_second * branch)
    grad_branch = (grad_second * gate_first).astype(BF)
    grad_mixed = dot_nt(grad_branch, w_out).astype(BF)
    grad_out = dot_tn(mixed, grad_branch).astype(BF)
    grad_queries, grad_keys, grad_values = attention_back(
        queries, kv_own, kv_peer, mixed, grad_mixed, lse
    )
    grad_modulation = (
        grad_gate_first,
        grad_shift_second,
        grad_scale_second,
        grad_gate_second,
    )
    grads = (grad_out, grad_fc1, grad_fc2)
    return grad_second, grad_modulation, grads, (grad_queries, grad_keys, grad_values)


def back_terms(grad_qkv, weights, core):
    w_q, w_kv = weights[:2]
    grad_queries, grad_keys, grad_values = grad_qkv
    tokens, half = grad_queries.shape
    w_k, w_v = w_kv[:, :half], w_kv[:, half:]
    far = (
        dot_nt(grad_keys[tokens:], w_k) + dot_nt(grad_values[tokens:], w_v)
    ).astype(BF)
    kept = rows_at(far, core * (tokens // 2), tokens // 2)
    given = rows_at(far, (1 - core) * (tokens // 2), tokens // 2)
    near = lambda: (
        dot_nt(grad_queries, w_q)
        + dot_nt(grad_keys[:tokens], w_k)
        + dot_nt(grad_values[:tokens], w_v)
    ).astype(BF)
    return kept, given, near


def add_low(one, two):
    return one.astype(F32) + two.astype(F32)


def back_end(grad_entry, grad_second, state, modulation):
    normal_first, inverse_first = state[:2]
    return grad_second + norm_back(
        grad_entry * (1.0 + modulation[1]), normal_first, inverse_first
    )


class PlaneSum:
    def __init__(self, block):
        self.x = lax.axis_index(RING_X)
        self.rows = block.shape[0]
        parts = block.astype(BF).reshape(4, self.rows // 4, block.shape[1])
        self.block = lambda i: pick(parts, i)
        self.step = 0

    def go(self, *given):
        self.step += 1
        if self.step == 1:
            return scatter_first(self.block, RING_X, self.x)
        if self.step == 2:
            return scatter_second(self.block, RING_X, self.x, *given)
        if self.step == 3:
            part = scatter_sum(self.block, self.x, *given).astype(BF)
            return part, swap(part, "zh")
        if self.step == 4:
            self.part = (given[0].astype(F32) + given[1].astype(F32)).astype(BF)
            return gather_near(self.part, RING_X)
        if self.step == 5:
            blocks = gather_far(self.part, *given, RING_X)
            return blocks[1] + blocks[2] + blocks[3]
        above, far_low, far_high, below = given
        blocks = [(self.part,), (above,), (far_low, far_high), (below,)]
        total = fill_rows(self.rows, blocks, self.x)
        return total, swap(total, "core")


def fill_fc_kernel(core_ref, mine_ref, other_ref, fc1_ref, fc2_ref):
    half = mine_ref.shape[1] // 2
    rows = fc1_ref.shape[0]
    first = core_ref[0] == 0
    mine, other = mine_ref[...].astype(F32), other_ref[...].astype(F32)
    for c, part in enumerate((jnp.where(first, mine, other), jnp.where(first, other, mine))):
        fc2_ref[half * c : half * (c + 1), :] = part[:half]
        for j in range(4):
            top = half + rows * (j // 2)
            left = half * (j % 2)
            to = half * (2 * j + c)
            fc1_ref[:, to : to + half] = part[top : top + rows, left : left + half]


def fill_attn_kernel(core_ref, mine_ref, other_ref, qkv_ref, out_ref):
    rows, width = out_ref.shape
    half = width // 2
    first = core_ref[0] == 0
    mine, other = mine_ref[...].astype(F32), other_ref[...].astype(F32)
    for c, part in enumerate((jnp.where(first, mine, other), jnp.where(first, other, mine))):
        at = half * c
        qkv_ref[:, at : at + half] = part[rows:, :half]
        qkv_ref[:, width + at : width + at + half] = part[:rows, :half]
        qkv_ref[:, 2 * width + at : 2 * width + at + half] = part[:rows, half:]
        out_ref[:, at : at + half] = part[rows:, half:]


def fill(kernel, core, total, other, shapes, name):
    whole = pl.BlockSpec(memory_space=pltpu.VMEM)
    return pl.pallas_call(
        kernel,
        in_specs=[pl.BlockSpec(memory_space=pltpu.SMEM), whole, whole],
        out_specs=[whole] * len(shapes),
        out_shape=[jax.ShapeDtypeStruct(shape, F32) for shape in shapes],
        compiler_params=pltpu.CompilerParams(vmem_limit_bytes=40 * 2**20),
        cost_estimate=pl.CostEstimate(flops=0, bytes_accessed=12 * total.size, transcendentals=0),
        name=name,
    )(core.astype(jnp.int32).reshape(1), total, other)


def on_device(ends, cond, w_ada, b_ada, w_qkv, w_out, w_fc1, w_fc2):
    section = lax.axis_index("section")
    d = lax.axis_index("dp")
    zh, xh = lax.axis_index("zh"), lax.axis_index("xh")
    a = zh * 2 + xh
    core = lax.axis_index("core")
    width = w_out.shape[2]
    half = width // 2
    rows_d = w_out.shape[1]
    columns = lambda array, start: lax.dynamic_slice_in_dim(array, start, half, 1)

    cond_float = cond.astype(F32).reshape(4, width)
    cond_low = jax.nn.silu(cond_float).astype(BF)
    cond_rows = cond_low.reshape(4, 4, rows_d).transpose(1, 0, 2)
    cond_parts = [pick(cond_rows, d)] + [
        shift(pick(cond_rows, (d + s) % 4), "dp", s) for s in (1, 2, 3)
    ]
    piece_attn = jnp.concatenate(
        [columns(w_qkv[0], width * i + half * core) for i in range(3)]
        + [columns(w_out[0], half * core)],
        axis=1,
    )

    blocks = ends[0].reshape(2, 2, *ends.shape[3:])
    mine = lax.dynamic_index_in_dim(blocks, xh, 1, keepdims=False)
    theirs = lax.dynamic_index_in_dim(blocks, 1 - xh, 1, keepdims=False)
    theirs = swap(theirs, "xh")
    piece_attn, theirs, *cond_parts = join(piece_attn, theirs, *cond_parts)
    blocks = jnp.stack([mine, theirs], axis=1)
    mine = jnp.stack([pick(blocks, zh), swap(pick(blocks, 1 - zh), "zh")])
    mine = mine.reshape(-1, width)
    tokens_half = mine.shape[0]

    below, above = gather_near(piece_attn, "dp")

    latent_rows = jnp.stack([pick(part, a) for part in cond_parts])
    bias = lax.dynamic_update_slice(
        jnp.zeros((6 * width,), F32), b_ada[0].astype(F32), (d * b_ada.shape[1],)
    )
    part_mod = dot(latent_rows, w_ada[0]) + bias[None]
    part_mod, below, above, mine = join(part_mod, below, above, mine)
    mod_parts = [shift(part_mod[s : s + 1], "dp", -s) for s in (1, 2, 3)]
    attn_blocks = gather_far(piece_attn, below, above, "dp")
    other = swap(mine, "core")
    peer = swap(mine, "xl")
    piece_fc1 = jnp.concatenate(
        [columns(w_fc1[0], width * j + half * core) for j in range(4)], axis=1
    )
    piece_fc2 = rows_at(w_fc2[0], half * core, half)
    attn_blocks, mod_parts, other, peer, piece_fc1 = join(
        attn_blocks, mod_parts, other, peer, piece_fc1
    )
    near_fc1 = gather_near(piece_fc1, "dp")
    modulation = part_mod[0:1] + mod_parts[0] + mod_parts[1] + mod_parts[2]
    modulation = [modulation[:, width * i : width * (i + 1)] for i in range(6)]
    start = ordered(core == 0, mine, other)
    start_peer = ordered(core == 0, peer, swap(peer, "core"))
    full_attn = fill_rows(width, attn_blocks, d)
    out_rows = full_attn[:, 3 * half :].reshape(2, half, half)
    full_out = ordered(
        core == 0, pick(out_rows, core), swap(pick(out_rows, 1 - core), "core"), axis=1
    )
    def across(value, pairs, with_peer):
        part = rows_at(value.astype(BF), core * tokens_half, tokens_half)
        part = lax.ppermute(part, "section", pairs)
        own = ordered(core == 0, part, swap(part, "core"))
        if not with_peer:
            return own, None
        peer = swap(part, "xl")
        return own, ordered(core == 0, peer, swap(peer, "core"))

    attn_weights = (full_attn[:, :half], full_attn[:, half : 3 * half], full_out)
    fetched = {}

    def fetch_early(queries):
        queries, fetched["near"], fetched["piece"] = join(queries, near_fc1, piece_fc2)
        fetched["fc1"] = gather_far(piece_fc1, *fetched["near"], "dp")
        return queries

    def fetch_late(mixed):
        mixed, fetched["fc1"] = join(mixed, fetched["fc1"])
        fetched["near"] = gather_near(fetched["piece"], "dp")
        return mixed

    attn_state = attend(
        start.astype(F32), start_peer, modulation, attn_weights, fetch_early, fetch_late
    )
    second, near_fc2 = join(attn_state[0], fetched["near"])
    attn_state = (second, *attn_state[1:])
    full_fc1 = fill_rows(width, fetched["fc1"], d)
    full_fc2 = fill_rows(4 * half, gather_far(piece_fc2, *near_fc2, "dp"), d)
    fc_weights = (full_fc1, full_fc2)
    weights = attn_weights + fc_weights
    result, unused = feed_forward(attn_state, modulation, fc_weights)
    arrived, arrived_peer = across(result, [(0, 1)], True)
    second_input = jnp.where(section == 0, start, arrived).astype(F32)
    second_peer = jnp.where(section == 0, start_peer, arrived_peer)
    attn_state = attend(second_input, second_peer, modulation, attn_weights)
    result, state = feed_forward(attn_state, modulation, fc_weights)

    grad_second, unused, unused_too, grad_qkv = back_front(
        start.astype(F32), state, modulation, weights
    )
    kept, given, near = back_terms(grad_qkv, weights, core)
    far = add_low(kept, swap(given, "core")).astype(BF)
    far = swap(far, "xl")
    near = near()
    near, far = join(add_low(near, swap(near, "core")), far)
    grad_entry = near + ordered(core == 0, far, swap(far, "core")).astype(F32)
    grad_input = back_end(grad_entry, grad_second, state, modulation)
    arrived, unused = across(grad_input, [(1, 0)], False)
    seed = jnp.where(section == 0, arrived, start).astype(F32)
    grad_second, grad_modulation, grads, grad_qkv = back_front(
        seed, state, modulation, weights, True
    )

    grad_out, grad_fc1, grad_fc2 = grads
    entry, entry_peer = state[2:4]
    out_own = ordered(
        core == 0,
        columns(grad_out, half * core),
        swap(columns(grad_out, half - half * core), "core"),
    )
    grad_queries, grad_keys, grad_values = grad_qkv
    entry_all = jnp.concatenate([entry, entry_peer])
    grad_q = dot_tn(entry, grad_queries).astype(BF)
    grad_k = dot_tn(entry_all, grad_keys).astype(BF)
    grad_v = dot_tn(entry_all, grad_values).astype(BF)
    kept, given, near = back_terms(grad_qkv, weights, core)
    given, grad_q, grad_k, grad_v, out_own = join(given, grad_q, grad_k, grad_v, out_own)

    def block_attn(i):
        k, v, q, out = (rows_at(g, i * rows_d, rows_d) for g in (grad_k, grad_v, grad_q, out_own))
        return jnp.concatenate(
            [jnp.concatenate([k, v], axis=1), jnp.concatenate([q, out], axis=1)]
        )

    attn = scatter_first(block_attn, "dp", d)
    given = swap(given, "core")
    near = near()
    attn, given, near = join(attn, given, near)

    attn = scatter_second(block_attn, "dp", d, *attn)
    far = swap(add_low(kept, given).astype(BF), "xl")
    near_other = swap(near, "core")
    attn, far, near_other = join(attn, far, near_other)

    plane_attn = PlaneSum(scatter_sum(block_attn, d, *attn))
    attn = plane_attn.go()
    far_other = swap(far, "core")
    attn, far_other = join(attn, far_other)

    attn = plane_attn.go(*attn)
    grad_entry = add_low(near, near_other) + ordered(core == 0, far, far_other).astype(F32)
    grad_input = back_end(grad_entry, grad_second, state, modulation)
    grad_mod = jnp.concatenate(
        [jnp.sum(grad_entry, axis=0), jnp.sum(grad_entry * state[0], axis=0), *grad_modulation]
    ).reshape(1, 6 * width)
    edge = jnp.where(section == 0, grad_input, result)
    edge = rows_at(edge, core * tokens_half, tokens_half).reshape(2, 2, -1, width)
    attn, grad_mod, edge, grad_fc1, grad_fc2 = join(attn, grad_mod, edge, grad_fc1, grad_fc2)

    attn = plane_attn.go(*attn)
    plane_fc = PlaneSum(jnp.concatenate([grad_fc2, grad_fc1[:, :width], grad_fc1[:, width:]]))
    fc = plane_fc.go()
    other = swap(grad_mod, "xl")
    attn, fc, other = join(attn, fc, other)

    attn = plane_attn.go(*attn)
    fc = plane_fc.go(*fc)
    grad_mod = grad_mod + other
    others = (
        swap(grad_mod, "xh"),
        swap(grad_mod, "zh"),
        lax.ppermute(grad_mod, ("zh", "xh"), [(i, 3 - i) for i in range(4)]),
    )
    attn, fc, others = join(attn, fc, others)

    attn = plane_attn.go(*attn)
    fc = plane_fc.go(*fc)
    plane_mod = ordered(
        zh == 0, ordered(xh == 0, grad_mod, others[0]), ordered(xh == 0, others[1], others[2])
    )
    others = [shift(plane_mod, "dp", s) for s in (1, 2, 3)]
    edge_other = swap(edge[1:].astype(BF), "zh")
    attn, fc, others, edge_other = join(attn, fc, others, edge_other)

    attn = plane_attn.go(*attn)
    fc = plane_fc.go(*fc)
    all_mod = jnp.concatenate([plane_mod, *others])
    grad_silu = lax.dot_general(
        all_mod,
        w_ada[0].astype(F32),
        (((1,), (1,)), ((), ())),
        precision=lax.Precision.HIGHEST,
    ).reshape(4, 4, rows_d)
    silu_parts = [grad_silu[0]] + [shift(grad_silu[s], "dp", -s) for s in (1, 2, 3)]
    edge = ordered(zh == 0, edge[:1], edge_other.astype(F32))
    edge_other = swap(edge[:, 1:].astype(BF), "xh")
    attn, fc, silu_parts, edge_other = join(attn, fc, silu_parts, edge_other)

    fc = plane_fc.go(*fc)
    silu_full = jnp.zeros((4, 4, rows_d), F32)
    for s in range(4):
        silu_full = lax.dynamic_update_index_in_dim(silu_full, silu_parts[s], (d + s) % 4, 0)
    silu_full = silu_full.transpose(1, 0, 2).reshape(4, width)
    silu_other = swap(silu_full, "section")
    out_qkv, out_out = fill(
        fill_attn_kernel, core, *attn, ((rows_d, 6 * half), (rows_d, width)), "fill_attn"
    )
    fc, silu_other, out_qkv = join(fc, silu_other, out_qkv)

    fc = plane_fc.go(*fc)
    unused, silu_pull = jax.vjp(jax.nn.silu, cond_float)
    out_cond = silu_pull(silu_full + silu_other)[0].reshape(cond.shape)
    all_cond = jnp.concatenate(cond_parts)
    out_ada = lax.dot_general(
        all_cond.astype(F32), all_mod, (((0,), (0,)), ((), ())), precision=lax.Precision.HIGHEST
    )
    out_bias = jnp.sum(
        lax.dynamic_slice_in_dim(all_mod, d * b_ada.shape[1], b_ada.shape[1], 1), axis=0
    )
    boundary = ordered(xh == 0, edge[:, :1], edge_other.astype(F32), axis=1).reshape(ends.shape)
    out_fc1, out_fc2 = fill(
        fill_fc_kernel, core, *fc, ((rows_d, 8 * half), (2 * half, width)), "fill_fc"
    )

    return (
        boundary,
        out_cond,
        out_ada[None],
        out_bias[None],
        out_qkv[None],
        out_out[None],
        out_fc1[None],
        out_fc2[None],
    )


def solution(mesh):
    finer = Mesh(
        mesh.devices.reshape(2, 4, 2, 2, 2, 2), ("section", "dp", "zh", "xh", "xl", "core")
    )
    ends_spec = P("section", None, "dp", CTX, None)
    cond_spec = P(None, "dp", None)
    matrix = P("section", "dp", None)
    vector = P("section", "dp")
    return jax.shard_map(
        on_device,
        mesh=finer,
        in_specs=(ends_spec, cond_spec, matrix, vector, matrix, matrix, matrix, matrix),
        out_specs=(ends_spec, cond_spec, matrix, vector, matrix, matrix, matrix, matrix),
        check_vma=False,
    )
```

```python
import jax
import jax.numpy as jnp
from jax import lax
from jax.experimental import pallas as pl
from jax.experimental.pallas import tpu as pltpu
from jax.sharding import Mesh
from jax.sharding import PartitionSpec as P

HEAD = 64
BF = jnp.bfloat16
F32 = jnp.float32
RING_X = ("xh", "xl")
CTX = ("zh", "xh", "xl", "core")


def shift(array, axis, by, size=4):
    return lax.ppermute(array, axis, [(i, (i + by) % size) for i in range(size)])


def swap(array, axis):
    return lax.ppermute(array, axis, [(0, 1), (1, 0)])


def swap_odd(array):
    return lax.ppermute(array, RING_X, [(0, 3), (1, 2), (2, 1), (3, 0)])


def pick(blocks, index):
    return lax.dynamic_index_in_dim(blocks, index, 0, keepdims=False)


def rows_at(array, start, size):
    return lax.dynamic_slice_in_dim(array, start, size, 0)


def ordered(first, mine, other, axis=0):
    return jnp.where(
        first,
        jnp.concatenate([mine, other], axis=axis),
        jnp.concatenate([other, mine], axis=axis),
    )


def gather_near(piece, axis):
    return shift(piece, axis, 1), shift(piece, axis, -1)


def gather_far(piece, below, above, axis):
    half = piece.shape[0] // 2
    far_low = shift(below[:half], axis, 1)
    far_high = shift(above[half:], axis, -1)
    return [(piece,), (above,), (far_low, far_high), (below,)]


def scatter_first(block, axis, index):
    far = block((index + 2) % 4)
    half = far.shape[0] // 2
    return shift(far[:half], axis, 1), shift(far[half:], axis, -1)


def scatter_second(block, axis, index, from_below, from_above):
    add = lambda one, two: (one.astype(F32) + two.astype(F32)).astype(BF)
    half = from_below.shape[0]
    up = block((index + 1) % 4)
    up = jnp.concatenate([add(up[:half], from_below), up[half:]])
    down = block((index + 3) % 4)
    down = jnp.concatenate([down[:half], add(down[half:], from_above)])
    return shift(up, axis, 1), shift(down, axis, -1)


def scatter_sum(block, index, got_up, got_down):
    return block(index).astype(F32) + got_up.astype(F32) + got_down.astype(F32)


def fill_rows(size, blocks, index):
    total = jnp.zeros((size, blocks[0][0].shape[1]), BF)
    for s, pieces in enumerate(blocks):
        at = (index + s) % 4 * (size // 4)
        for piece in pieces:
            total = lax.dynamic_update_slice(total, piece, (at, 0))
            at = at + piece.shape[0]
    return total


def join(*values):
    return lax.optimization_barrier(values)


def dot(left, right):
    return jnp.dot(left, right, preferred_element_type=F32)


def dot_nt(left, right):
    return lax.dot_general(left, right, (((1,), (1,)), ((), ())), preferred_element_type=F32)


def dot_tn(left, right):
    return lax.dot_general(left, right, (((0,), (0,)), ((), ())), preferred_element_type=F32)


def attention_kernel(q_ref, ko_ref, kp_ref, vo_ref, vp_ref, out_ref, lse_ref):
    rows = q_ref.shape[0]
    step = 256
    for h in range(2):
        cols = slice(HEAD * h, HEAD * (h + 1))
        keys_own, keys_peer = ko_ref[:, cols], kp_ref[:, cols]
        values_own, values_peer = vo_ref[:, cols], vp_ref[:, cols]
        for start in range(0, rows, step):
            queries = q_ref[start : start + step, cols] * HEAD ** (-0.5)
            scores_own = dot_nt(keys_own, queries)
            scores_peer = dot_nt(keys_peer, queries)
            top = jnp.maximum(
                jnp.max(scores_own, axis=0, keepdims=True),
                jnp.max(scores_peer, axis=0, keepdims=True),
            )
            probs_own = jnp.exp(scores_own - top)
            probs_peer = jnp.exp(scores_peer - top)
            total = jnp.sum(probs_own, axis=0, keepdims=True) + jnp.sum(
                probs_peer, axis=0, keepdims=True
            )
            mixed = dot_tn(values_own, probs_own.astype(BF)) + dot_tn(
                values_peer, probs_peer.astype(BF)
            )
            mixed = mixed / total
            out_ref[start : start + step, cols] = mixed.T.astype(BF)
            lse_ref[0, h : h + 1, start : start + step] = top + jnp.log(total)


def attention(queries, kv_own, kv_peer):
    rows, width = queries.shape
    pairs = width // 128
    block = lambda offset: pl.BlockSpec((rows, 128), lambda h: (0, h + offset))
    return pl.pallas_call(
        attention_kernel,
        grid=(pairs,),
        in_specs=[block(0), block(0), block(0), block(pairs), block(pairs)],
        out_specs=[block(0), pl.BlockSpec((1, 2, rows), lambda h: (h, 0, 0))],
        out_shape=[
            jax.ShapeDtypeStruct((rows, width), BF),
            jax.ShapeDtypeStruct((pairs, 2, rows), F32),
        ],
        compiler_params=pltpu.CompilerParams(vmem_limit_bytes=40 * 2**20),
        cost_estimate=pl.CostEstimate(
            flops=100 * rows * rows * width,
            bytes_accessed=12 * rows * width,
            transcendentals=2 * rows * rows * width // HEAD,
        ),
        name="attention",
    )(queries, kv_own, kv_peer, kv_own, kv_peer)


def attention_back_kernel(
    q_ref, ko_ref, kp_ref, vo_ref, vp_ref, out_ref, gout_ref, lse_ref, gq_ref, gk_ref, gv_ref
):
    rows = q_ref.shape[0]
    step = 256
    scale = HEAD ** (-0.5)
    for h in range(2):
        cols = slice(HEAD * h, HEAD * (h + 1))
        sides = ((ko_ref, vo_ref), (kp_ref, vp_ref))
        grad_kv = [[None, None], [None, None]]
        for start in range(0, rows, step):
            span = slice(start, start + step)
            queries = q_ref[span, cols] * scale
            grad_out = gout_ref[span, cols]
            lse = lse_ref[0, h : h + 1, span]
            both = grad_out.astype(F32) * out_ref[span, cols].astype(F32)
            row_total = jnp.sum(both.T, axis=0, keepdims=True)
            grad_queries = None
            for side, (k_ref, v_ref) in enumerate(sides):
                keys, values = k_ref[:, cols], v_ref[:, cols]
                probs = jnp.exp(dot_nt(keys, queries) - lse)
                grad_probs = dot_nt(values, grad_out)
                grad_scores = (probs * (grad_probs - row_total)).astype(BF)
                part = dot_tn(keys, grad_scores)
                grad_queries = part if grad_queries is None else grad_queries + part
                terms = (dot(grad_scores, queries), dot(probs.astype(BF), grad_out))
                for i in range(2):
                    old = grad_kv[side][i]
                    grad_kv[side][i] = terms[i] if old is None else old + terms[i]
            gq_ref[span, cols] = (grad_queries * scale).T.astype(BF)
        for side in range(2):
            span = slice(rows * side, rows * (side + 1))
            gk_ref[span, cols] = grad_kv[side][0].astype(BF)
            gv_ref[span, cols] = grad_kv[side][1].astype(BF)


def attention_back(queries, kv_own, kv_peer, mixed, grad_mixed, lse):
    rows, width = queries.shape
    pairs = width // 128
    block = lambda offset: pl.BlockSpec((rows, 128), lambda h: (0, h + offset))
    double = pl.BlockSpec((2 * rows, 128), lambda h: (0, h))
    return pl.pallas_call(
        attention_back_kernel,
        grid=(pairs,),
        in_specs=[
            block(0),
            block(0),
            block(0),
            block(pairs),
            block(pairs),
            block(0),
            block(0),
            pl.BlockSpec((1, 2, rows), lambda h: (h, 0, 0)),
        ],
        out_specs=[block(0), double, double],
        out_shape=[
            jax.ShapeDtypeStruct((rows, width), BF),
            jax.ShapeDtypeStruct((2 * rows, width), BF),
            jax.ShapeDtypeStruct((2 * rows, width), BF),
        ],
        compiler_params=pltpu.CompilerParams(vmem_limit_bytes=40 * 2**20),
        cost_estimate=pl.CostEstimate(
            flops=130 * rows * rows * width,
            bytes_accessed=24 * rows * width,
            transcendentals=2 * rows * rows * width // HEAD,
        ),
        name="attention_back",
    )(queries, kv_own, kv_peer, kv_own, kv_peer, mixed, grad_mixed, lse)


def norm_stats(activations):
    center = activations - jnp.mean(activations, axis=-1, keepdims=True)
    inverse = lax.rsqrt(jnp.mean(center * center, axis=-1, keepdims=True) + 1e-06)
    return (center * inverse, inverse)


def norm_back(grad_norm, normal, inverse):
    return inverse * (
        grad_norm
        - jnp.mean(grad_norm, axis=-1, keepdims=True)
        - normal * jnp.mean(grad_norm * normal, axis=-1, keepdims=True)
    )


def core_sum(partial_sum):
    low = partial_sum.astype(BF)
    return low.astype(F32) + swap(low, "core").astype(F32)


def gelu_and_slope(pre_act):
    linear = 2.0 * (2.0 / jnp.pi) ** 0.5
    cubic = 0.044715 * linear
    square = pre_act * pre_act
    gate = 1.0 / (1.0 + jnp.exp(-pre_act * (linear + cubic * square)))
    value = pre_act * gate
    slope = gate + value * (1.0 - gate) * (linear + 3.0 * cubic * square)
    return value.astype(BF), slope.astype(BF)


def attend(activations, activations_peer, modulation, weights, before=None, after=None):
    w_q, w_kv, w_out = weights
    shift_first, scale_first, gate_first = modulation[:3]
    normal_first, inverse_first = norm_stats(activations)
    entry = (normal_first * (1.0 + scale_first) + shift_first).astype(BF)
    kv_own = dot(entry, w_kv).astype(BF)
    queries = dot(entry, w_q).astype(BF)
    activations_peer, kv_own, queries = lax.optimization_barrier(
        (activations_peer, kv_own, queries)
    )
    entry_peer = norm_stats(activations_peer.astype(F32))[0] * (1.0 + scale_first) + shift_first
    entry_peer = entry_peer.astype(BF)
    kv_peer = dot(entry_peer, w_kv).astype(BF)
    if before:
        queries = before(queries)
    mixed, lse = attention(queries, kv_own, kv_peer)
    if after:
        mixed = after(mixed)
    branch = core_sum(dot(mixed, w_out))
    second = activations + gate_first * branch
    return (
        second,
        normal_first,
        inverse_first,
        entry,
        entry_peer,
        queries,
        kv_own,
        kv_peer,
        lse,
        mixed,
        branch,
    )


def feed_forward(attn_state, modulation, weights):
    w_fc1, w_fc2 = weights
    shift_second, scale_second, gate_second = modulation[3:]
    second, *kept = attn_state
    normal_second, inverse_second = norm_stats(second)
    mlp_input = (normal_second * (1.0 + scale_second) + shift_second).astype(BF)
    hidden, slope = gelu_and_slope(dot(mlp_input, w_fc1))
    branch_mlp = core_sum(dot(hidden, w_fc2))
    result = second + gate_second * branch_mlp
    state = (*kept, normal_second, inverse_second, mlp_input, slope, hidden, branch_mlp)
    return (result, state)


def back_front(grad_result, state, modulation, weights, reduced=False):
    w_q, w_kv, w_out, w_fc1, w_fc2 = weights
    shift_first, scale_first, gate_first, shift_second, scale_second, gate_second = modulation
    (
        normal_first,
        inverse_first,
        entry,
        entry_peer,
        queries,
        kv_own,
        kv_peer,
        lse,
        mixed,
        branch,
        normal_second,
        inverse_second,
        mlp_input,
        slope,
        hidden,
        branch_mlp,
    ) = state
    rows = lambda value: jnp.sum(value, axis=0)
    grad_gate_second = rows(grad_result * branch_mlp)
    grad_branch_mlp = (grad_result * gate_second).astype(BF)
    grad_hidden = dot_nt(grad_branch_mlp, w_fc2)
    grad_pre = (grad_hidden * slope.astype(F32)).astype(BF)
    grad_mlp_input = core_sum(dot_nt(grad_pre, w_fc1))
    grad_fc2 = dot_tn(hidden, grad_branch_mlp).astype(BF)
    grad_fc1 = dot_tn(mlp_input, grad_pre).astype(BF)
    if reduced:
        grad_fc2 = lax.psum_scatter(grad_fc2, "dp", scatter_dimension=0, tiled=True)
    grad_scale_second = rows(grad_mlp_input * normal_second)
    grad_shift_second = rows(grad_mlp_input)
    grad_second = grad_result + norm_back(
        grad_mlp_input * (1.0 + scale_second), normal_second, inverse_second
    )
    grad_gate_first = rows(grad_second * branch)
    grad_branch = (grad_second * gate_first).astype(BF)
    grad_mixed = dot_nt(grad_branch, w_out).astype(BF)
    grad_out = dot_tn(mixed, grad_branch).astype(BF)
    grad_queries, grad_keys, grad_values = attention_back(
        queries, kv_own, kv_peer, mixed, grad_mixed, lse
    )
    grad_modulation = (
        grad_gate_first,
        grad_shift_second,
        grad_scale_second,
        grad_gate_second,
    )
    if reduced:
        grad_queries, grad_fc2, grad_fc1 = join(grad_queries, grad_fc2, grad_fc1)
        grad_fc1 = lax.psum_scatter(grad_fc1, "dp", scatter_dimension=0, tiled=True)
    grads = (grad_out, grad_fc1, grad_fc2)
    return grad_second, grad_modulation, grads, (grad_queries, grad_keys, grad_values)


def back_terms(grad_qkv, weights, core):
    w_q, w_kv = weights[:2]
    grad_queries, grad_keys, grad_values = grad_qkv
    tokens, half = grad_queries.shape
    w_k, w_v = w_kv[:, :half], w_kv[:, half:]
    far = (
        dot_nt(grad_keys[tokens:], w_k) + dot_nt(grad_values[tokens:], w_v)
    ).astype(BF)
    kept = rows_at(far, core * (tokens // 2), tokens // 2)
    given = rows_at(far, (1 - core) * (tokens // 2), tokens // 2)
    near = lambda: (
        dot_nt(grad_queries, w_q)
        + dot_nt(grad_keys[:tokens], w_k)
        + dot_nt(grad_values[:tokens], w_v)
    ).astype(BF)
    return kept, given, near


def add_low(one, two):
    return one.astype(F32) + two.astype(F32)


def back_end(grad_entry, grad_second, state, modulation):
    normal_first, inverse_first = state[:2]
    return grad_second + norm_back(
        grad_entry * (1.0 + modulation[1]), normal_first, inverse_first
    )


class PlaneSum:
    def __init__(self, block):
        x = lax.axis_index(RING_X)
        self.half, self.quarter = (x + 1) // 2 % 2, x // 2
        self.kept = block.astype(BF)
        self.step = 0

    def go(self, got=None, rider=None):
        self.step += 1
        if self.step in (2, 3, 4):
            self.kept = add_low(self.kept, got).astype(BF)
        elif self.step > 4:
            first = (self.quarter if self.step == 5 else self.half) == 0
            self.kept = ordered(first, self.kept, got)
        sent = self.kept
        if self.step < 3:
            index = self.half if self.step == 1 else self.quarter
            parts = sent.reshape(2, -1, sent.shape[1])
            self.kept, sent = pick(parts, index), pick(parts, 1 - index)
        rows = sent.shape[0]
        if rider is not None:
            sent = jnp.concatenate([sent, rider])
        axis = (None, "xl", "odd", "zh", "odd", "xl", "core")[self.step]
        got = swap_odd(sent) if axis == "odd" else swap(sent, axis)
        return got if rider is None else (got[:rows], got[rows:])


def fill_fc1_kernel(core_ref, mine_ref, other_ref, fc1_ref):
    half = mine_ref.shape[1] // 2
    rows = fc1_ref.shape[0]
    first = core_ref[0] == 0
    mine, other = mine_ref[...].astype(F32), other_ref[...].astype(F32)
    for c, part in enumerate((jnp.where(first, mine, other), jnp.where(first, other, mine))):
        for j in range(4):
            top = rows * (j // 2)
            left = half * (j % 2)
            to = half * (2 * j + c)
            fc1_ref[:, to : to + half] = part[top : top + rows, left : left + half]


def fill_rest_kernel(core_ref, mine_ref, other_ref, qkv_ref, out_ref, fc2_ref):
    rows, width = out_ref.shape
    half = width // 2
    first = core_ref[0] == 0
    mine, other = mine_ref[...].astype(F32), other_ref[...].astype(F32)
    for c, part in enumerate((jnp.where(first, mine, other), jnp.where(first, other, mine))):
        at = half * c
        qkv_ref[:, at : at + half] = part[rows : 2 * rows, :half]
        qkv_ref[:, width + at : width + at + half] = part[:rows, :half]
        qkv_ref[:, 2 * width + at : 2 * width + at + half] = part[:rows, half:]
        out_ref[:, at : at + half] = part[rows : 2 * rows, half:]
        fc2_ref[half * c : half * (c + 1), :] = part[2 * rows :]


def fill(kernel, core, total, other, shapes, name):
    whole = pl.BlockSpec(memory_space=pltpu.VMEM)
    return pl.pallas_call(
        kernel,
        in_specs=[pl.BlockSpec(memory_space=pltpu.SMEM), whole, whole],
        out_specs=[whole] * len(shapes),
        out_shape=[jax.ShapeDtypeStruct(shape, F32) for shape in shapes],
        compiler_params=pltpu.CompilerParams(vmem_limit_bytes=40 * 2**20),
        cost_estimate=pl.CostEstimate(flops=0, bytes_accessed=12 * total.size, transcendentals=0),
        name=name,
    )(core.astype(jnp.int32).reshape(1), total, other)


def on_device(ends, cond, w_ada, b_ada, w_qkv, w_out, w_fc1, w_fc2):
    section = lax.axis_index("section")
    d = lax.axis_index("dp")
    zh, xh = lax.axis_index("zh"), lax.axis_index("xh")
    a = zh * 2 + xh
    core = lax.axis_index("core")
    width = w_out.shape[2]
    half = width // 2
    rows_d = w_out.shape[1]
    columns = lambda array, start: lax.dynamic_slice_in_dim(array, start, half, 1)

    cond_float = cond.astype(F32).reshape(4, width)
    cond_low = jax.nn.silu(cond_float).astype(BF)
    cond_rows = cond_low.reshape(4, 4, rows_d).transpose(1, 0, 2)
    cond_parts = [pick(cond_rows, d)] + [
        shift(pick(cond_rows, (d + s) % 4), "dp", s) for s in (1, 2, 3)
    ]
    piece_attn = jnp.concatenate(
        [columns(w_qkv[0], width * i + half * core) for i in range(3)]
        + [columns(w_out[0], half * core)],
        axis=1,
    )

    blocks = ends[0].reshape(2, 2, *ends.shape[3:])
    mine = lax.dynamic_index_in_dim(blocks, xh, 1, keepdims=False)
    theirs = lax.dynamic_index_in_dim(blocks, 1 - xh, 1, keepdims=False)
    theirs = swap_odd(theirs)
    piece_attn, theirs, *cond_parts = join(piece_attn, theirs, *cond_parts)
    blocks = jnp.stack([mine, theirs], axis=1)
    mine = jnp.stack([pick(blocks, zh), swap(pick(blocks, 1 - zh), "zh")])
    mine = mine.reshape(-1, width)
    tokens_half = mine.shape[0]

    below, above = gather_near(piece_attn, "dp")

    latent_rows = jnp.stack([pick(part, a) for part in cond_parts])
    bias = lax.dynamic_update_slice(
        jnp.zeros((6 * width,), F32), b_ada[0].astype(F32), (d * b_ada.shape[1],)
    )
    part_mod = dot(latent_rows, w_ada[0]) + bias[None]
    part_mod, below, above, mine = join(part_mod, below, above, mine)
    mod_parts = [shift(part_mod[s : s + 1], "dp", -s) for s in (1, 2, 3)]
    attn_blocks = gather_far(piece_attn, below, above, "dp")
    other = swap(mine, "core")
    peer = swap(mine, "xl")
    piece_fc1 = jnp.concatenate(
        [columns(w_fc1[0], width * j + half * core) for j in range(4)], axis=1
    )
    piece_fc2 = rows_at(w_fc2[0], half * core, half)
    attn_blocks, mod_parts, other, peer, piece_fc1 = join(
        attn_blocks, mod_parts, other, peer, piece_fc1
    )
    near_fc1 = gather_near(piece_fc1, "dp")
    modulation = part_mod[0:1] + mod_parts[0] + mod_parts[1] + mod_parts[2]
    modulation = [modulation[:, width * i : width * (i + 1)] for i in range(6)]
    start = ordered(core == 0, mine, other)
    start_peer = ordered(core == 0, peer, swap(peer, "core"))
    full_attn = fill_rows(width, attn_blocks, d)
    out_rows = full_attn[:, 3 * half :].reshape(2, half, half)
    full_out = ordered(
        core == 0, pick(out_rows, core), swap(pick(out_rows, 1 - core), "core"), axis=1
    )
    def across(value, pairs, with_peer):
        part = rows_at(value.astype(BF), core * tokens_half, tokens_half)
        part = lax.ppermute(part, "section", pairs)
        own = ordered(core == 0, part, swap(part, "core"))
        if not with_peer:
            return own, None
        peer = swap(part, "xl")
        return own, ordered(core == 0, peer, swap(peer, "core"))

    attn_weights = (full_attn[:, :half], full_attn[:, half : 3 * half], full_out)
    fetched = {}

    def fetch_early(queries):
        queries, fetched["near"], fetched["piece"] = join(queries, near_fc1, piece_fc2)
        fetched["fc1"] = gather_far(piece_fc1, *fetched["near"], "dp")
        return queries

    def fetch_late(mixed):
        mixed, fetched["fc1"] = join(mixed, fetched["fc1"])
        fetched["near"] = gather_near(fetched["piece"], "dp")
        return mixed

    attn_state = attend(
        start.astype(F32), start_peer, modulation, attn_weights, fetch_early, fetch_late
    )
    second, near_fc2 = join(attn_state[0], fetched["near"])
    attn_state = (second, *attn_state[1:])
    full_fc1 = fill_rows(width, fetched["fc1"], d)
    full_fc2 = fill_rows(4 * half, gather_far(piece_fc2, *near_fc2, "dp"), d)
    fc_weights = (full_fc1, full_fc2)
    weights = attn_weights + fc_weights
    result, unused = feed_forward(attn_state, modulation, fc_weights)
    arrived, arrived_peer = across(result, [(0, 1)], True)
    second_input = jnp.where(section == 0, start, arrived).astype(F32)
    second_peer = jnp.where(section == 0, start_peer, arrived_peer)
    attn_state = attend(second_input, second_peer, modulation, attn_weights)
    result, state = feed_forward(attn_state, modulation, fc_weights)

    grad_second, unused, unused_too, grad_qkv = back_front(
        start.astype(F32), state, modulation, weights
    )
    kept, given, near = back_terms(grad_qkv, weights, core)
    far = add_low(kept, swap(given, "core")).astype(BF)
    far = swap(far, "xl")
    near = near()
    near, far = join(add_low(near, swap(near, "core")), far)
    grad_entry = near + ordered(core == 0, far, swap(far, "core")).astype(F32)
    grad_input = back_end(grad_entry, grad_second, state, modulation)
    arrived, unused = across(grad_input, [(1, 0)], False)
    seed = jnp.where(section == 0, arrived, start).astype(F32)
    grad_second, grad_modulation, grads, grad_qkv = back_front(
        seed, state, modulation, weights, True
    )

    grad_out, grad_fc1, grad_fc2 = grads
    entry, entry_peer = state[2:4]
    out_own = ordered(
        core == 0,
        columns(grad_out, half * core),
        swap(columns(grad_out, half - half * core), "core"),
    )
    grad_queries, grad_keys, grad_values = grad_qkv
    entry_all = jnp.concatenate([entry, entry_peer])
    grad_q = dot_tn(entry, grad_queries).astype(BF)
    grad_k = dot_tn(entry_all, grad_keys).astype(BF)
    grad_v = dot_tn(entry_all, grad_values).astype(BF)
    kept, given, near = back_terms(grad_qkv, weights, core)
    given, grad_q, grad_k, grad_v, out_own = join(given, grad_q, grad_k, grad_v, out_own)

    def block_attn(i):
        k, v, q, out = (rows_at(g, i * rows_d, rows_d) for g in (grad_k, grad_v, grad_q, out_own))
        return jnp.concatenate(
            [jnp.concatenate([k, v], axis=1), jnp.concatenate([q, out], axis=1)]
        )

    attn = scatter_first(block_attn, "dp", d)
    given = swap(given, "core")
    near = near()
    attn, given, near = join(attn, given, near)

    attn = scatter_second(block_attn, "dp", d, *attn)
    far = swap(add_low(kept, given).astype(BF), "xl")
    near_other = swap(near, "core")
    attn, far, near_other = join(attn, far, near_other)

    plane_main = PlaneSum(jnp.concatenate([scatter_sum(block_attn, d, *attn), grad_fc2]))
    main = plane_main.go()
    far_other = swap(far, "core")
    main, far_other = join(main, far_other)

    main = plane_main.go(main)
    grad_entry = add_low(near, near_other) + ordered(core == 0, far, far_other).astype(F32)
    grad_input = back_end(grad_entry, grad_second, state, modulation)
    grad_mod = [jnp.sum(grad_entry, axis=0), jnp.sum(grad_entry * state[0], axis=0)]
    grad_mod = jnp.stack([*grad_mod, *grad_modulation]).astype(BF)
    grad_mod = jnp.pad(grad_mod, ((0, 10), (0, 0)))
    edge = jnp.where(section == 0, grad_input, result)
    edge = rows_at(edge, core * tokens_half, tokens_half).reshape(2, 2, -1, width)
    main, grad_mod, edge, grad_fc1 = join(main, grad_mod, edge, grad_fc1)

    plane_late = PlaneSum(jnp.concatenate([grad_fc1[:, :width], grad_fc1[:, width:]]))
    main = plane_main.go(main)
    late = plane_late.go(None, grad_mod)
    main, late = join(main, late)

    main = plane_main.go(main)
    late, other = late
    grad_mod = add_low(grad_mod, other).astype(BF)
    late = plane_late.go(late, grad_mod)
    main, late = join(main, late)

    main = plane_main.go(main)
    late, other = late
    plane_mod = ordered(xh == 0, grad_mod, other)
    late = plane_late.go(
        late, jnp.concatenate([plane_mod, edge[1].reshape(-1, width).astype(BF)])
    )
    main, late = join(main, late)

    main = plane_main.go(main)
    late, other = late
    mod_rows = plane_mod.shape[0]
    plane_mod = ordered(zh == 0, plane_mod, other[:mod_rows]).reshape(4, -1, width)[:, :6]
    plane_mod = plane_mod.astype(F32).reshape(4, 6 * width)
    other = other[mod_rows:].reshape(edge[1:].shape).astype(F32)
    edge = ordered(zh == 0, edge[:1], other)
    late = plane_late.go(late, edge[:, 1].reshape(-1, width).astype(BF))
    others = [shift(plane_mod, "dp", s) for s in (1, 2, 3)]
    main, late, others = join(main, late, others)

    late, other = late
    other = other.reshape(edge[:, 1:].shape).astype(F32)
    boundary = ordered(xh == 0, edge[:, :1], other, axis=1).reshape(ends.shape)
    late = plane_late.go(late)
    all_mod = jnp.concatenate([plane_mod, *others])
    grad_silu = lax.dot_general(
        all_mod,
        w_ada[0].astype(F32),
        (((1,), (1,)), ((), ())),
        precision=lax.Precision.HIGHEST,
    ).reshape(4, 4, rows_d)
    silu_parts = [grad_silu[0]] + [shift(grad_silu[s], "dp", -s) for s in (1, 2, 3)]
    out_qkv, out_out, out_fc2 = fill(
        fill_rest_kernel,
        core,
        plane_main.kept,
        main,
        ((rows_d, 6 * half), (rows_d, width), (2 * half, width)),
        "fill_rest",
    )
    late, silu_parts, out_qkv = join(late, silu_parts, out_qkv)

    late = plane_late.go(late)
    silu_full = jnp.zeros((4, 4, rows_d), F32)
    for s in range(4):
        silu_full = lax.dynamic_update_index_in_dim(silu_full, silu_parts[s], (d + s) % 4, 0)
    silu_full = silu_full.transpose(1, 0, 2).reshape(4, width)
    silu_other = swap(silu_full, "section")
    all_cond = jnp.concatenate(cond_parts)
    out_ada = lax.dot_general(
        all_cond.astype(F32), all_mod, (((0,), (0,)), ((), ())), precision=lax.Precision.HIGHEST
    )
    out_bias = jnp.sum(
        lax.dynamic_slice_in_dim(all_mod, d * b_ada.shape[1], b_ada.shape[1], 1), axis=0
    )
    unused, silu_pull = jax.vjp(jax.nn.silu, cond_float)
    out_cond = silu_pull(silu_full + silu_other)[0].reshape(cond.shape)
    (out_fc1,) = fill(
        fill_fc1_kernel, core, plane_late.kept, late, ((rows_d, 8 * half),), "fill_fc1"
    )

    return (
        boundary,
        out_cond,
        out_ada[None],
        out_bias[None],
        out_qkv[None],
        out_out[None],
        out_fc1[None],
        out_fc2[None],
    )


def solution(mesh):
    finer = Mesh(
        mesh.devices.reshape(2, 4, 2, 2, 2, 2), ("section", "dp", "zh", "xh", "xl", "core")
    )
    ends_spec = P("section", None, "dp", CTX, None)
    cond_spec = P(None, "dp", None)
    matrix = P("section", "dp", None)
    vector = P("section", "dp")
    return jax.shard_map(
        on_device,
        mesh=finer,
        in_specs=(ends_spec, cond_spec, matrix, vector, matrix, matrix, matrix, matrix),
        out_specs=(ends_spec, cond_spec, matrix, vector, matrix, matrix, matrix, matrix),
        check_vma=False,
    )
```

```python
import jax
import jax.numpy as jnp
from jax import lax
from jax.experimental import pallas as pl
from jax.experimental.pallas import tpu as pltpu
from jax.sharding import Mesh
from jax.sharding import PartitionSpec as P

HEAD = 64
BF = jnp.bfloat16
F32 = jnp.float32
RING_X = ("xh", "xl")
CTX = ("zh", "xh", "xl", "core")


def shift(array, axis, by, size=4):
    return lax.ppermute(array, axis, [(i, (i + by) % size) for i in range(size)])


def swap(array, axis):
    return lax.ppermute(array, axis, [(0, 1), (1, 0)])


def swap_odd(array, axis):
    return lax.ppermute(array, axis, [(0, 3), (1, 2), (2, 1), (3, 0)])


def swap_even(array, axis):
    return lax.ppermute(array, axis, [(0, 1), (1, 0), (2, 3), (3, 2)])


def pick(blocks, index):
    return lax.dynamic_index_in_dim(blocks, index, 0, keepdims=False)


def rows_at(array, start, size):
    return lax.dynamic_slice_in_dim(array, start, size, 0)


def ordered(first, mine, other, axis=0):
    return jnp.where(
        first,
        jnp.concatenate([mine, other], axis=axis),
        jnp.concatenate([other, mine], axis=axis),
    )


def gather_small(piece, axis, index):
    two = ordered(index % 2 == 0, piece, swap_even(piece, axis))
    return ordered(index < 2, two, swap_odd(two, axis))


def gather_near(piece, axis):
    return shift(piece, axis, 1), shift(piece, axis, -1)


def gather_far(piece, below, above, axis):
    half = piece.shape[0] // 2
    far_low = shift(below[:half], axis, 1)
    far_high = shift(above[half:], axis, -1)
    return [(piece,), (above,), (far_low, far_high), (below,)]


def fill_rows(size, blocks, index):
    total = jnp.zeros((size, blocks[0][0].shape[1]), BF)
    for s, pieces in enumerate(blocks):
        at = (index + s) % 4 * (size // 4)
        for piece in pieces:
            total = lax.dynamic_update_slice(total, piece, (at, 0))
            at = at + piece.shape[0]
    return total


def join(*values):
    return lax.optimization_barrier(values)


def scatter_ring(block, axis, index, after):
    add = lambda one, two: (one.astype(F32) + two.astype(F32)).astype(BF)
    far = block((index + 2) % 4)
    half = far.shape[0] // 2
    from_below = shift(far[:half], axis, 1)
    from_above = shift(far[half:], axis, -1)
    from_below, from_above, after = join(from_below, from_above, after)
    up = block((index + 1) % 4)
    up = jnp.concatenate([add(up[:half], from_below), up[half:]])
    down = block((index + 3) % 4)
    down = jnp.concatenate([down[:half], add(down[half:], from_above)])
    got_up = shift(up, axis, 1)
    got_down = shift(down, axis, -1)
    return block(index).astype(F32) + got_up.astype(F32) + got_down.astype(F32)


def dot(left, right):
    return jnp.dot(left, right, preferred_element_type=F32)


def dot_nt(left, right):
    return lax.dot_general(left, right, (((1,), (1,)), ((), ())), preferred_element_type=F32)


def dot_tn(left, right):
    return lax.dot_general(left, right, (((0,), (0,)), ((), ())), preferred_element_type=F32)


def attention_kernel(q_ref, ko_ref, kp_ref, vo_ref, vp_ref, out_ref, lse_ref):
    rows = q_ref.shape[0]
    step = 256
    for h in range(2):
        cols = slice(HEAD * h, HEAD * (h + 1))
        keys_own, keys_peer = ko_ref[:, cols], kp_ref[:, cols]
        values_own, values_peer = vo_ref[:, cols], vp_ref[:, cols]
        for start in range(0, rows, step):
            queries = q_ref[start : start + step, cols] * HEAD ** (-0.5)
            scores_own = dot_nt(keys_own, queries)
            scores_peer = dot_nt(keys_peer, queries)
            top = jnp.maximum(
                jnp.max(scores_own, axis=0, keepdims=True),
                jnp.max(scores_peer, axis=0, keepdims=True),
            )
            probs_own = jnp.exp(scores_own - top)
            probs_peer = jnp.exp(scores_peer - top)
            total = jnp.sum(probs_own, axis=0, keepdims=True) + jnp.sum(
                probs_peer, axis=0, keepdims=True
            )
            mixed = dot_tn(values_own, probs_own.astype(BF)) + dot_tn(
                values_peer, probs_peer.astype(BF)
            )
            mixed = mixed / total
            out_ref[start : start + step, cols] = mixed.T.astype(BF)
            lse_ref[0, h : h + 1, start : start + step] = top + jnp.log(total)


def attention(queries, kv_own, kv_peer):
    rows, width = queries.shape
    pairs = width // 128
    block = lambda offset: pl.BlockSpec((rows, 128), lambda h: (0, h + offset))
    return pl.pallas_call(
        attention_kernel,
        grid=(pairs,),
        in_specs=[block(0), block(0), block(0), block(pairs), block(pairs)],
        out_specs=[block(0), pl.BlockSpec((1, 2, rows), lambda h: (h, 0, 0))],
        out_shape=[
            jax.ShapeDtypeStruct((rows, width), BF),
            jax.ShapeDtypeStruct((pairs, 2, rows), F32),
        ],
        compiler_params=pltpu.CompilerParams(vmem_limit_bytes=40 * 2**20),
        cost_estimate=pl.CostEstimate(
            flops=8 * rows * rows * width,
            bytes_accessed=12 * rows * width,
            transcendentals=2 * rows * rows * width // HEAD,
        ),
        name="attention",
    )(queries, kv_own, kv_peer, kv_own, kv_peer)


def attention_back_kernel(
    q_ref, ko_ref, kp_ref, vo_ref, vp_ref, out_ref, gout_ref, lse_ref, gq_ref, go_ref, gp_ref
):
    rows = q_ref.shape[0]
    step = 256
    scale = HEAD ** (-0.5)
    for h in range(2):
        cols = slice(HEAD * h, HEAD * (h + 1))
        sides = ((ko_ref, vo_ref, go_ref), (kp_ref, vp_ref, gp_ref))
        grad_kv = [[None, None], [None, None]]
        for start in range(0, rows, step):
            span = slice(start, start + step)
            queries = q_ref[span, cols] * scale
            grad_out = gout_ref[span, cols]
            lse = lse_ref[0, h : h + 1, span]
            both = grad_out.astype(F32) * out_ref[span, cols].astype(F32)
            row_total = jnp.sum(both.T, axis=0, keepdims=True)
            grad_queries = None
            for side, (k_ref, v_ref, g_ref) in enumerate(sides):
                keys, values = k_ref[:, cols], v_ref[:, cols]
                probs = jnp.exp(dot_nt(keys, queries) - lse)
                grad_probs = dot_nt(values, grad_out)
                grad_scores = (probs * (grad_probs - row_total)).astype(BF)
                part = dot_tn(keys, grad_scores)
                grad_queries = part if grad_queries is None else grad_queries + part
                terms = (dot(grad_scores, queries), dot(probs.astype(BF), grad_out))
                for i in range(2):
                    old = grad_kv[side][i]
                    grad_kv[side][i] = terms[i] if old is None else old + terms[i]
            gq_ref[span, cols] = (grad_queries * scale).T.astype(BF)
        for side, (k_ref, v_ref, g_ref) in enumerate(sides):
            for i in range(2):
                g_ref[i, :, cols] = grad_kv[side][i].astype(g_ref.dtype)


def attention_back(queries, kv_own, kv_peer, mixed, grad_mixed, lse):
    rows, width = queries.shape
    pairs = width // 128
    block = lambda offset: pl.BlockSpec((rows, 128), lambda h: (0, h + offset))
    double = pl.BlockSpec((2, rows, 128), lambda h: (0, 0, h))
    return pl.pallas_call(
        attention_back_kernel,
        grid=(pairs,),
        in_specs=[
            block(0),
            block(0),
            block(0),
            block(pairs),
            block(pairs),
            block(0),
            block(0),
            pl.BlockSpec((1, 2, rows), lambda h: (h, 0, 0)),
        ],
        out_specs=[block(0), double, double],
        out_shape=[
            jax.ShapeDtypeStruct((rows, width), BF),
            jax.ShapeDtypeStruct((2, rows, width), F32),
            jax.ShapeDtypeStruct((2, rows, width), BF),
        ],
        compiler_params=pltpu.CompilerParams(vmem_limit_bytes=40 * 2**20),
        cost_estimate=pl.CostEstimate(
            flops=20 * rows * rows * width,
            bytes_accessed=24 * rows * width,
            transcendentals=2 * rows * rows * width // HEAD,
        ),
        name="attention_back",
    )(queries, kv_own, kv_peer, kv_own, kv_peer, mixed, grad_mixed, lse)


def norm_stats(activations):
    center = activations - jnp.mean(activations, axis=-1, keepdims=True)
    inverse = lax.rsqrt(jnp.mean(center * center, axis=-1, keepdims=True) + 1e-06)
    return (center * inverse, inverse)


def norm_back(grad_norm, normal, inverse):
    return inverse * (
        grad_norm
        - jnp.mean(grad_norm, axis=-1, keepdims=True)
        - normal * jnp.mean(grad_norm * normal, axis=-1, keepdims=True)
    )


def core_sum(partial_sum):
    low = partial_sum.astype(BF)
    return low.astype(F32) + swap(low, "core").astype(F32)


def gelu_and_slope(pre_act):
    linear = 2.0 * (2.0 / jnp.pi) ** 0.5
    cubic = 0.044715 * linear
    square = pre_act * pre_act
    gate = 1.0 / (1.0 + jnp.exp(-pre_act * (linear + cubic * square)))
    value = pre_act * gate
    slope = gate + value * (1.0 - gate) * (linear + 3.0 * cubic * square)
    return value.astype(BF), slope.astype(BF)


def attend(activations, activations_peer, modulation, weights, before=None, after=None):
    w_q, w_kv, w_out = weights
    shift_first, scale_first, gate_first = modulation[:3]
    normal_first, inverse_first = norm_stats(activations)
    entry = (normal_first * (1.0 + scale_first) + shift_first).astype(BF)
    kv_own = dot(entry, w_kv).astype(BF)
    queries = dot(entry, w_q).astype(BF)
    activations_peer, kv_own, queries = lax.optimization_barrier(
        (activations_peer, kv_own, queries)
    )
    entry_peer = norm_stats(activations_peer.astype(F32))[0] * (1.0 + scale_first) + shift_first
    entry_peer = entry_peer.astype(BF)
    kv_peer = dot(entry_peer, w_kv).astype(BF)
    if before:
        queries = before(queries)
    mixed, lse = attention(queries, kv_own, kv_peer)
    if after:
        mixed = after(mixed)
    branch = core_sum(dot(mixed, w_out))
    second = activations + gate_first * branch
    return (
        second,
        normal_first,
        inverse_first,
        entry,
        entry_peer,
        queries,
        kv_own,
        kv_peer,
        lse,
        mixed,
        branch,
    )


def feed_forward(attn_state, modulation, weights):
    w_fc1, w_fc2 = weights
    shift_second, scale_second, gate_second = modulation[3:]
    second, *kept = attn_state
    normal_second, inverse_second = norm_stats(second)
    mlp_input = (normal_second * (1.0 + scale_second) + shift_second).astype(BF)
    hidden, slope = gelu_and_slope(dot(mlp_input, w_fc1))
    branch_mlp = core_sum(dot(hidden, w_fc2))
    result = second + gate_second * branch_mlp
    state = (*kept, normal_second, inverse_second, mlp_input, slope, hidden, branch_mlp)
    return (result, state)


def layer_backward(grad_result, state, modulation, weights):
    w_q, w_kv, w_out, w_fc1, w_fc2 = weights
    shift_first, scale_first, gate_first, shift_second, scale_second, gate_second = modulation
    (
        normal_first,
        inverse_first,
        entry,
        unused,
        queries,
        kv_own,
        kv_peer,
        lse,
        mixed,
        branch,
        normal_second,
        inverse_second,
        mlp_input,
        slope,
        hidden,
        branch_mlp,
    ) = state
    rows = lambda value: jnp.sum(value, axis=0)
    grad_gate_second = rows(grad_result * branch_mlp)
    grad_branch_mlp = (grad_result * gate_second).astype(BF)
    grad_hidden = dot_nt(grad_branch_mlp, w_fc2)
    grad_pre = (grad_hidden * slope.astype(F32)).astype(BF)
    grad_mlp_input = core_sum(dot_nt(grad_pre, w_fc1))
    grad_fc2 = dot_tn(hidden, grad_branch_mlp).astype(BF)
    grad_fc1 = dot_tn(mlp_input, grad_pre).astype(BF)
    grad_scale_second = rows(grad_mlp_input * normal_second)
    grad_shift_second = rows(grad_mlp_input)
    grad_second = grad_result + norm_back(
        grad_mlp_input * (1.0 + scale_second), normal_second, inverse_second
    )
    grad_gate_first = rows(grad_second * branch)
    grad_branch = (grad_second * gate_first).astype(BF)
    grad_mixed = dot_nt(grad_branch, w_out).astype(BF)
    grad_out = dot_tn(mixed, grad_branch).astype(BF)
    grad_queries, grad_own, grad_peer = attention_back(
        queries, kv_own, kv_peer, mixed, grad_mixed, lse
    )
    grad_kv = (grad_own + swap(grad_peer, "xl").astype(F32)).astype(BF)
    grad_kv = jnp.concatenate([grad_kv[0], grad_kv[1]], axis=1)
    grad_entry = core_sum(dot_nt(grad_queries, w_q) + dot_nt(grad_kv, w_kv))
    grad_q_proj = dot_tn(entry, grad_queries).astype(BF)
    grad_kv_proj = dot_tn(entry, grad_kv).astype(BF)
    grad_scale_first = rows(grad_entry * normal_first)
    grad_shift_first = rows(grad_entry)
    grad_input = grad_second + norm_back(
        grad_entry * (1.0 + scale_first), normal_first, inverse_first
    )
    grad_modulation = jnp.stack(
        [
            grad_shift_first,
            grad_scale_first,
            grad_gate_first,
            grad_shift_second,
            grad_scale_second,
            grad_gate_second,
        ]
    )
    return (grad_input, grad_modulation, (grad_q_proj, grad_kv_proj, grad_out, grad_fc1, grad_fc2))


def sum_over_plane(block):
    x = lax.axis_index(RING_X)
    half, quarter = (x + 1) // 2 % 2, x // 2
    rows, columns = block.shape
    parts = block.astype(BF).reshape(2, rows // 2, columns)
    part = pick(parts, half).astype(F32) + swap(pick(parts, 1 - half), "xl").astype(F32)
    parts = part.astype(BF).reshape(2, rows // 4, columns)
    part = pick(parts, quarter).astype(F32) + swap_odd(pick(parts, 1 - quarter), RING_X).astype(F32)
    part = part.astype(BF)
    part = (part.astype(F32) + swap(part, "zh").astype(F32)).astype(BF)
    part = ordered(quarter == 0, part, swap_odd(part, RING_X))
    return ordered(half == 0, part, swap(part, "xl"))


def fill_fc_kernel(core_ref, mine_ref, other_ref, fc1_ref, fc2_ref):
    half = mine_ref.shape[1] // 2
    rows = fc1_ref.shape[0]
    first = core_ref[0] == 0
    mine, other = mine_ref[...].astype(F32), other_ref[...].astype(F32)
    for c, part in enumerate((jnp.where(first, mine, other), jnp.where(first, other, mine))):
        fc2_ref[half * c : half * (c + 1), :] = part[:half]
        for j in range(4):
            top = half + rows * (j // 2)
            left = half * (j % 2)
            to = half * (2 * j + c)
            fc1_ref[:, to : to + half] = part[top : top + rows, left : left + half]


def fill_attn_kernel(core_ref, mine_ref, other_ref, qkv_ref, out_ref):
    rows, width = out_ref.shape
    half = width // 2
    first = core_ref[0] == 0
    mine, other = mine_ref[...].astype(F32), other_ref[...].astype(F32)
    for c, part in enumerate((jnp.where(first, mine, other), jnp.where(first, other, mine))):
        at = half * c
        qkv_ref[:, at : at + half] = part[rows:, :half]
        qkv_ref[:, width + at : width + at + half] = part[:rows, :half]
        qkv_ref[:, 2 * width + at : 2 * width + at + half] = part[:rows, half:]
        out_ref[:, at : at + half] = part[rows:, half:]


def fill(kernel, core, total, shapes, name):
    whole = pl.BlockSpec(memory_space=pltpu.VMEM)
    return pl.pallas_call(
        kernel,
        in_specs=[pl.BlockSpec(memory_space=pltpu.SMEM), whole, whole],
        out_specs=[whole] * len(shapes),
        out_shape=[jax.ShapeDtypeStruct(shape, F32) for shape in shapes],
        compiler_params=pltpu.CompilerParams(vmem_limit_bytes=40 * 2**20),
        cost_estimate=pl.CostEstimate(flops=0, bytes_accessed=12 * total.size, transcendentals=0),
        name=name,
    )(core.astype(jnp.int32).reshape(1), total, swap(total, "core"))


def on_device(ends, cond, w_ada, b_ada, w_qkv, w_out, w_fc1, w_fc2):
    section = lax.axis_index("section")
    d = lax.axis_index("dp")
    zh, xh = lax.axis_index("zh"), lax.axis_index("xh")
    a = zh * 2 + xh
    core = lax.axis_index("core")
    width = w_out.shape[2]
    half = width // 2
    rows_d = w_out.shape[1]
    columns = lambda array, start: lax.dynamic_slice_in_dim(array, start, half, 1)

    cond_float = cond.astype(F32).reshape(4, width)
    cond_low = jax.nn.silu(cond_float).astype(BF)
    cond_rows = cond_low.reshape(4, 4, rows_d).transpose(1, 0, 2)
    cond_parts = [pick(cond_rows, d)] + [
        shift(pick(cond_rows, (d + s) % 4), "dp", s) for s in (1, 2, 3)
    ]
    piece_attn = jnp.concatenate(
        [columns(w_qkv[0], width * i + half * core) for i in range(3)]
        + [columns(w_out[0], half * core)],
        axis=1,
    )

    blocks = ends[0].reshape(2, 2, *ends.shape[3:])
    mine = lax.dynamic_index_in_dim(blocks, xh, 1, keepdims=False)
    theirs = lax.dynamic_index_in_dim(blocks, 1 - xh, 1, keepdims=False)
    theirs = swap_odd(theirs, RING_X)
    piece_attn, theirs, *cond_parts = join(piece_attn, theirs, *cond_parts)
    blocks = jnp.stack([mine, theirs], axis=1)
    mine = jnp.stack([pick(blocks, zh), swap(pick(blocks, 1 - zh), "zh")])
    mine = mine.reshape(-1, width)
    tokens_half = mine.shape[0]

    below, above = gather_near(piece_attn, "dp")

    latent_rows = jnp.stack([pick(part, a) for part in cond_parts])
    bias = lax.dynamic_update_slice(
        jnp.zeros((6 * width,), F32), b_ada[0].astype(F32), (d * b_ada.shape[1],)
    )
    part_mod = dot(latent_rows, w_ada[0]) + bias[None]
    part_mod, below, above, mine = join(part_mod, below, above, mine)
    mod_parts = [shift(part_mod[s : s + 1], "dp", -s) for s in (1, 2, 3)]
    attn_blocks = gather_far(piece_attn, below, above, "dp")
    other = swap(mine, "core")
    peer = swap(mine, "xl")
    piece_fc1 = jnp.concatenate(
        [columns(w_fc1[0], width * j + half * core) for j in range(4)], axis=1
    )
    piece_fc2 = rows_at(w_fc2[0], half * core, half)
    attn_blocks, mod_parts, other, peer, piece_fc1 = join(
        attn_blocks, mod_parts, other, peer, piece_fc1
    )
    near_fc1 = gather_near(piece_fc1, "dp")
    modulation = part_mod[0:1] + mod_parts[0] + mod_parts[1] + mod_parts[2]
    modulation = [modulation[:, width * i : width * (i + 1)] for i in range(6)]
    start = ordered(core == 0, mine, other)
    start_peer = ordered(core == 0, peer, swap(peer, "core"))
    full_attn = fill_rows(width, attn_blocks, d)
    out_rows = full_attn[:, 3 * half :].reshape(2, half, half)
    full_out = ordered(
        core == 0, pick(out_rows, core), swap(pick(out_rows, 1 - core), "core"), axis=1
    )
    def across(value, pairs, with_peer):
        part = rows_at(value.astype(BF), core * tokens_half, tokens_half)
        part = lax.ppermute(part, "section", pairs)
        own = ordered(core == 0, part, swap(part, "core"))
        if not with_peer:
            return own, None
        peer = swap(part, "xl")
        return own, ordered(core == 0, peer, swap(peer, "core"))

    attn_weights = (full_attn[:, :half], full_attn[:, half : 3 * half], full_out)
    fetched = {}

    def fetch_early(queries):
        queries, fetched["near"], fetched["piece"] = join(queries, near_fc1, piece_fc2)
        fetched["fc1"] = gather_far(piece_fc1, *fetched["near"], "dp")
        return queries

    def fetch_late(mixed):
        mixed, fetched["fc1"] = join(mixed, fetched["fc1"])
        fetched["near"] = gather_near(fetched["piece"], "dp")
        return mixed

    attn_state = attend(
        start.astype(F32), start_peer, modulation, attn_weights, fetch_early, fetch_late
    )
    second, near_fc2 = join(attn_state[0], fetched["near"])
    attn_state = (second, *attn_state[1:])
    full_fc1 = fill_rows(width, fetched["fc1"], d)
    full_fc2 = fill_rows(4 * half, gather_far(piece_fc2, *near_fc2, "dp"), d)
    fc_weights = (full_fc1, full_fc2)
    weights = attn_weights + fc_weights
    result, unused = feed_forward(attn_state, modulation, fc_weights)
    arrived, arrived_peer = across(result, [(0, 1)], True)
    second_input = jnp.where(section == 0, start, arrived).astype(F32)
    second_peer = jnp.where(section == 0, start_peer, arrived_peer)
    attn_state = attend(second_input, second_peer, modulation, attn_weights)
    result, state = feed_forward(attn_state, modulation, fc_weights)

    grad_input, unused, unused_too = layer_backward(start.astype(F32), state, modulation, weights)
    arrived, unused = across(grad_input, [(1, 0)], False)
    seed = jnp.where(section == 0, arrived, start).astype(F32)
    grad_input, grad_modulation, grads = layer_backward(seed, state, modulation, weights)
    grad_q, grad_kv, grad_out, grad_fc1, grad_fc2 = grads

    def block_fc(i):
        one = rows_at(grad_fc1, i * rows_d, rows_d)
        return jnp.concatenate([rows_at(grad_fc2, i * half, half), one[:, :width], one[:, width:]])

    sum_fc = sum_over_plane(scatter_ring(block_fc, "dp", d, grad_q))
    out_fc1, out_fc2 = fill(
        fill_fc_kernel, core, sum_fc, ((rows_d, 8 * half), (2 * half, width)), "fill_fc"
    )
    out_own = ordered(
        core == 0,
        columns(grad_out, half * core),
        swap(columns(grad_out, half - half * core), "core"),
    )

    def block_attn(i):
        kv, q, out = (rows_at(g, i * rows_d, rows_d) for g in (grad_kv, grad_q, out_own))
        return jnp.concatenate([kv, jnp.concatenate([q, out], axis=1)])

    sum_attn = sum_over_plane(scatter_ring(block_attn, "dp", d, grad_input))
    out_qkv, out_out = fill(
        fill_attn_kernel, core, sum_attn, ((rows_d, 6 * half), (rows_d, width)), "fill_attn"
    )

    grad_mod = grad_modulation.reshape(1, 6 * width)
    grad_mod = grad_mod + swap(grad_mod, "xl")
    plane_mod = ordered(xh == 0, grad_mod, swap(grad_mod, "xh"))
    plane_mod = ordered(zh == 0, plane_mod, swap(plane_mod, "zh"))
    all_mod = gather_small(plane_mod, "dp", d)
    all_cond = jnp.zeros((4, 4, rows_d), BF)
    for s in range(4):
        all_cond = lax.dynamic_update_index_in_dim(all_cond, cond_parts[s], (d + 4 - s) % 4, 0)
    all_cond = all_cond.reshape(16, rows_d)
    out_ada = lax.dot_general(
        all_cond.astype(F32), all_mod, (((0,), (0,)), ((), ())), precision=lax.Precision.HIGHEST
    )
    out_bias = jnp.sum(
        lax.dynamic_slice_in_dim(all_mod, d * b_ada.shape[1], b_ada.shape[1], 1), axis=0
    )
    grad_silu = lax.dot_general(
        all_mod,
        w_ada[0].astype(F32),
        (((1,), (1,)), ((), ())),
        precision=lax.Precision.HIGHEST,
    ).reshape(2, 2, 4, rows_d)
    same = jnp.stack([pick(grad_silu, d // 2), swap_odd(pick(grad_silu, 1 - d // 2), "dp")], axis=1)
    got = swap_even(pick(same, 1 - d % 2), "dp")
    same = pick(same, d % 2)
    silu_full = jnp.zeros((4, 4, rows_d), F32)
    beside = d + 1 - 2 * (d % 2)
    for part, place in ((same[0], d), (same[1], 3 - d), (got[0], beside), (got[1], 3 - beside)):
        silu_full = lax.dynamic_update_index_in_dim(silu_full, part, place, 0)
    silu_full = silu_full.transpose(1, 0, 2).reshape(4, width)
    silu_full = silu_full + swap(silu_full, "section")
    unused, silu_pull = jax.vjp(jax.nn.silu, cond_float)
    out_cond = silu_pull(silu_full)[0].reshape(cond.shape)

    edge = jnp.where(section == 0, grad_input, result)
    edge = rows_at(edge, core * tokens_half, tokens_half).reshape(2, 2, -1, width)
    edge = ordered(zh == 0, edge[:1], swap(edge[1:].astype(BF), "zh").astype(F32))
    boundary = ordered(
        xh == 0, edge[:, :1], swap_odd(edge[:, 1:].astype(BF), RING_X).astype(F32), axis=1
    ).reshape(ends.shape)

    return (
        boundary,
        out_cond,
        out_ada[None],
        out_bias[None],
        out_qkv[None],
        out_out[None],
        out_fc1[None],
        out_fc2[None],
    )


def solution(mesh):
    finer = Mesh(
        mesh.devices.reshape(2, 4, 2, 2, 2, 2), ("section", "dp", "zh", "xh", "xl", "core")
    )
    ends_spec = P("section", None, "dp", CTX, None)
    cond_spec = P(None, "dp", None)
    matrix = P("section", "dp", None)
    vector = P("section", "dp")
    return jax.shard_map(
        on_device,
        mesh=finer,
        in_specs=(ends_spec, cond_spec, matrix, vector, matrix, matrix, matrix, matrix),
        out_specs=(ends_spec, cond_spec, matrix, vector, matrix, matrix, matrix, matrix),
        check_vma=False,
    )
```

```python
import jax
import jax.numpy as jnp
from jax import lax
from jax.experimental import pallas as pl
from jax.experimental.pallas import tpu as pltpu
from jax.sharding import Mesh
from jax.sharding import PartitionSpec as P

HEAD = 64
BF = jnp.bfloat16
F32 = jnp.float32
RING_X = ("xh", "xl")
CTX = ("zh", "xh", "xl", "core")


def shift(array, axis, by, size=4):
    return lax.ppermute(array, axis, [(i, (i + by) % size) for i in range(size)])


def swap(array, axis):
    return lax.ppermute(array, axis, [(0, 1), (1, 0)])


def swap_odd(array, axis):
    return lax.ppermute(array, axis, [(0, 3), (1, 2), (2, 1), (3, 0)])


def swap_even(array, axis):
    return lax.ppermute(array, axis, [(0, 1), (1, 0), (2, 3), (3, 2)])


def pick(blocks, index):
    return lax.dynamic_index_in_dim(blocks, index, 0, keepdims=False)


def rows_at(array, start, size):
    return lax.dynamic_slice_in_dim(array, start, size, 0)


def ordered(first, mine, other, axis=0):
    return jnp.where(
        first,
        jnp.concatenate([mine, other], axis=axis),
        jnp.concatenate([other, mine], axis=axis),
    )


def gather_small(piece, axis, index):
    two = ordered(index % 2 == 0, piece, swap_even(piece, axis))
    return ordered(index < 2, two, swap_odd(two, axis))


def gather_near(piece, axis):
    return shift(piece, axis, 1), shift(piece, axis, -1)


def gather_far(piece, below, above, axis):
    half = piece.shape[0] // 2
    far_low = shift(below[:half], axis, 1)
    far_high = shift(above[half:], axis, -1)
    return [(piece,), (above,), (far_low, far_high), (below,)]


def fill_rows(size, blocks, index):
    total = jnp.zeros((size, blocks[0][0].shape[1]), BF)
    for s, pieces in enumerate(blocks):
        at = (index + s) % 4 * (size // 4)
        for piece in pieces:
            total = lax.dynamic_update_slice(total, piece, (at, 0))
            at = at + piece.shape[0]
    return total


def join(*values):
    return lax.optimization_barrier(values)


def scatter_ring(block, axis, index, after):
    add = lambda one, two: (one.astype(F32) + two.astype(F32)).astype(BF)
    far = block((index + 2) % 4)
    half = far.shape[0] // 2
    from_below = shift(far[:half], axis, 1)
    from_above = shift(far[half:], axis, -1)
    from_below, from_above, after = join(from_below, from_above, after)
    up = block((index + 1) % 4)
    up = jnp.concatenate([add(up[:half], from_below), up[half:]])
    down = block((index + 3) % 4)
    down = jnp.concatenate([down[:half], add(down[half:], from_above)])
    got_up = shift(up, axis, 1)
    got_down = shift(down, axis, -1)
    return block(index).astype(F32) + got_up.astype(F32) + got_down.astype(F32)


def dot(left, right):
    return jnp.dot(left, right, preferred_element_type=F32)


def dot_nt(left, right):
    return lax.dot_general(left, right, (((1,), (1,)), ((), ())), preferred_element_type=F32)


def dot_tn(left, right):
    return lax.dot_general(left, right, (((0,), (0,)), ((), ())), preferred_element_type=F32)


def attention_kernel(q_ref, ko_ref, kp_ref, vo_ref, vp_ref, out_ref, lse_ref):
    rows = q_ref.shape[0]
    step = 256
    for h in range(2):
        cols = slice(HEAD * h, HEAD * (h + 1))
        keys_own, keys_peer = ko_ref[:, cols], kp_ref[:, cols]
        values_own, values_peer = vo_ref[:, cols], vp_ref[:, cols]
        for start in range(0, rows, step):
            queries = q_ref[start : start + step, cols] * HEAD ** (-0.5)
            scores_own = dot_nt(keys_own, queries)
            scores_peer = dot_nt(keys_peer, queries)
            top = jnp.maximum(
                jnp.max(scores_own, axis=0, keepdims=True),
                jnp.max(scores_peer, axis=0, keepdims=True),
            )
            probs_own = jnp.exp(scores_own - top)
            probs_peer = jnp.exp(scores_peer - top)
            total = jnp.sum(probs_own, axis=0, keepdims=True) + jnp.sum(
                probs_peer, axis=0, keepdims=True
            )
            mixed = dot_tn(values_own, probs_own.astype(BF)) + dot_tn(
                values_peer, probs_peer.astype(BF)
            )
            mixed = mixed / total
            out_ref[start : start + step, cols] = mixed.T.astype(BF)
            lse_ref[0, h : h + 1, start : start + step] = top + jnp.log(total)


def attention(queries, kv_own, kv_peer):
    rows, width = queries.shape
    pairs = width // 128
    block = lambda offset: pl.BlockSpec((rows, 128), lambda h: (0, h + offset))
    return pl.pallas_call(
        attention_kernel,
        grid=(pairs,),
        in_specs=[block(0), block(0), block(0), block(pairs), block(pairs)],
        out_specs=[block(0), pl.BlockSpec((1, 2, rows), lambda h: (h, 0, 0))],
        out_shape=[
            jax.ShapeDtypeStruct((rows, width), BF),
            jax.ShapeDtypeStruct((pairs, 2, rows), F32),
        ],
        compiler_params=pltpu.CompilerParams(vmem_limit_bytes=40 * 2**20),
        cost_estimate=pl.CostEstimate(
            flops=8 * rows * rows * width,
            bytes_accessed=12 * rows * width,
            transcendentals=2 * rows * rows * width // HEAD,
        ),
        name="attention",
    )(queries, kv_own, kv_peer, kv_own, kv_peer)


def attention_back_kernel(
    q_ref, ko_ref, kp_ref, vo_ref, vp_ref, out_ref, gout_ref, lse_ref, gq_ref, go_ref, gp_ref
):
    rows = q_ref.shape[0]
    step = 256
    scale = HEAD ** (-0.5)
    for h in range(2):
        cols = slice(HEAD * h, HEAD * (h + 1))
        sides = ((ko_ref, vo_ref, go_ref), (kp_ref, vp_ref, gp_ref))
        grad_kv = [[None, None], [None, None]]
        for start in range(0, rows, step):
            span = slice(start, start + step)
            queries = q_ref[span, cols] * scale
            grad_out = gout_ref[span, cols]
            lse = lse_ref[0, h : h + 1, span]
            both = grad_out.astype(F32) * out_ref[span, cols].astype(F32)
            row_total = jnp.sum(both.T, axis=0, keepdims=True)
            grad_queries = None
            for side, (k_ref, v_ref, g_ref) in enumerate(sides):
                keys, values = k_ref[:, cols], v_ref[:, cols]
                probs = jnp.exp(dot_nt(keys, queries) - lse)
                grad_probs = dot_nt(values, grad_out)
                grad_scores = (probs * (grad_probs - row_total)).astype(BF)
                part = dot_tn(keys, grad_scores)
                grad_queries = part if grad_queries is None else grad_queries + part
                terms = (dot(grad_scores, queries), dot(probs.astype(BF), grad_out))
                for i in range(2):
                    old = grad_kv[side][i]
                    grad_kv[side][i] = terms[i] if old is None else old + terms[i]
            gq_ref[span, cols] = (grad_queries * scale).T.astype(BF)
        for side, (k_ref, v_ref, g_ref) in enumerate(sides):
            for i in range(2):
                g_ref[i, :, cols] = grad_kv[side][i].astype(g_ref.dtype)


def attention_back(queries, kv_own, kv_peer, mixed, grad_mixed, lse):
    rows, width = queries.shape
    pairs = width // 128
    block = lambda offset: pl.BlockSpec((rows, 128), lambda h: (0, h + offset))
    double = pl.BlockSpec((2, rows, 128), lambda h: (0, 0, h))
    return pl.pallas_call(
        attention_back_kernel,
        grid=(pairs,),
        in_specs=[
            block(0),
            block(0),
            block(0),
            block(pairs),
            block(pairs),
            block(0),
            block(0),
            pl.BlockSpec((1, 2, rows), lambda h: (h, 0, 0)),
        ],
        out_specs=[block(0), double, double],
        out_shape=[
            jax.ShapeDtypeStruct((rows, width), BF),
            jax.ShapeDtypeStruct((2, rows, width), F32),
            jax.ShapeDtypeStruct((2, rows, width), BF),
        ],
        compiler_params=pltpu.CompilerParams(vmem_limit_bytes=40 * 2**20),
        cost_estimate=pl.CostEstimate(
            flops=20 * rows * rows * width,
            bytes_accessed=24 * rows * width,
            transcendentals=2 * rows * rows * width // HEAD,
        ),
        name="attention_back",
    )(queries, kv_own, kv_peer, kv_own, kv_peer, mixed, grad_mixed, lse)


def norm_stats(activations):
    center = activations - jnp.mean(activations, axis=-1, keepdims=True)
    inverse = lax.rsqrt(jnp.mean(center * center, axis=-1, keepdims=True) + 1e-06)
    return (center * inverse, inverse)


def norm_back(grad_norm, normal, inverse):
    return inverse * (
        grad_norm
        - jnp.mean(grad_norm, axis=-1, keepdims=True)
        - normal * jnp.mean(grad_norm * normal, axis=-1, keepdims=True)
    )


def core_sum(partial_sum):
    low = partial_sum.astype(BF)
    return low.astype(F32) + swap(low, "core").astype(F32)


def gelu_and_slope(pre_act):
    linear = 2.0 * (2.0 / jnp.pi) ** 0.5
    cubic = 0.044715 * linear
    square = pre_act * pre_act
    gate = 1.0 / (1.0 + jnp.exp(-pre_act * (linear + cubic * square)))
    value = pre_act * gate
    slope = gate + value * (1.0 - gate) * (linear + 3.0 * cubic * square)
    return value.astype(BF), slope.astype(BF)


def attend(activations, activations_peer, modulation, weights, before=None, after=None):
    w_q, w_kv, w_out = weights
    shift_first, scale_first, gate_first = modulation[:3]
    normal_first, inverse_first = norm_stats(activations)
    entry = (normal_first * (1.0 + scale_first) + shift_first).astype(BF)
    kv_own = dot(entry, w_kv).astype(BF)
    queries = dot(entry, w_q).astype(BF)
    activations_peer, kv_own, queries = lax.optimization_barrier(
        (activations_peer, kv_own, queries)
    )
    entry_peer = norm_stats(activations_peer.astype(F32))[0] * (1.0 + scale_first) + shift_first
    entry_peer = entry_peer.astype(BF)
    kv_peer = dot(entry_peer, w_kv).astype(BF)
    if before:
        queries = before(queries)
    mixed, lse = attention(queries, kv_own, kv_peer)
    if after:
        mixed = after(mixed)
    branch = core_sum(dot(mixed, w_out))
    second = activations + gate_first * branch
    return (
        second,
        normal_first,
        inverse_first,
        entry,
        entry_peer,
        queries,
        kv_own,
        kv_peer,
        lse,
        mixed,
        branch,
    )


def feed_forward(attn_state, modulation, weights):
    w_fc1, w_fc2 = weights
    shift_second, scale_second, gate_second = modulation[3:]
    second, *kept = attn_state
    normal_second, inverse_second = norm_stats(second)
    mlp_input = (normal_second * (1.0 + scale_second) + shift_second).astype(BF)
    hidden, slope = gelu_and_slope(dot(mlp_input, w_fc1))
    branch_mlp = core_sum(dot(hidden, w_fc2))
    result = second + gate_second * branch_mlp
    state = (*kept, normal_second, inverse_second, mlp_input, slope, hidden, branch_mlp)
    return (result, state)


def layer_backward(grad_result, state, modulation, weights, core=None):
    w_q, w_kv, w_out, w_fc1, w_fc2 = weights
    shift_first, scale_first, gate_first, shift_second, scale_second, gate_second = modulation
    (
        normal_first,
        inverse_first,
        entry,
        unused,
        queries,
        kv_own,
        kv_peer,
        lse,
        mixed,
        branch,
        normal_second,
        inverse_second,
        mlp_input,
        slope,
        hidden,
        branch_mlp,
    ) = state
    rows = lambda value: jnp.sum(value, axis=0)
    grad_gate_second = rows(grad_result * branch_mlp)
    grad_branch_mlp = (grad_result * gate_second).astype(BF)
    grad_hidden = dot_nt(grad_branch_mlp, w_fc2)
    grad_pre = (grad_hidden * slope.astype(F32)).astype(BF)
    grad_mlp_input = core_sum(dot_nt(grad_pre, w_fc1))
    grad_fc2 = dot_tn(hidden, grad_branch_mlp).astype(BF)
    grad_fc1 = dot_tn(mlp_input, grad_pre).astype(BF)
    grad_scale_second = rows(grad_mlp_input * normal_second)
    grad_shift_second = rows(grad_mlp_input)
    grad_second = grad_result + norm_back(
        grad_mlp_input * (1.0 + scale_second), normal_second, inverse_second
    )
    grad_gate_first = rows(grad_second * branch)
    grad_branch = (grad_second * gate_first).astype(BF)
    grad_mixed = dot_nt(grad_branch, w_out).astype(BF)
    grad_out = dot_tn(mixed, grad_branch).astype(BF)
    grad_queries, grad_own, grad_peer = attention_back(
        queries, kv_own, kv_peer, mixed, grad_mixed, lse
    )
    if core is not None:
        tokens, half = mixed.shape
        w_k, w_v = w_kv[:, :half], w_kv[:, half:]
        far = (dot_nt(grad_peer[0], w_k) + dot_nt(grad_peer[1], w_v)).astype(BF)
        kept = rows_at(far, core * (tokens // 2), tokens // 2).astype(F32)
        given = rows_at(far, (1 - core) * (tokens // 2), tokens // 2)
        far = swap((kept + swap(given, "core").astype(F32)).astype(BF), "xl")
        grad_own = grad_own.astype(BF)
        near = core_sum(
            dot_nt(grad_queries, w_q) + dot_nt(grad_own[0], w_k) + dot_nt(grad_own[1], w_v)
        )
        near, far = join(near, far)
        grad_entry = near + ordered(core == 0, far, swap(far, "core")).astype(F32)
        return grad_second + norm_back(
            grad_entry * (1.0 + scale_first), normal_first, inverse_first
        )
    grad_kv = (grad_own + swap(grad_peer, "xl").astype(F32)).astype(BF)
    grad_kv = jnp.concatenate([grad_kv[0], grad_kv[1]], axis=1)
    grad_entry = core_sum(dot_nt(grad_queries, w_q) + dot_nt(grad_kv, w_kv))
    grad_q_proj = dot_tn(entry, grad_queries).astype(BF)
    grad_kv_proj = dot_tn(entry, grad_kv).astype(BF)
    grad_scale_first = rows(grad_entry * normal_first)
    grad_shift_first = rows(grad_entry)
    grad_input = grad_second + norm_back(
        grad_entry * (1.0 + scale_first), normal_first, inverse_first
    )
    grad_modulation = jnp.stack(
        [
            grad_shift_first,
            grad_scale_first,
            grad_gate_first,
            grad_shift_second,
            grad_scale_second,
            grad_gate_second,
        ]
    )
    return (grad_input, grad_modulation, (grad_q_proj, grad_kv_proj, grad_out, grad_fc1, grad_fc2))


def sum_over_plane(block):
    x = lax.axis_index(RING_X)
    half, quarter = (x + 1) // 2 % 2, x // 2
    rows, columns = block.shape
    parts = block.astype(BF).reshape(2, rows // 2, columns)
    part = pick(parts, half).astype(F32) + swap(pick(parts, 1 - half), "xl").astype(F32)
    parts = part.astype(BF).reshape(2, rows // 4, columns)
    part = pick(parts, quarter).astype(F32) + swap_odd(pick(parts, 1 - quarter), RING_X).astype(F32)
    part = part.astype(BF)
    part = (part.astype(F32) + swap(part, "zh").astype(F32)).astype(BF)
    part = ordered(quarter == 0, part, swap_odd(part, RING_X))
    return ordered(half == 0, part, swap(part, "xl"))


def fill_fc_kernel(core_ref, mine_ref, other_ref, fc1_ref, fc2_ref):
    half = mine_ref.shape[1] // 2
    rows = fc1_ref.shape[0]
    first = core_ref[0] == 0
    mine, other = mine_ref[...].astype(F32), other_ref[...].astype(F32)
    for c, part in enumerate((jnp.where(first, mine, other), jnp.where(first, other, mine))):
        fc2_ref[half * c : half * (c + 1), :] = part[:half]
        for j in range(4):
            top = half + rows * (j // 2)
            left = half * (j % 2)
            to = half * (2 * j + c)
            fc1_ref[:, to : to + half] = part[top : top + rows, left : left + half]


def fill_attn_kernel(core_ref, mine_ref, other_ref, qkv_ref, out_ref):
    rows, width = out_ref.shape
    half = width // 2
    first = core_ref[0] == 0
    mine, other = mine_ref[...].astype(F32), other_ref[...].astype(F32)
    for c, part in enumerate((jnp.where(first, mine, other), jnp.where(first, other, mine))):
        at = half * c
        qkv_ref[:, at : at + half] = part[rows:, :half]
        qkv_ref[:, width + at : width + at + half] = part[:rows, :half]
        qkv_ref[:, 2 * width + at : 2 * width + at + half] = part[:rows, half:]
        out_ref[:, at : at + half] = part[rows:, half:]


def fill(kernel, core, total, shapes, name):
    whole = pl.BlockSpec(memory_space=pltpu.VMEM)
    return pl.pallas_call(
        kernel,
        in_specs=[pl.BlockSpec(memory_space=pltpu.SMEM), whole, whole],
        out_specs=[whole] * len(shapes),
        out_shape=[jax.ShapeDtypeStruct(shape, F32) for shape in shapes],
        compiler_params=pltpu.CompilerParams(vmem_limit_bytes=40 * 2**20),
        cost_estimate=pl.CostEstimate(flops=0, bytes_accessed=12 * total.size, transcendentals=0),
        name=name,
    )(core.astype(jnp.int32).reshape(1), total, swap(total, "core"))


def on_device(ends, cond, w_ada, b_ada, w_qkv, w_out, w_fc1, w_fc2):
    section = lax.axis_index("section")
    d = lax.axis_index("dp")
    zh, xh = lax.axis_index("zh"), lax.axis_index("xh")
    a = zh * 2 + xh
    core = lax.axis_index("core")
    width = w_out.shape[2]
    half = width // 2
    rows_d = w_out.shape[1]
    columns = lambda array, start: lax.dynamic_slice_in_dim(array, start, half, 1)

    cond_float = cond.astype(F32).reshape(4, width)
    cond_low = jax.nn.silu(cond_float).astype(BF)
    cond_rows = cond_low.reshape(4, 4, rows_d).transpose(1, 0, 2)
    cond_parts = [pick(cond_rows, d)] + [
        shift(pick(cond_rows, (d + s) % 4), "dp", s) for s in (1, 2, 3)
    ]
    piece_attn = jnp.concatenate(
        [columns(w_qkv[0], width * i + half * core) for i in range(3)]
        + [columns(w_out[0], half * core)],
        axis=1,
    )

    blocks = ends[0].reshape(2, 2, *ends.shape[3:])
    mine = lax.dynamic_index_in_dim(blocks, xh, 1, keepdims=False)
    theirs = lax.dynamic_index_in_dim(blocks, 1 - xh, 1, keepdims=False)
    theirs = swap_odd(theirs, RING_X)
    piece_attn, theirs, *cond_parts = join(piece_attn, theirs, *cond_parts)
    blocks = jnp.stack([mine, theirs], axis=1)
    mine = jnp.stack([pick(blocks, zh), swap(pick(blocks, 1 - zh), "zh")])
    mine = mine.reshape(-1, width)
    tokens_half = mine.shape[0]

    below, above = gather_near(piece_attn, "dp")

    latent_rows = jnp.stack([pick(part, a) for part in cond_parts])
    bias = lax.dynamic_update_slice(
        jnp.zeros((6 * width,), F32), b_ada[0].astype(F32), (d * b_ada.shape[1],)
    )
    part_mod = dot(latent_rows, w_ada[0]) + bias[None]
    part_mod, below, above, mine = join(part_mod, below, above, mine)
    mod_parts = [shift(part_mod[s : s + 1], "dp", -s) for s in (1, 2, 3)]
    attn_blocks = gather_far(piece_attn, below, above, "dp")
    other = swap(mine, "core")
    peer = swap(mine, "xl")
    piece_fc1 = jnp.concatenate(
        [columns(w_fc1[0], width * j + half * core) for j in range(4)], axis=1
    )
    piece_fc2 = rows_at(w_fc2[0], half * core, half)
    attn_blocks, piece_fc1 = join(attn_blocks, piece_fc1)
    near_fc1 = gather_near(piece_fc1, "dp")
    modulation = part_mod[0:1] + mod_parts[0] + mod_parts[1] + mod_parts[2]
    modulation = [modulation[:, width * i : width * (i + 1)] for i in range(6)]
    start = ordered(core == 0, mine, other)
    start_peer = ordered(core == 0, peer, swap(peer, "core"))
    full_attn = fill_rows(width, attn_blocks, d)
    out_rows = full_attn[:, 3 * half :].reshape(2, half, half)
    full_out = ordered(
        core == 0, pick(out_rows, core), swap(pick(out_rows, 1 - core), "core"), axis=1
    )
    def across(value, pairs, with_peer):
        part = rows_at(value.astype(BF), core * tokens_half, tokens_half)
        part = lax.ppermute(part, "section", pairs)
        own = ordered(core == 0, part, swap(part, "core"))
        if not with_peer:
            return own, None
        peer = swap(part, "xl")
        return own, ordered(core == 0, peer, swap(peer, "core"))

    attn_weights = (full_attn[:, :half], full_attn[:, half : 3 * half], full_out)
    fetched = {}

    def fetch_early(queries):
        queries, fetched["near"], fetched["piece"] = join(queries, near_fc1, piece_fc2)
        fetched["fc1"] = gather_far(piece_fc1, *fetched["near"], "dp")
        return queries

    def fetch_late(mixed):
        mixed, fetched["fc1"] = join(mixed, fetched["fc1"])
        fetched["near"] = gather_near(fetched["piece"], "dp")
        return mixed

    attn_state = attend(
        start.astype(F32), start_peer, modulation, attn_weights, fetch_early, fetch_late
    )
    second, near_fc2 = join(attn_state[0], fetched["near"])
    attn_state = (second, *attn_state[1:])
    full_fc1 = fill_rows(width, fetched["fc1"], d)
    full_fc2 = fill_rows(4 * half, gather_far(piece_fc2, *near_fc2, "dp"), d)
    fc_weights = (full_fc1, full_fc2)
    weights = attn_weights + fc_weights
    result, unused = feed_forward(attn_state, modulation, fc_weights)
    arrived, arrived_peer = across(result, [(0, 1)], True)
    second_input = jnp.where(section == 0, start, arrived).astype(F32)
    second_peer = jnp.where(section == 0, start_peer, arrived_peer)
    attn_state = attend(second_input, second_peer, modulation, attn_weights)
    result, state = feed_forward(attn_state, modulation, fc_weights)

    grad_input = layer_backward(start.astype(F32), state, modulation, weights, core)
    arrived, unused = across(grad_input, [(1, 0)], False)
    seed = jnp.where(section == 0, arrived, start).astype(F32)
    grad_input, grad_modulation, grads = layer_backward(seed, state, modulation, weights)
    grad_q, grad_kv, grad_out, grad_fc1, grad_fc2 = grads

    def block_fc(i):
        one = rows_at(grad_fc1, i * rows_d, rows_d)
        return jnp.concatenate([rows_at(grad_fc2, i * half, half), one[:, :width], one[:, width:]])

    sum_fc = sum_over_plane(scatter_ring(block_fc, "dp", d, grad_q))
    out_fc1, out_fc2 = fill(
        fill_fc_kernel, core, sum_fc, ((rows_d, 8 * half), (2 * half, width)), "fill_fc"
    )
    out_own = ordered(
        core == 0,
        columns(grad_out, half * core),
        swap(columns(grad_out, half - half * core), "core"),
    )

    def block_attn(i):
        kv, q, out = (rows_at(g, i * rows_d, rows_d) for g in (grad_kv, grad_q, out_own))
        return jnp.concatenate([kv, jnp.concatenate([q, out], axis=1)])

    sum_attn = sum_over_plane(scatter_ring(block_attn, "dp", d, grad_input))
    out_qkv, out_out = fill(
        fill_attn_kernel, core, sum_attn, ((rows_d, 6 * half), (rows_d, width)), "fill_attn"
    )

    grad_mod = grad_modulation.reshape(1, 6 * width)
    grad_mod = grad_mod + swap(grad_mod, "xl")
    plane_mod = ordered(xh == 0, grad_mod, swap(grad_mod, "xh"))
    plane_mod = ordered(zh == 0, plane_mod, swap(plane_mod, "zh"))
    all_mod = gather_small(plane_mod, "dp", d)
    all_cond = jnp.zeros((4, 4, rows_d), BF)
    for s in range(4):
        all_cond = lax.dynamic_update_index_in_dim(all_cond, cond_parts[s], (d + 4 - s) % 4, 0)
    all_cond = all_cond.reshape(16, rows_d)
    out_ada = lax.dot_general(
        all_cond.astype(F32), all_mod, (((0,), (0,)), ((), ())), precision=lax.Precision.HIGHEST
    )
    out_bias = jnp.sum(
        lax.dynamic_slice_in_dim(all_mod, d * b_ada.shape[1], b_ada.shape[1], 1), axis=0
    )
    grad_silu = lax.dot_general(
        all_mod,
        w_ada[0].astype(F32),
        (((1,), (1,)), ((), ())),
        precision=lax.Precision.HIGHEST,
    ).reshape(2, 2, 4, rows_d)
    same = jnp.stack([pick(grad_silu, d // 2), swap_odd(pick(grad_silu, 1 - d // 2), "dp")], axis=1)
    got = swap_even(pick(same, 1 - d % 2), "dp")
    same = pick(same, d % 2)
    silu_full = jnp.zeros((4, 4, rows_d), F32)
    beside = d + 1 - 2 * (d % 2)
    for part, place in ((same[0], d), (same[1], 3 - d), (got[0], beside), (got[1], 3 - beside)):
        silu_full = lax.dynamic_update_index_in_dim(silu_full, part, place, 0)
    silu_full = silu_full.transpose(1, 0, 2).reshape(4, width)
    silu_full = silu_full + swap(silu_full, "section")
    unused, silu_pull = jax.vjp(jax.nn.silu, cond_float)
    out_cond = silu_pull(silu_full)[0].reshape(cond.shape)

    edge = jnp.where(section == 0, grad_input, result)
    edge = rows_at(edge, core * tokens_half, tokens_half).reshape(2, 2, -1, width)
    edge = ordered(zh == 0, edge[:1], swap(edge[1:].astype(BF), "zh").astype(F32))
    boundary = ordered(
        xh == 0, edge[:, :1], swap_odd(edge[:, 1:].astype(BF), RING_X).astype(F32), axis=1
    ).reshape(ends.shape)

    return (
        boundary,
        out_cond,
        out_ada[None],
        out_bias[None],
        out_qkv[None],
        out_out[None],
        out_fc1[None],
        out_fc2[None],
    )


def solution(mesh):
    finer = Mesh(
        mesh.devices.reshape(2, 4, 2, 2, 2, 2), ("section", "dp", "zh", "xh", "xl", "core")
    )
    ends_spec = P("section", None, "dp", CTX, None)
    cond_spec = P(None, "dp", None)
    matrix = P("section", "dp", None)
    vector = P("section", "dp")
    return jax.shard_map(
        on_device,
        mesh=finer,
        in_specs=(ends_spec, cond_spec, matrix, vector, matrix, matrix, matrix, matrix),
        out_specs=(ends_spec, cond_spec, matrix, vector, matrix, matrix, matrix, matrix),
        check_vma=False,
    )
```

```python
import jax
import jax.numpy as jnp
from jax import lax
from jax.experimental import pallas as pl
from jax.experimental.pallas import tpu as pltpu
from jax.sharding import Mesh
from jax.sharding import PartitionSpec as P

HEAD = 64
BF = jnp.bfloat16
F32 = jnp.float32
RING_X = ("xh", "xl")
CTX = ("zh", "xh", "xl", "core")


def shift(array, axis, by, size=4):
    return lax.ppermute(array, axis, [(i, (i + by) % size) for i in range(size)])


def swap(array, axis):
    return lax.ppermute(array, axis, [(0, 1), (1, 0)])


def swap_odd(array, axis):
    return lax.ppermute(array, axis, [(0, 3), (1, 2), (2, 1), (3, 0)])


def swap_even(array, axis):
    return lax.ppermute(array, axis, [(0, 1), (1, 0), (2, 3), (3, 2)])


def pick(blocks, index):
    return lax.dynamic_index_in_dim(blocks, index, 0, keepdims=False)


def rows_at(array, start, size):
    return lax.dynamic_slice_in_dim(array, start, size, 0)


def ordered(first, mine, other, axis=0):
    return jnp.where(
        first,
        jnp.concatenate([mine, other], axis=axis),
        jnp.concatenate([other, mine], axis=axis),
    )


def gather_small(piece, axis, index):
    two = ordered(index % 2 == 0, piece, swap_even(piece, axis))
    return ordered(index < 2, two, swap_odd(two, axis))


def gather_near(piece, axis):
    return shift(piece, axis, 1), shift(piece, axis, -1)


def gather_far(piece, below, above, axis):
    half = piece.shape[0] // 2
    far_low = shift(below[:half], axis, 1)
    far_high = shift(above[half:], axis, -1)
    return [(piece,), (above,), (far_low, far_high), (below,)]


def fill_rows(size, blocks, index):
    total = jnp.zeros((size, blocks[0][0].shape[1]), BF)
    for s, pieces in enumerate(blocks):
        at = (index + s) % 4 * (size // 4)
        for piece in pieces:
            total = lax.dynamic_update_slice(total, piece, (at, 0))
            at = at + piece.shape[0]
    return total


def join(*values):
    return lax.optimization_barrier(values)


def scatter_ring(block, axis, index, after):
    add = lambda one, two: (one.astype(F32) + two.astype(F32)).astype(BF)
    far = block((index + 2) % 4)
    half = far.shape[0] // 2
    from_below = shift(far[:half], axis, 1)
    from_above = shift(far[half:], axis, -1)
    from_below, from_above, after = join(from_below, from_above, after)
    up = block((index + 1) % 4)
    up = jnp.concatenate([add(up[:half], from_below), up[half:]])
    down = block((index + 3) % 4)
    down = jnp.concatenate([down[:half], add(down[half:], from_above)])
    got_up = shift(up, axis, 1)
    got_down = shift(down, axis, -1)
    return block(index).astype(F32) + got_up.astype(F32) + got_down.astype(F32)


def dot(left, right):
    return jnp.dot(left, right, preferred_element_type=F32)


def dot_nt(left, right):
    return lax.dot_general(left, right, (((1,), (1,)), ((), ())), preferred_element_type=F32)


def dot_tn(left, right):
    return lax.dot_general(left, right, (((0,), (0,)), ((), ())), preferred_element_type=F32)


def attention_kernel(q_ref, ko_ref, kp_ref, vo_ref, vp_ref, out_ref, lse_ref):
    rows = q_ref.shape[0]
    step = 256
    for h in range(2):
        cols = slice(HEAD * h, HEAD * (h + 1))
        keys_own, keys_peer = ko_ref[:, cols], kp_ref[:, cols]
        values_own, values_peer = vo_ref[:, cols], vp_ref[:, cols]
        for start in range(0, rows, step):
            queries = q_ref[start : start + step, cols] * HEAD ** (-0.5)
            scores_own = dot_nt(keys_own, queries)
            scores_peer = dot_nt(keys_peer, queries)
            top = jnp.maximum(
                jnp.max(scores_own, axis=0, keepdims=True),
                jnp.max(scores_peer, axis=0, keepdims=True),
            )
            probs_own = jnp.exp(scores_own - top)
            probs_peer = jnp.exp(scores_peer - top)
            total = jnp.sum(probs_own, axis=0, keepdims=True) + jnp.sum(
                probs_peer, axis=0, keepdims=True
            )
            mixed = dot_tn(values_own, probs_own.astype(BF)) + dot_tn(
                values_peer, probs_peer.astype(BF)
            )
            mixed = mixed / total
            out_ref[start : start + step, cols] = mixed.T.astype(BF)
            lse_ref[0, h : h + 1, start : start + step] = top + jnp.log(total)


def attention(queries, kv_own, kv_peer):
    rows, width = queries.shape
    pairs = width // 128
    block = lambda offset: pl.BlockSpec((rows, 128), lambda h: (0, h + offset))
    return pl.pallas_call(
        attention_kernel,
        grid=(pairs,),
        in_specs=[block(0), block(0), block(0), block(pairs), block(pairs)],
        out_specs=[block(0), pl.BlockSpec((1, 2, rows), lambda h: (h, 0, 0))],
        out_shape=[
            jax.ShapeDtypeStruct((rows, width), BF),
            jax.ShapeDtypeStruct((pairs, 2, rows), F32),
        ],
        compiler_params=pltpu.CompilerParams(vmem_limit_bytes=40 * 2**20),
        cost_estimate=pl.CostEstimate(
            flops=8 * rows * rows * width,
            bytes_accessed=12 * rows * width,
            transcendentals=2 * rows * rows * width // HEAD,
        ),
        name="attention",
    )(queries, kv_own, kv_peer, kv_own, kv_peer)


def attention_back_kernel(
    q_ref, ko_ref, kp_ref, vo_ref, vp_ref, out_ref, gout_ref, lse_ref, gq_ref, go_ref, gp_ref
):
    rows = q_ref.shape[0]
    step = 256
    scale = HEAD ** (-0.5)
    for h in range(2):
        cols = slice(HEAD * h, HEAD * (h + 1))
        sides = ((ko_ref, vo_ref, go_ref), (kp_ref, vp_ref, gp_ref))
        grad_kv = [[None, None], [None, None]]
        for start in range(0, rows, step):
            span = slice(start, start + step)
            queries = q_ref[span, cols] * scale
            grad_out = gout_ref[span, cols]
            lse = lse_ref[0, h : h + 1, span]
            both = grad_out.astype(F32) * out_ref[span, cols].astype(F32)
            row_total = jnp.sum(both.T, axis=0, keepdims=True)
            grad_queries = None
            for side, (k_ref, v_ref, g_ref) in enumerate(sides):
                keys, values = k_ref[:, cols], v_ref[:, cols]
                probs = jnp.exp(dot_nt(keys, queries) - lse)
                grad_probs = dot_nt(values, grad_out)
                grad_scores = (probs * (grad_probs - row_total)).astype(BF)
                part = dot_tn(keys, grad_scores)
                grad_queries = part if grad_queries is None else grad_queries + part
                terms = (dot(grad_scores, queries), dot(probs.astype(BF), grad_out))
                for i in range(2):
                    old = grad_kv[side][i]
                    grad_kv[side][i] = terms[i] if old is None else old + terms[i]
            gq_ref[span, cols] = (grad_queries * scale).T.astype(BF)
        for side, (k_ref, v_ref, g_ref) in enumerate(sides):
            for i in range(2):
                g_ref[i, :, cols] = grad_kv[side][i].astype(g_ref.dtype)


def attention_back(queries, kv_own, kv_peer, mixed, grad_mixed, lse):
    rows, width = queries.shape
    pairs = width // 128
    block = lambda offset: pl.BlockSpec((rows, 128), lambda h: (0, h + offset))
    double = pl.BlockSpec((2, rows, 128), lambda h: (0, 0, h))
    return pl.pallas_call(
        attention_back_kernel,
        grid=(pairs,),
        in_specs=[
            block(0),
            block(0),
            block(0),
            block(pairs),
            block(pairs),
            block(0),
            block(0),
            pl.BlockSpec((1, 2, rows), lambda h: (h, 0, 0)),
        ],
        out_specs=[block(0), double, double],
        out_shape=[
            jax.ShapeDtypeStruct((rows, width), BF),
            jax.ShapeDtypeStruct((2, rows, width), F32),
            jax.ShapeDtypeStruct((2, rows, width), BF),
        ],
        compiler_params=pltpu.CompilerParams(vmem_limit_bytes=40 * 2**20),
        cost_estimate=pl.CostEstimate(
            flops=20 * rows * rows * width,
            bytes_accessed=24 * rows * width,
            transcendentals=2 * rows * rows * width // HEAD,
        ),
        name="attention_back",
    )(queries, kv_own, kv_peer, kv_own, kv_peer, mixed, grad_mixed, lse)


def norm_stats(activations):
    center = activations - jnp.mean(activations, axis=-1, keepdims=True)
    inverse = lax.rsqrt(jnp.mean(center * center, axis=-1, keepdims=True) + 1e-06)
    return (center * inverse, inverse)


def norm_back(grad_norm, normal, inverse):
    return inverse * (
        grad_norm
        - jnp.mean(grad_norm, axis=-1, keepdims=True)
        - normal * jnp.mean(grad_norm * normal, axis=-1, keepdims=True)
    )


def core_sum(partial_sum):
    low = partial_sum.astype(BF)
    return low.astype(F32) + swap(low, "core").astype(F32)


def gelu_and_slope(pre_act):
    linear = 2.0 * (2.0 / jnp.pi) ** 0.5
    cubic = 0.044715 * linear
    square = pre_act * pre_act
    gate = 1.0 / (1.0 + jnp.exp(-pre_act * (linear + cubic * square)))
    value = pre_act * gate
    slope = gate + value * (1.0 - gate) * (linear + 3.0 * cubic * square)
    return value.astype(BF), slope.astype(BF)


def attend(activations, activations_peer, modulation, weights, before=None, after=None):
    w_q, w_kv, w_out = weights
    shift_first, scale_first, gate_first = modulation[:3]
    normal_first, inverse_first = norm_stats(activations)
    entry = (normal_first * (1.0 + scale_first) + shift_first).astype(BF)
    kv_own = dot(entry, w_kv).astype(BF)
    queries = dot(entry, w_q).astype(BF)
    activations_peer, kv_own, queries = lax.optimization_barrier(
        (activations_peer, kv_own, queries)
    )
    entry_peer = norm_stats(activations_peer.astype(F32))[0] * (1.0 + scale_first) + shift_first
    entry_peer = entry_peer.astype(BF)
    kv_peer = dot(entry_peer, w_kv).astype(BF)
    if before:
        queries = before(queries)
    mixed, lse = attention(queries, kv_own, kv_peer)
    if after:
        mixed = after(mixed)
    branch = core_sum(dot(mixed, w_out))
    second = activations + gate_first * branch
    return (
        second,
        normal_first,
        inverse_first,
        entry,
        entry_peer,
        queries,
        kv_own,
        kv_peer,
        lse,
        mixed,
        branch,
    )


def feed_forward(attn_state, modulation, weights):
    w_fc1, w_fc2 = weights
    shift_second, scale_second, gate_second = modulation[3:]
    second, *kept = attn_state
    normal_second, inverse_second = norm_stats(second)
    mlp_input = (normal_second * (1.0 + scale_second) + shift_second).astype(BF)
    hidden, slope = gelu_and_slope(dot(mlp_input, w_fc1))
    branch_mlp = core_sum(dot(hidden, w_fc2))
    result = second + gate_second * branch_mlp
    state = (*kept, normal_second, inverse_second, mlp_input, slope, hidden, branch_mlp)
    return (result, state)


def layer_backward(grad_result, state, modulation, weights, core=None):
    w_q, w_kv, w_out, w_fc1, w_fc2 = weights
    shift_first, scale_first, gate_first, shift_second, scale_second, gate_second = modulation
    (
        normal_first,
        inverse_first,
        entry,
        unused,
        queries,
        kv_own,
        kv_peer,
        lse,
        mixed,
        branch,
        normal_second,
        inverse_second,
        mlp_input,
        slope,
        hidden,
        branch_mlp,
    ) = state
    rows = lambda value: jnp.sum(value, axis=0)
    grad_gate_second = rows(grad_result * branch_mlp)
    grad_branch_mlp = (grad_result * gate_second).astype(BF)
    grad_hidden = dot_nt(grad_branch_mlp, w_fc2)
    grad_pre = (grad_hidden * slope.astype(F32)).astype(BF)
    grad_mlp_input = core_sum(dot_nt(grad_pre, w_fc1))
    grad_fc2 = dot_tn(hidden, grad_branch_mlp).astype(BF)
    grad_fc1 = dot_tn(mlp_input, grad_pre).astype(BF)
    grad_scale_second = rows(grad_mlp_input * normal_second)
    grad_shift_second = rows(grad_mlp_input)
    grad_second = grad_result + norm_back(
        grad_mlp_input * (1.0 + scale_second), normal_second, inverse_second
    )
    grad_gate_first = rows(grad_second * branch)
    grad_branch = (grad_second * gate_first).astype(BF)
    grad_mixed = dot_nt(grad_branch, w_out).astype(BF)
    grad_out = dot_tn(mixed, grad_branch).astype(BF)
    grad_queries, grad_own, grad_peer = attention_back(
        queries, kv_own, kv_peer, mixed, grad_mixed, lse
    )
    if core is not None:
        tokens, half = mixed.shape
        w_k, w_v = w_kv[:, :half], w_kv[:, half:]
        far = (dot_nt(grad_peer[0], w_k) + dot_nt(grad_peer[1], w_v)).astype(BF)
        kept = rows_at(far, core * (tokens // 2), tokens // 2).astype(F32)
        given = rows_at(far, (1 - core) * (tokens // 2), tokens // 2)
        far = swap((kept + swap(given, "core").astype(F32)).astype(BF), "xl")
        grad_own = grad_own.astype(BF)
        near = core_sum(
            dot_nt(grad_queries, w_q) + dot_nt(grad_own[0], w_k) + dot_nt(grad_own[1], w_v)
        )
        near, far = join(near, far)
        grad_entry = near + ordered(core == 0, far, swap(far, "core")).astype(F32)
        return grad_second + norm_back(
            grad_entry * (1.0 + scale_first), normal_first, inverse_first
        )
    grad_kv = (grad_own + swap(grad_peer, "xl").astype(F32)).astype(BF)
    grad_kv = jnp.concatenate([grad_kv[0], grad_kv[1]], axis=1)
    grad_entry = core_sum(dot_nt(grad_queries, w_q) + dot_nt(grad_kv, w_kv))
    grad_q_proj = dot_tn(entry, grad_queries).astype(BF)
    grad_kv_proj = dot_tn(entry, grad_kv).astype(BF)
    grad_scale_first = rows(grad_entry * normal_first)
    grad_shift_first = rows(grad_entry)
    grad_input = grad_second + norm_back(
        grad_entry * (1.0 + scale_first), normal_first, inverse_first
    )
    grad_modulation = jnp.stack(
        [
            grad_shift_first,
            grad_scale_first,
            grad_gate_first,
            grad_shift_second,
            grad_scale_second,
            grad_gate_second,
        ]
    )
    return (grad_input, grad_modulation, (grad_q_proj, grad_kv_proj, grad_out, grad_fc1, grad_fc2))


def sum_over_plane(block):
    x = lax.axis_index(RING_X)
    half, quarter = (x + 1) // 2 % 2, x // 2
    rows, columns = block.shape
    parts = block.astype(BF).reshape(2, rows // 2, columns)
    part = pick(parts, half).astype(F32) + swap(pick(parts, 1 - half), "xl").astype(F32)
    parts = part.astype(BF).reshape(2, rows // 4, columns)
    part = pick(parts, quarter).astype(F32) + swap_odd(pick(parts, 1 - quarter), RING_X).astype(F32)
    part = part.astype(BF)
    part = (part.astype(F32) + swap(part, "zh").astype(F32)).astype(BF)
    part = ordered(quarter == 0, part, swap_odd(part, RING_X))
    return ordered(half == 0, part, swap(part, "xl"))


def fill_fc_kernel(core_ref, mine_ref, other_ref, fc1_ref, fc2_ref):
    half = mine_ref.shape[1] // 2
    rows = fc1_ref.shape[0]
    first = core_ref[0] == 0
    mine, other = mine_ref[...].astype(F32), other_ref[...].astype(F32)
    for c, part in enumerate((jnp.where(first, mine, other), jnp.where(first, other, mine))):
        fc2_ref[half * c : half * (c + 1), :] = part[:half]
        for j in range(4):
            top = half + rows * (j // 2)
            left = half * (j % 2)
            to = half * (2 * j + c)
            fc1_ref[:, to : to + half] = part[top : top + rows, left : left + half]


def fill_attn_kernel(core_ref, mine_ref, other_ref, qkv_ref, out_ref):
    rows, width = out_ref.shape
    half = width // 2
    first = core_ref[0] == 0
    mine, other = mine_ref[...].astype(F32), other_ref[...].astype(F32)
    for c, part in enumerate((jnp.where(first, mine, other), jnp.where(first, other, mine))):
        at = half * c
        qkv_ref[:, at : at + half] = part[rows:, :half]
        qkv_ref[:, width + at : width + at + half] = part[:rows, :half]
        qkv_ref[:, 2 * width + at : 2 * width + at + half] = part[:rows, half:]
        out_ref[:, at : at + half] = part[rows:, half:]


def fill(kernel, core, total, shapes, name):
    whole = pl.BlockSpec(memory_space=pltpu.VMEM)
    return pl.pallas_call(
        kernel,
        in_specs=[pl.BlockSpec(memory_space=pltpu.SMEM), whole, whole],
        out_specs=[whole] * len(shapes),
        out_shape=[jax.ShapeDtypeStruct(shape, F32) for shape in shapes],
        compiler_params=pltpu.CompilerParams(vmem_limit_bytes=40 * 2**20),
        cost_estimate=pl.CostEstimate(flops=0, bytes_accessed=12 * total.size, transcendentals=0),
        name=name,
    )(core.astype(jnp.int32).reshape(1), total, swap(total, "core"))


def on_device(ends, cond, w_ada, b_ada, w_qkv, w_out, w_fc1, w_fc2):
    section = lax.axis_index("section")
    d = lax.axis_index("dp")
    zh, xh = lax.axis_index("zh"), lax.axis_index("xh")
    a = zh * 2 + xh
    core = lax.axis_index("core")
    width = w_out.shape[2]
    half = width // 2
    rows_d = w_out.shape[1]
    columns = lambda array, start: lax.dynamic_slice_in_dim(array, start, half, 1)

    cond_float = cond.astype(F32).reshape(4, width)
    cond_low = jax.nn.silu(cond_float).astype(BF)
    cond_rows = cond_low.reshape(4, 4, rows_d).transpose(1, 0, 2)
    cond_parts = [pick(cond_rows, d)] + [
        shift(pick(cond_rows, (d + s) % 4), "dp", s) for s in (1, 2, 3)
    ]
    piece_attn = jnp.concatenate(
        [columns(w_qkv[0], width * i + half * core) for i in range(3)]
        + [columns(w_out[0], half * core)],
        axis=1,
    )

    blocks = ends[0].reshape(2, 2, *ends.shape[3:])
    mine = lax.dynamic_index_in_dim(blocks, xh, 1, keepdims=False)
    theirs = lax.dynamic_index_in_dim(blocks, 1 - xh, 1, keepdims=False)
    theirs = swap_odd(theirs, RING_X)
    piece_attn, theirs, *cond_parts = join(piece_attn, theirs, *cond_parts)
    blocks = jnp.stack([mine, theirs], axis=1)
    mine = jnp.stack([pick(blocks, zh), swap(pick(blocks, 1 - zh), "zh")])
    mine = mine.reshape(-1, width)
    tokens_half = mine.shape[0]

    below, above = gather_near(piece_attn, "dp")

    latent_rows = jnp.stack([pick(part, a) for part in cond_parts])
    bias = lax.dynamic_update_slice(
        jnp.zeros((6 * width,), F32), b_ada[0].astype(F32), (d * b_ada.shape[1],)
    )
    part_mod = dot(latent_rows, w_ada[0]) + bias[None]
    part_mod, below, above, mine = join(part_mod, below, above, mine)
    mod_parts = [shift(part_mod[s : s + 1], "dp", -s) for s in (1, 2, 3)]
    attn_blocks = gather_far(piece_attn, below, above, "dp")
    other = swap(mine, "core")
    peer = swap(mine, "xl")
    piece_fc1 = jnp.concatenate(
        [columns(w_fc1[0], width * j + half * core) for j in range(4)], axis=1
    )
    piece_fc2 = rows_at(w_fc2[0], half * core, half)
    attn_blocks, mod_parts, other, peer, piece_fc1 = join(
        attn_blocks, mod_parts, other, peer, piece_fc1
    )
    near_fc1 = gather_near(piece_fc1, "dp")
    modulation = part_mod[0:1] + mod_parts[0] + mod_parts[1] + mod_parts[2]
    modulation = [modulation[:, width * i : width * (i + 1)] for i in range(6)]
    start = ordered(core == 0, mine, other)
    start_peer = ordered(core == 0, peer, swap(peer, "core"))
    full_attn = fill_rows(width, attn_blocks, d)
    out_rows = full_attn[:, 3 * half :].reshape(2, half, half)
    full_out = ordered(
        core == 0, pick(out_rows, core), swap(pick(out_rows, 1 - core), "core"), axis=1
    )
    def across(value, pairs, with_peer):
        part = rows_at(value.astype(BF), core * tokens_half, tokens_half)
        part = lax.ppermute(part, "section", pairs)
        own = ordered(core == 0, part, swap(part, "core"))
        if not with_peer:
            return own, None
        peer = swap(part, "xl")
        return own, ordered(core == 0, peer, swap(peer, "core"))

    attn_weights = (full_attn[:, :half], full_attn[:, half : 3 * half], full_out)
    fetched = {}

    def fetch_early(queries):
        queries, fetched["near"], fetched["piece"] = join(queries, near_fc1, piece_fc2)
        fetched["fc1"] = gather_far(piece_fc1, *fetched["near"], "dp")
        return queries

    def fetch_late(mixed):
        mixed, fetched["fc1"] = join(mixed, fetched["fc1"])
        fetched["near"] = gather_near(fetched["piece"], "dp")
        return mixed

    attn_state = attend(
        start.astype(F32), start_peer, modulation, attn_weights, fetch_early, fetch_late
    )
    second, near_fc2 = join(attn_state[0], fetched["near"])
    attn_state = (second, *attn_state[1:])
    full_fc1 = fill_rows(width, fetched["fc1"], d)
    full_fc2 = fill_rows(4 * half, gather_far(piece_fc2, *near_fc2, "dp"), d)
    fc_weights = (full_fc1, full_fc2)
    weights = attn_weights + fc_weights
    result, unused = feed_forward(attn_state, modulation, fc_weights)
    arrived, arrived_peer = across(result, [(0, 1)], True)
    second_input = jnp.where(section == 0, start, arrived).astype(F32)
    second_peer = jnp.where(section == 0, start_peer, arrived_peer)
    attn_state = attend(second_input, second_peer, modulation, attn_weights)
    result, state = feed_forward(attn_state, modulation, fc_weights)

    grad_input = layer_backward(start.astype(F32), state, modulation, weights, core)
    arrived, unused = across(grad_input, [(1, 0)], False)
    seed = jnp.where(section == 0, arrived, start).astype(F32)
    grad_input, grad_modulation, grads = layer_backward(seed, state, modulation, weights)
    grad_q, grad_kv, grad_out, grad_fc1, grad_fc2 = grads

    def block_fc(i):
        one = rows_at(grad_fc1, i * rows_d, rows_d)
        return jnp.concatenate([rows_at(grad_fc2, i * half, half), one[:, :width], one[:, width:]])

    sum_fc = sum_over_plane(scatter_ring(block_fc, "dp", d, grad_q))
    out_fc1, out_fc2 = fill(
        fill_fc_kernel, core, sum_fc, ((rows_d, 8 * half), (2 * half, width)), "fill_fc"
    )
    out_own = ordered(
        core == 0,
        columns(grad_out, half * core),
        swap(columns(grad_out, half - half * core), "core"),
    )

    def block_attn(i):
        kv, q, out = (rows_at(g, i * rows_d, rows_d) for g in (grad_kv, grad_q, out_own))
        return jnp.concatenate([kv, jnp.concatenate([q, out], axis=1)])

    sum_attn = sum_over_plane(scatter_ring(block_attn, "dp", d, grad_input))
    out_qkv, out_out = fill(
        fill_attn_kernel, core, sum_attn, ((rows_d, 6 * half), (rows_d, width)), "fill_attn"
    )

    grad_mod = grad_modulation.reshape(1, 6 * width)
    grad_mod = grad_mod + swap(grad_mod, "xl")
    plane_mod = ordered(xh == 0, grad_mod, swap_odd(grad_mod, RING_X))
    plane_mod = ordered(zh == 0, plane_mod, swap(plane_mod, "zh"))
    all_mod = gather_small(plane_mod, "dp", d)
    all_cond = jnp.zeros((4, 4, rows_d), BF)
    for s in range(4):
        all_cond = lax.dynamic_update_index_in_dim(all_cond, cond_parts[s], (d + 4 - s) % 4, 0)
    all_cond = all_cond.reshape(16, rows_d)
    out_ada = lax.dot_general(
        all_cond.astype(F32), all_mod, (((0,), (0,)), ((), ())), precision=lax.Precision.HIGHEST
    )
    out_bias = jnp.sum(
        lax.dynamic_slice_in_dim(all_mod, d * b_ada.shape[1], b_ada.shape[1], 1), axis=0
    )
    grad_silu = lax.dot_general(
        all_mod,
        w_ada[0].astype(F32),
        (((1,), (1,)), ((), ())),
        precision=lax.Precision.HIGHEST,
    ).reshape(2, 2, 4, rows_d)
    same = jnp.stack([pick(grad_silu, d // 2), swap_odd(pick(grad_silu, 1 - d // 2), "dp")], axis=1)
    got = swap_even(pick(same, 1 - d % 2), "dp")
    same = pick(same, d % 2)
    silu_full = jnp.zeros((4, 4, rows_d), F32)
    beside = d + 1 - 2 * (d % 2)
    for part, place in ((same[0], d), (same[1], 3 - d), (got[0], beside), (got[1], 3 - beside)):
        silu_full = lax.dynamic_update_index_in_dim(silu_full, part, place, 0)
    silu_full = silu_full.transpose(1, 0, 2).reshape(4, width)
    silu_full = silu_full + swap(silu_full, "section")
    unused, silu_pull = jax.vjp(jax.nn.silu, cond_float)
    out_cond = silu_pull(silu_full)[0].reshape(cond.shape)

    edge = jnp.where(section == 0, grad_input, result)
    edge = rows_at(edge, core * tokens_half, tokens_half).reshape(2, 2, -1, width)
    edge = ordered(zh == 0, edge[:1], swap(edge[1:].astype(BF), "zh").astype(F32))
    boundary = ordered(
        xh == 0, edge[:, :1], swap_odd(edge[:, 1:].astype(BF), RING_X).astype(F32), axis=1
    ).reshape(ends.shape)

    return (
        boundary,
        out_cond,
        out_ada[None],
        out_bias[None],
        out_qkv[None],
        out_out[None],
        out_fc1[None],
        out_fc2[None],
    )


def solution(mesh):
    finer = Mesh(
        mesh.devices.reshape(2, 4, 2, 2, 2, 2), ("section", "dp", "zh", "xh", "xl", "core")
    )
    ends_spec = P("section", None, "dp", CTX, None)
    cond_spec = P(None, "dp", None)
    matrix = P("section", "dp", None)
    vector = P("section", "dp")
    return jax.shard_map(
        on_device,
        mesh=finer,
        in_specs=(ends_spec, cond_spec, matrix, vector, matrix, matrix, matrix, matrix),
        out_specs=(ends_spec, cond_spec, matrix, vector, matrix, matrix, matrix, matrix),
        check_vma=False,
    )
```

```python
import jax
import jax.numpy as jnp
from jax import lax
from jax.experimental import pallas as pl
from jax.experimental.pallas import tpu as pltpu
from jax.sharding import Mesh
from jax.sharding import PartitionSpec as P

HEAD = 64
BF = jnp.bfloat16
F32 = jnp.float32
RING_X = ("xh", "xl")
CTX = ("zh", "xh", "xl", "core")


def shift(array, axis, by, size=4):
    return lax.ppermute(array, axis, [(i, (i + by) % size) for i in range(size)])


def swap(array, axis):
    return lax.ppermute(array, axis, [(0, 1), (1, 0)])


def swap_odd(array, axis):
    return lax.ppermute(array, axis, [(0, 3), (1, 2), (2, 1), (3, 0)])


def swap_even(array, axis):
    return lax.ppermute(array, axis, [(0, 1), (1, 0), (2, 3), (3, 2)])


def pick(blocks, index):
    return lax.dynamic_index_in_dim(blocks, index, 0, keepdims=False)


def rows_at(array, start, size):
    return lax.dynamic_slice_in_dim(array, start, size, 0)


def ordered(first, mine, other, axis=0):
    return jnp.where(
        first,
        jnp.concatenate([mine, other], axis=axis),
        jnp.concatenate([other, mine], axis=axis),
    )


def gather_small(piece, axis, index):
    two = ordered(index % 2 == 0, piece, swap_even(piece, axis))
    return ordered(index < 2, two, swap_odd(two, axis))


def gather_near(piece, axis):
    return shift(piece, axis, 1), shift(piece, axis, -1)


def gather_far(piece, below, above, axis):
    half = piece.shape[0] // 2
    far_low = shift(below[:half], axis, 1)
    far_high = shift(above[half:], axis, -1)
    return [(piece,), (above,), (far_low, far_high), (below,)]


def fill_rows(size, blocks, index):
    total = jnp.zeros((size, blocks[0][0].shape[1]), BF)
    for s, pieces in enumerate(blocks):
        at = (index + s) % 4 * (size // 4)
        for piece in pieces:
            total = lax.dynamic_update_slice(total, piece, (at, 0))
            at = at + piece.shape[0]
    return total


def join(*values):
    return lax.optimization_barrier(values)


def scatter_ring(block, axis, index, after):
    add = lambda one, two: (one.astype(F32) + two.astype(F32)).astype(BF)
    far = block((index + 2) % 4)
    half = far.shape[0] // 2
    from_below = shift(far[:half], axis, 1)
    from_above = shift(far[half:], axis, -1)
    from_below, from_above, after = join(from_below, from_above, after)
    up = block((index + 1) % 4)
    up = jnp.concatenate([add(up[:half], from_below), up[half:]])
    down = block((index + 3) % 4)
    down = jnp.concatenate([down[:half], add(down[half:], from_above)])
    got_up = shift(up, axis, 1)
    got_down = shift(down, axis, -1)
    return block(index).astype(F32) + got_up.astype(F32) + got_down.astype(F32)


def dot(left, right):
    return jnp.dot(left, right, preferred_element_type=F32)


def dot_nt(left, right):
    return lax.dot_general(left, right, (((1,), (1,)), ((), ())), preferred_element_type=F32)


def dot_tn(left, right):
    return lax.dot_general(left, right, (((0,), (0,)), ((), ())), preferred_element_type=F32)


def attention_kernel(q_ref, ko_ref, kp_ref, vo_ref, vp_ref, out_ref, lse_ref):
    rows = q_ref.shape[0]
    step = 256
    for h in range(2):
        cols = slice(HEAD * h, HEAD * (h + 1))
        keys_own, keys_peer = ko_ref[:, cols], kp_ref[:, cols]
        values_own, values_peer = vo_ref[:, cols], vp_ref[:, cols]
        for start in range(0, rows, step):
            queries = q_ref[start : start + step, cols] * HEAD ** (-0.5)
            scores_own = dot_nt(keys_own, queries)
            scores_peer = dot_nt(keys_peer, queries)
            top = jnp.maximum(
                jnp.max(scores_own, axis=0, keepdims=True),
                jnp.max(scores_peer, axis=0, keepdims=True),
            )
            probs_own = jnp.exp(scores_own - top)
            probs_peer = jnp.exp(scores_peer - top)
            total = jnp.sum(probs_own, axis=0, keepdims=True) + jnp.sum(
                probs_peer, axis=0, keepdims=True
            )
            mixed = dot_tn(values_own, probs_own.astype(BF)) + dot_tn(
                values_peer, probs_peer.astype(BF)
            )
            mixed = mixed / total
            out_ref[start : start + step, cols] = mixed.T.astype(BF)
            lse_ref[0, h : h + 1, start : start + step] = top + jnp.log(total)


def attention(queries, kv_own, kv_peer):
    rows, width = queries.shape
    pairs = width // 128
    block = lambda offset: pl.BlockSpec((rows, 128), lambda h: (0, h + offset))
    return pl.pallas_call(
        attention_kernel,
        grid=(pairs,),
        in_specs=[block(0), block(0), block(0), block(pairs), block(pairs)],
        out_specs=[block(0), pl.BlockSpec((1, 2, rows), lambda h: (h, 0, 0))],
        out_shape=[
            jax.ShapeDtypeStruct((rows, width), BF),
            jax.ShapeDtypeStruct((pairs, 2, rows), F32),
        ],
        compiler_params=pltpu.CompilerParams(vmem_limit_bytes=40 * 2**20),
        cost_estimate=pl.CostEstimate(
            flops=8 * rows * rows * width,
            bytes_accessed=12 * rows * width,
            transcendentals=2 * rows * rows * width // HEAD,
        ),
        name="attention",
    )(queries, kv_own, kv_peer, kv_own, kv_peer)


def attention_back_kernel(
    q_ref, ko_ref, kp_ref, vo_ref, vp_ref, out_ref, gout_ref, lse_ref, gq_ref, go_ref, gp_ref
):
    rows = q_ref.shape[0]
    step = 256
    scale = HEAD ** (-0.5)
    for h in range(2):
        cols = slice(HEAD * h, HEAD * (h + 1))
        sides = ((ko_ref, vo_ref, go_ref), (kp_ref, vp_ref, gp_ref))
        grad_kv = [[None, None], [None, None]]
        for start in range(0, rows, step):
            span = slice(start, start + step)
            queries = q_ref[span, cols] * scale
            grad_out = gout_ref[span, cols]
            lse = lse_ref[0, h : h + 1, span]
            both = grad_out.astype(F32) * out_ref[span, cols].astype(F32)
            row_total = jnp.sum(both.T, axis=0, keepdims=True)
            grad_queries = None
            for side, (k_ref, v_ref, g_ref) in enumerate(sides):
                keys, values = k_ref[:, cols], v_ref[:, cols]
                probs = jnp.exp(dot_nt(keys, queries) - lse)
                grad_probs = dot_nt(values, grad_out)
                grad_scores = (probs * (grad_probs - row_total)).astype(BF)
                part = dot_tn(keys, grad_scores)
                grad_queries = part if grad_queries is None else grad_queries + part
                terms = (dot(grad_scores, queries), dot(probs.astype(BF), grad_out))
                for i in range(2):
                    old = grad_kv[side][i]
                    grad_kv[side][i] = terms[i] if old is None else old + terms[i]
            gq_ref[span, cols] = (grad_queries * scale).T.astype(BF)
        for side, (k_ref, v_ref, g_ref) in enumerate(sides):
            for i in range(2):
                g_ref[i, :, cols] = grad_kv[side][i].astype(g_ref.dtype)


def attention_back(queries, kv_own, kv_peer, mixed, grad_mixed, lse):
    rows, width = queries.shape
    pairs = width // 128
    block = lambda offset: pl.BlockSpec((rows, 128), lambda h: (0, h + offset))
    double = pl.BlockSpec((2, rows, 128), lambda h: (0, 0, h))
    return pl.pallas_call(
        attention_back_kernel,
        grid=(pairs,),
        in_specs=[
            block(0),
            block(0),
            block(0),
            block(pairs),
            block(pairs),
            block(0),
            block(0),
            pl.BlockSpec((1, 2, rows), lambda h: (h, 0, 0)),
        ],
        out_specs=[block(0), double, double],
        out_shape=[
            jax.ShapeDtypeStruct((rows, width), BF),
            jax.ShapeDtypeStruct((2, rows, width), F32),
            jax.ShapeDtypeStruct((2, rows, width), BF),
        ],
        compiler_params=pltpu.CompilerParams(vmem_limit_bytes=40 * 2**20),
        cost_estimate=pl.CostEstimate(
            flops=20 * rows * rows * width,
            bytes_accessed=24 * rows * width,
            transcendentals=2 * rows * rows * width // HEAD,
        ),
        name="attention_back",
    )(queries, kv_own, kv_peer, kv_own, kv_peer, mixed, grad_mixed, lse)


def norm_stats(activations):
    center = activations - jnp.mean(activations, axis=-1, keepdims=True)
    inverse = lax.rsqrt(jnp.mean(center * center, axis=-1, keepdims=True) + 1e-06)
    return (center * inverse, inverse)


def norm_back(grad_norm, normal, inverse):
    return inverse * (
        grad_norm
        - jnp.mean(grad_norm, axis=-1, keepdims=True)
        - normal * jnp.mean(grad_norm * normal, axis=-1, keepdims=True)
    )


def core_sum(partial_sum):
    low = partial_sum.astype(BF)
    return low.astype(F32) + swap(low, "core").astype(F32)


def gelu_and_slope(pre_act):
    linear = 2.0 * (2.0 / jnp.pi) ** 0.5
    cubic = 0.044715 * linear
    square = pre_act * pre_act
    gate = 1.0 / (1.0 + jnp.exp(-pre_act * (linear + cubic * square)))
    value = pre_act * gate
    slope = gate + value * (1.0 - gate) * (linear + 3.0 * cubic * square)
    return value.astype(BF), slope.astype(BF)


def attend(activations, activations_peer, modulation, weights, before=None, after=None):
    w_q, w_kv, w_out = weights
    shift_first, scale_first, gate_first = modulation[:3]
    normal_first, inverse_first = norm_stats(activations)
    entry = (normal_first * (1.0 + scale_first) + shift_first).astype(BF)
    kv_own = dot(entry, w_kv).astype(BF)
    queries = dot(entry, w_q).astype(BF)
    activations_peer, kv_own, queries = lax.optimization_barrier(
        (activations_peer, kv_own, queries)
    )
    entry_peer = norm_stats(activations_peer.astype(F32))[0] * (1.0 + scale_first) + shift_first
    entry_peer = entry_peer.astype(BF)
    kv_peer = dot(entry_peer, w_kv).astype(BF)
    if before:
        queries = before(queries)
    mixed, lse = attention(queries, kv_own, kv_peer)
    if after:
        mixed = after(mixed)
    branch = core_sum(dot(mixed, w_out))
    second = activations + gate_first * branch
    return (
        second,
        normal_first,
        inverse_first,
        entry,
        entry_peer,
        queries,
        kv_own,
        kv_peer,
        lse,
        mixed,
        branch,
    )


def feed_forward(attn_state, modulation, weights):
    w_fc1, w_fc2 = weights
    shift_second, scale_second, gate_second = modulation[3:]
    second, *kept = attn_state
    normal_second, inverse_second = norm_stats(second)
    mlp_input = (normal_second * (1.0 + scale_second) + shift_second).astype(BF)
    hidden, slope = gelu_and_slope(dot(mlp_input, w_fc1))
    branch_mlp = core_sum(dot(hidden, w_fc2))
    result = second + gate_second * branch_mlp
    state = (*kept, normal_second, inverse_second, mlp_input, slope, hidden, branch_mlp)
    return (result, state)


def layer_backward(grad_result, state, modulation, weights, core=None):
    w_q, w_kv, w_out, w_fc1, w_fc2 = weights
    shift_first, scale_first, gate_first, shift_second, scale_second, gate_second = modulation
    (
        normal_first,
        inverse_first,
        entry,
        unused,
        queries,
        kv_own,
        kv_peer,
        lse,
        mixed,
        branch,
        normal_second,
        inverse_second,
        mlp_input,
        slope,
        hidden,
        branch_mlp,
    ) = state
    rows = lambda value: jnp.sum(value, axis=0)
    grad_gate_second = rows(grad_result * branch_mlp)
    grad_branch_mlp = (grad_result * gate_second).astype(BF)
    grad_hidden = dot_nt(grad_branch_mlp, w_fc2)
    grad_pre = (grad_hidden * slope.astype(F32)).astype(BF)
    grad_mlp_input = core_sum(dot_nt(grad_pre, w_fc1))
    grad_fc2 = dot_tn(hidden, grad_branch_mlp).astype(BF)
    grad_fc1 = dot_tn(mlp_input, grad_pre).astype(BF)
    grad_scale_second = rows(grad_mlp_input * normal_second)
    grad_shift_second = rows(grad_mlp_input)
    grad_second = grad_result + norm_back(
        grad_mlp_input * (1.0 + scale_second), normal_second, inverse_second
    )
    grad_gate_first = rows(grad_second * branch)
    grad_branch = (grad_second * gate_first).astype(BF)
    grad_mixed = dot_nt(grad_branch, w_out).astype(BF)
    grad_out = dot_tn(mixed, grad_branch).astype(BF)
    grad_queries, grad_own, grad_peer = attention_back(
        queries, kv_own, kv_peer, mixed, grad_mixed, lse
    )
    if core is not None:
        tokens, half = mixed.shape
        w_k, w_v = w_kv[:, :half], w_kv[:, half:]
        far = (dot_nt(grad_peer[0], w_k) + dot_nt(grad_peer[1], w_v)).astype(BF)
        kept = rows_at(far, core * (tokens // 2), tokens // 2).astype(F32)
        given = rows_at(far, (1 - core) * (tokens // 2), tokens // 2)
        far = swap((kept + swap(given, "core").astype(F32)).astype(BF), "xl")
        grad_own = grad_own.astype(BF)
        near = core_sum(
            dot_nt(grad_queries, w_q) + dot_nt(grad_own[0], w_k) + dot_nt(grad_own[1], w_v)
        )
        near, far = join(near, far)
        grad_entry = near + ordered(core == 0, far, swap(far, "core")).astype(F32)
        return grad_second + norm_back(
            grad_entry * (1.0 + scale_first), normal_first, inverse_first
        )
    grad_kv = (grad_own + swap(grad_peer, "xl").astype(F32)).astype(BF)
    grad_kv = jnp.concatenate([grad_kv[0], grad_kv[1]], axis=1)
    grad_entry = core_sum(dot_nt(grad_queries, w_q) + dot_nt(grad_kv, w_kv))
    grad_q_proj = dot_tn(entry, grad_queries).astype(BF)
    grad_kv_proj = dot_tn(entry, grad_kv).astype(BF)
    grad_scale_first = rows(grad_entry * normal_first)
    grad_shift_first = rows(grad_entry)
    grad_input = grad_second + norm_back(
        grad_entry * (1.0 + scale_first), normal_first, inverse_first
    )
    grad_modulation = jnp.stack(
        [
            grad_shift_first,
            grad_scale_first,
            grad_gate_first,
            grad_shift_second,
            grad_scale_second,
            grad_gate_second,
        ]
    )
    return (grad_input, grad_modulation, (grad_q_proj, grad_kv_proj, grad_out, grad_fc1, grad_fc2))


def sum_over_plane(block):
    x = lax.axis_index(RING_X)
    half, quarter = (x + 1) // 2 % 2, x // 2
    rows, columns = block.shape
    parts = block.astype(BF).reshape(2, rows // 2, columns)
    part = pick(parts, half).astype(F32) + swap(pick(parts, 1 - half), "xl").astype(F32)
    parts = part.astype(BF).reshape(2, rows // 4, columns)
    part = pick(parts, quarter).astype(F32) + swap_odd(pick(parts, 1 - quarter), RING_X).astype(F32)
    part = part.astype(BF)
    part = (part.astype(F32) + swap(part, "zh").astype(F32)).astype(BF)
    part = ordered(quarter == 0, part, swap_odd(part, RING_X))
    return ordered(half == 0, part, swap(part, "xl"))


def fill_fc_kernel(core_ref, mine_ref, other_ref, fc1_ref, fc2_ref):
    half = mine_ref.shape[1] // 2
    rows = fc1_ref.shape[0]
    first = core_ref[0] == 0
    mine, other = mine_ref[...].astype(F32), other_ref[...].astype(F32)
    for c, part in enumerate((jnp.where(first, mine, other), jnp.where(first, other, mine))):
        fc2_ref[half * c : half * (c + 1), :] = part[:half]
        for j in range(4):
            top = half + rows * (j // 2)
            left = half * (j % 2)
            to = half * (2 * j + c)
            fc1_ref[:, to : to + half] = part[top : top + rows, left : left + half]


def fill_attn_kernel(core_ref, mine_ref, other_ref, qkv_ref, out_ref):
    rows, width = out_ref.shape
    half = width // 2
    first = core_ref[0] == 0
    mine, other = mine_ref[...].astype(F32), other_ref[...].astype(F32)
    for c, part in enumerate((jnp.where(first, mine, other), jnp.where(first, other, mine))):
        at = half * c
        qkv_ref[:, at : at + half] = part[rows:, :half]
        qkv_ref[:, width + at : width + at + half] = part[:rows, :half]
        qkv_ref[:, 2 * width + at : 2 * width + at + half] = part[:rows, half:]
        out_ref[:, at : at + half] = part[rows:, half:]


def fill(kernel, core, total, shapes, name):
    whole = pl.BlockSpec(memory_space=pltpu.VMEM)
    return pl.pallas_call(
        kernel,
        in_specs=[pl.BlockSpec(memory_space=pltpu.SMEM), whole, whole],
        out_specs=[whole] * len(shapes),
        out_shape=[jax.ShapeDtypeStruct(shape, F32) for shape in shapes],
        compiler_params=pltpu.CompilerParams(vmem_limit_bytes=40 * 2**20),
        cost_estimate=pl.CostEstimate(flops=0, bytes_accessed=12 * total.size, transcendentals=0),
        name=name,
    )(core.astype(jnp.int32).reshape(1), total, swap(total, "core"))


def on_device(ends, cond, w_ada, b_ada, w_qkv, w_out, w_fc1, w_fc2):
    section = lax.axis_index("section")
    d = lax.axis_index("dp")
    zh, xh = lax.axis_index("zh"), lax.axis_index("xh")
    a = zh * 2 + xh
    core = lax.axis_index("core")
    width = w_out.shape[2]
    half = width // 2
    rows_d = w_out.shape[1]
    columns = lambda array, start: lax.dynamic_slice_in_dim(array, start, half, 1)

    cond_float = cond.astype(F32).reshape(4, width)
    cond_low = jax.nn.silu(cond_float).astype(BF)
    cond_rows = cond_low.reshape(4, 4, rows_d).transpose(1, 0, 2)
    cond_parts = [pick(cond_rows, d)] + [
        shift(pick(cond_rows, (d + s) % 4), "dp", s) for s in (1, 2, 3)
    ]
    piece_attn = jnp.concatenate(
        [columns(w_qkv[0], width * i + half * core) for i in range(3)]
        + [columns(w_out[0], half * core)],
        axis=1,
    )

    blocks = ends[0].reshape(2, 2, *ends.shape[3:])
    mine = lax.dynamic_index_in_dim(blocks, xh, 1, keepdims=False)
    theirs = lax.dynamic_index_in_dim(blocks, 1 - xh, 1, keepdims=False)
    theirs = swap_odd(theirs, RING_X)
    piece_attn, theirs, *cond_parts = join(piece_attn, theirs, *cond_parts)
    blocks = jnp.stack([mine, theirs], axis=1)
    mine = jnp.stack([pick(blocks, zh), swap(pick(blocks, 1 - zh), "zh")])
    mine = mine.reshape(-1, width)
    tokens_half = mine.shape[0]

    below, above = gather_near(piece_attn, "dp")

    latent_rows = jnp.stack([pick(part, a) for part in cond_parts])
    bias = lax.dynamic_update_slice(
        jnp.zeros((6 * width,), F32), b_ada[0].astype(F32), (d * b_ada.shape[1],)
    )
    part_mod = dot(latent_rows, w_ada[0]) + bias[None]
    part_mod, below, above, mine = join(part_mod, below, above, mine)
    mod_parts = [shift(part_mod[s : s + 1], "dp", -s) for s in (1, 2, 3)]
    attn_blocks = gather_far(piece_attn, below, above, "dp")
    other = swap(mine, "core")
    peer = swap(mine, "xl")
    piece_fc1 = jnp.concatenate(
        [columns(w_fc1[0], width * j + half * core) for j in range(4)], axis=1
    )
    piece_fc2 = rows_at(w_fc2[0], half * core, half)
    attn_blocks, mod_parts, other, peer, piece_fc1 = join(
        attn_blocks, mod_parts, other, peer, piece_fc1
    )
    near_fc1 = gather_near(piece_fc1, "dp")
    modulation = part_mod[0:1] + mod_parts[0] + mod_parts[1] + mod_parts[2]
    modulation = [modulation[:, width * i : width * (i + 1)] for i in range(6)]
    start = ordered(core == 0, mine, other)
    start_peer = ordered(core == 0, peer, swap(peer, "core"))
    full_attn = fill_rows(width, attn_blocks, d)
    out_rows = full_attn[:, 3 * half :].reshape(2, half, half)
    full_out = ordered(
        core == 0, pick(out_rows, core), swap(pick(out_rows, 1 - core), "core"), axis=1
    )
    def across(value, pairs, with_peer):
        part = rows_at(value.astype(BF), core * tokens_half, tokens_half)
        part = lax.ppermute(part, "section", pairs)
        own = ordered(core == 0, part, swap(part, "core"))
        if not with_peer:
            return own, None
        peer = swap(part, "xl")
        return own, ordered(core == 0, peer, swap(peer, "core"))

    attn_weights = (full_attn[:, :half], full_attn[:, half : 3 * half], full_out)
    fetched = {}

    def fetch_early(queries):
        queries, fetched["near"], fetched["piece"] = join(queries, near_fc1, piece_fc2)
        fetched["fc1"] = gather_far(piece_fc1, *fetched["near"], "dp")
        return queries

    def fetch_late(mixed):
        mixed, fetched["fc1"] = join(mixed, fetched["fc1"])
        fetched["near"] = gather_near(fetched["piece"], "dp")
        return mixed

    attn_state = attend(
        start.astype(F32), start_peer, modulation, attn_weights, fetch_early, fetch_late
    )
    second, near_fc2 = join(attn_state[0], fetched["near"])
    attn_state = (second, *attn_state[1:])
    full_fc1 = fill_rows(width, fetched["fc1"], d)
    full_fc2 = fill_rows(4 * half, gather_far(piece_fc2, *near_fc2, "dp"), d)
    fc_weights = (full_fc1, full_fc2)
    weights = attn_weights + fc_weights
    result, unused = feed_forward(attn_state, modulation, fc_weights)
    arrived, arrived_peer = across(result, [(0, 1)], True)
    second_input = jnp.where(section == 0, start, arrived).astype(F32)
    second_peer = jnp.where(section == 0, start_peer, arrived_peer)
    attn_state = attend(second_input, second_peer, modulation, attn_weights)
    result, state = feed_forward(attn_state, modulation, fc_weights)

    grad_input = layer_backward(start.astype(F32), state, modulation, weights, core)
    arrived, unused = across(grad_input, [(1, 0)], False)
    seed = jnp.where(section == 0, arrived, start).astype(F32)
    grad_input, grad_modulation, grads = layer_backward(seed, state, modulation, weights)
    grad_q, grad_kv, grad_out, grad_fc1, grad_fc2 = grads

    def block_fc(i):
        one = rows_at(grad_fc1, i * rows_d, rows_d)
        return jnp.concatenate([rows_at(grad_fc2, i * half, half), one[:, :width], one[:, width:]])

    sum_fc = sum_over_plane(scatter_ring(block_fc, "dp", d, grad_q))
    out_fc1, out_fc2 = fill(
        fill_fc_kernel, core, sum_fc, ((rows_d, 8 * half), (2 * half, width)), "fill_fc"
    )
    out_own = ordered(
        core == 0,
        columns(grad_out, half * core),
        swap(columns(grad_out, half - half * core), "core"),
    )

    def block_attn(i):
        kv, q, out = (rows_at(g, i * rows_d, rows_d) for g in (grad_kv, grad_q, out_own))
        return jnp.concatenate([kv, jnp.concatenate([q, out], axis=1)])

    sum_attn = sum_over_plane(scatter_ring(block_attn, "dp", d, grad_q))
    out_qkv, out_out = fill(
        fill_attn_kernel, core, sum_attn, ((rows_d, 6 * half), (rows_d, width)), "fill_attn"
    )

    grad_mod = grad_modulation.reshape(1, 6 * width)
    grad_mod = grad_mod + swap(grad_mod, "xl")
    plane_mod = ordered(xh == 0, grad_mod, swap_odd(grad_mod, RING_X))
    plane_mod = ordered(zh == 0, plane_mod, swap(plane_mod, "zh"))
    all_mod = gather_small(plane_mod, "dp", d)
    all_cond = jnp.zeros((4, 4, rows_d), BF)
    for s in range(4):
        all_cond = lax.dynamic_update_index_in_dim(all_cond, cond_parts[s], (d + 4 - s) % 4, 0)
    all_cond = all_cond.reshape(16, rows_d)
    out_ada = lax.dot_general(
        all_cond.astype(F32), all_mod, (((0,), (0,)), ((), ())), precision=lax.Precision.HIGHEST
    )
    out_bias = jnp.sum(
        lax.dynamic_slice_in_dim(all_mod, d * b_ada.shape[1], b_ada.shape[1], 1), axis=0
    )
    grad_silu = lax.dot_general(
        all_mod,
        w_ada[0].astype(F32),
        (((1,), (1,)), ((), ())),
        precision=lax.Precision.HIGHEST,
    ).reshape(2, 2, 4, rows_d)
    same = jnp.stack([pick(grad_silu, d // 2), swap_odd(pick(grad_silu, 1 - d // 2), "dp")], axis=1)
    got = swap_even(pick(same, 1 - d % 2), "dp")
    same = pick(same, d % 2)
    silu_full = jnp.zeros((4, 4, rows_d), F32)
    beside = d + 1 - 2 * (d % 2)
    for part, place in ((same[0], d), (same[1], 3 - d), (got[0], beside), (got[1], 3 - beside)):
        silu_full = lax.dynamic_update_index_in_dim(silu_full, part, place, 0)
    silu_full = silu_full.transpose(1, 0, 2).reshape(4, width)
    silu_full = silu_full + swap(silu_full, "section")
    unused, silu_pull = jax.vjp(jax.nn.silu, cond_float)
    out_cond = silu_pull(silu_full)[0].reshape(cond.shape)

    edge = jnp.where(section == 0, grad_input, result)
    edge = rows_at(edge, core * tokens_half, tokens_half).reshape(2, 2, -1, width)
    edge = ordered(zh == 0, edge[:1], swap(edge[1:].astype(BF), "zh").astype(F32))
    boundary = ordered(
        xh == 0, edge[:, :1], swap_odd(edge[:, 1:].astype(BF), RING_X).astype(F32), axis=1
    ).reshape(ends.shape)

    return (
        boundary,
        out_cond,
        out_ada[None],
        out_bias[None],
        out_qkv[None],
        out_out[None],
        out_fc1[None],
        out_fc2[None],
    )


def solution(mesh):
    finer = Mesh(
        mesh.devices.reshape(2, 4, 2, 2, 2, 2), ("section", "dp", "zh", "xh", "xl", "core")
    )
    ends_spec = P("section", None, "dp", CTX, None)
    cond_spec = P(None, "dp", None)
    matrix = P("section", "dp", None)
    vector = P("section", "dp")
    return jax.shard_map(
        on_device,
        mesh=finer,
        in_specs=(ends_spec, cond_spec, matrix, vector, matrix, matrix, matrix, matrix),
        out_specs=(ends_spec, cond_spec, matrix, vector, matrix, matrix, matrix, matrix),
        check_vma=False,
    )
```
